32 devices in a mesh: gy: 8 (over z, core), gz: 4 (over y, x).
Axes of the slice: x: 2, y: 2, z: 4, core: 2. Of those that a mesh axis runs over, the one named last changes fastest.
Arguments:
- field_in: bfloat16 [64, 256, 128, 256], P(None, 'gy', 'gz'), may hold values from -42 to 42
- spectral_weight: bfloat16 [32, 32, 32, 64, 128], P('gz', 'gy'), may hold values from -1.5258789e-05 to 1.5258789e-05
- point_weight: bfloat16 [64, 64], replicated, may hold values from -0.75 to 0.75
- point_bias: float32 [64], replicated, may hold values from -3 to 3
- out_weight: bfloat16 [64, 3], replicated, may hold values from -0.75 to 0.75
- out_bias: float32 [3], replicated, may hold values from -4 to 4
Outputs:
- loss_value: float32 [], replicated
- grad_spectral: float32 [32, 32, 32, 64, 128], P('gz', 'gy')
- grad_point: float32 [64, 64], replicated
- grad_point_bias: float32 [64], replicated
- grad_out: float32 [64, 3], replicated
- grad_out_bias: float32 [3], replicated
The draws below stay inside these ranges and needn't reach their ends.
All inputs are finite; a program needn't handle non-finite values.
Results may differ from the reference program's by a relative error of at most 0.01.
Values may be sent and summed in bfloat16 or wider, within the bound.
No kernel may reach another device: no remote copies, remote signals or barrier semaphores. Data moves between devices by JAX's collectives and lax.ppermute only.
A program may use at most 320 MiB of HBM per device.

```python
import math
import jax
import jax.numpy as jnp
from jax import lax

C = 64
NX = 256
NY = 256
NZ = 128
MX = 32
MY = 32
MZ = 32
CY = 32
N_GY = 8


def draw_field_in(key, part):
    noise_key, column_key = jax.random.split(key, 2)
    y_pos = jnp.arange(NY, dtype=jnp.float32) / NY
    z_pos = jnp.arange(NZ, dtype=jnp.float32) / NZ
    height_trend = jnp.exp(math.log(6.0) * (y_pos[:, None] - 0.5 + (0.5 - z_pos[None, :])))
    column_scale = jnp.exp(jax.random.uniform(column_key, (NY, NZ), jnp.float32, -0.8, 0.8))
    values = jnp.clip(jax.random.normal(noise_key, (C, NY, NZ, NX), jnp.float32), -2.5, 2.5)
    return (values * (height_trend * column_scale)[None, :, :, None]).astype(jnp.bfloat16)


def shard_levels(rng, shape, shards, low, high):
    def one(dim, parts):
        draws = jax.random.uniform(jax.random.fold_in(jax.random.fold_in(rng, 6), dim), (parts,), jnp.float32, low / len(shards), high / len(shards))
        return jnp.repeat(jnp.exp(draws), shape[dim] // parts).reshape((-1,) + (1,) * (len(shape) - dim - 1))

    factor_of = one(*shards[0])
    for cut in shards[1:]:
        factor_of = factor_of * one(*cut)
    return factor_of


def centred(own_key, dims, scale, limit, pieces=(), kind=jnp.bfloat16):
    gain = shard_levels(own_key, dims, pieces, -0.22, 0.18) if pieces else 1.0
    entries = jax.random.normal(own_key, dims, jnp.float32) * scale * gain
    return jnp.minimum(jnp.maximum(entries, -limit), limit).astype(kind)


def setup_inputs(seed: int = 0) -> dict:
    splits = jax.random.split(jax.random.key(seed), 7)
    return {
        "field_in": draw_field_in(jax.random.fold_in(splits[6], 71), 0),
        "spectral_weight": centred(splits[1], (MZ, MY, MX, C, 2 * C), (2 * C * (MX * MY * MZ) ** 2) ** -0.5, 1.52587890625e-05, ((0, 4), (1, 8))),
        "point_weight": centred(splits[2], (C, C), C ** -0.5, 0.75),
        "point_bias": centred(splits[3], (C,), 0.5, 3.0, (), jnp.float32),
        "out_weight": centred(splits[4], (C, 3), C ** -0.5, 0.75),
        "out_bias": centred(splits[5], (3,), 1.0, 4.0, (), jnp.float32),
    }


def frequencies(first_mode, mode_count, mode_total):
    mode_index = first_mode + jnp.arange(mode_count, dtype=jnp.int32)
    return jnp.where(mode_index < mode_total // 2, mode_index, mode_index - mode_total)

def twiddle(positions, wave_numbers, length):
    product = positions[:, None] * wave_numbers[None, :] % length
    phases = product.astype(jnp.float32) * (2.0 * math.pi / length)
    return (jnp.cos(phases).astype(jnp.bfloat16), jnp.sin(phases).astype(jnp.bfloat16))

def rotate(with_cos, with_sin, forward):
    half_width = with_cos.shape[-1] // 2
    cos_real, cos_imag = (with_cos[..., :half_width], with_cos[..., half_width:])
    sin_real, sin_imag = (with_sin[..., :half_width], with_sin[..., half_width:])
    if forward:
        return jnp.concatenate([cos_real + sin_imag, cos_imag - sin_real], axis=-1)
    return jnp.concatenate([cos_real - sin_imag, cos_imag + sin_real], axis=-1)

def x_tables(length, mode_total):
    cos_part, sin_part = twiddle(jnp.arange(length, dtype=jnp.int32), frequencies(0, mode_total, mode_total), length)
    forward_table = jnp.stack([cos_part, -sin_part], axis=1)
    inverse_table = jnp.stack([cos_part.T, -sin_part.T], axis=0)
    return (forward_table, inverse_table)

def to_modes(x_modes, factor):
    y_cos, y_sin = twiddle(jnp.arange(NY, dtype=jnp.int32), frequencies(0, MY, MY), NY)
    operand = x_modes.astype(jnp.float32)
    with_cos = jnp.einsum('yzkc,yj->jzkc', operand, y_cos.astype(jnp.float32))
    with_sin = jnp.einsum('yzkc,yj->jzkc', operand, y_sin.astype(jnp.float32))
    y_modes = rotate(with_cos, with_sin, True).astype(jnp.bfloat16)
    z_cos, z_sin = twiddle(jnp.arange(NZ, dtype=jnp.int32), frequencies(0, MZ, MZ), NZ)
    operand = y_modes.astype(jnp.float32)
    with_cos = jnp.einsum('bzkc,zj->jbkc', operand, z_cos.astype(jnp.float32))
    with_sin = jnp.einsum('bzkc,zj->jbkc', operand, z_sin.astype(jnp.float32))
    return (rotate(with_cos, with_sin, True) * factor).astype(jnp.bfloat16)

def from_modes(modes_out):
    z_cos, z_sin = twiddle(jnp.arange(NZ, dtype=jnp.int32), frequencies(0, MZ, MZ), NZ)
    operand = modes_out.astype(jnp.float32)
    with_cos = jnp.einsum('jbkc,zj->bzkc', operand, z_cos.astype(jnp.float32))
    with_sin = jnp.einsum('jbkc,zj->bzkc', operand, z_sin.astype(jnp.float32))
    z_back = rotate(with_cos, with_sin, False).astype(jnp.bfloat16)
    y_cos, y_sin = twiddle(jnp.arange(NY, dtype=jnp.int32), frequencies(0, MY, MY), NY)
    operand = z_back.astype(jnp.float32)
    with_cos = jnp.einsum('jzkc,yj->yzkc', operand, y_cos.astype(jnp.float32))
    with_sin = jnp.einsum('jzkc,yj->yzkc', operand, y_sin.astype(jnp.float32))
    return rotate(with_cos, with_sin, False).astype(jnp.bfloat16)

def mix_modes(modes_in, spectral_weight):

    def one_plane(plane_pair):
        plane_in, plane_weight = plane_pair
        channels = plane_weight.shape[-2]
        operand = plane_in.astype(jnp.float32)
        weights_f = plane_weight.astype(jnp.float32)
        with_real = jnp.einsum('bki,bkio->bko', operand[..., :channels], weights_f)
        with_imag = jnp.einsum('bki,bkio->bko', operand[..., channels:], weights_f)
        return jnp.concatenate([with_real[..., :channels] - with_imag[..., channels:], with_real[..., channels:] + with_imag[..., :channels]], axis=-1).astype(jnp.bfloat16)
    return lax.map(one_plane, (modes_in, spectral_weight))

def weight_grad(modes_in, grad_modes):

    def one_plane(plane_pair):
        plane_in, plane_grad = plane_pair
        channels = plane_in.shape[-1] // 2
        operand = plane_in.astype(jnp.float32)
        grads_f = plane_grad.astype(jnp.float32)
        with_real = jnp.einsum('bki,bko->bkio', operand[..., :channels], grads_f)
        with_imag = jnp.einsum('bki,bko->bkio', operand[..., channels:], grads_f)
        return jnp.concatenate([with_real[..., :channels] + with_imag[..., channels:], with_real[..., channels:] - with_imag[..., :channels]], axis=-1)
    return lax.map(one_plane, (modes_in, grad_modes))

def cell_loss(field_b, slope_x, slope_y, slope_z):
    current_x = slope_y[2] - slope_z[1]
    current_y = slope_z[0] - slope_x[2]
    current_z = slope_x[1] - slope_y[0]
    force_x = current_y * field_b[2] - current_z * field_b[1]
    force_y = current_z * field_b[0] - current_x * field_b[2]
    force_z = current_x * field_b[1] - current_y * field_b[0]
    spread = slope_x[0] + slope_y[1] + slope_z[2]
    strength = field_b[0] * field_b[0] + field_b[1] * field_b[1] + field_b[2] * field_b[2] + 1.0
    return (force_x * force_x + force_y * force_y + force_z * force_z) / strength + spread * spread

def loss_total(b_field):
    padded = jnp.pad(b_field, ((0, 0), (1, 1), (1, 1), (1, 1)))
    center = padded[:, 1:-1, 1:-1, 1:-1]
    slope_x = (padded[:, 1:-1, 1:-1, 2:] - padded[:, 1:-1, 1:-1, :-2]) * 0.5
    slope_y = (padded[:, 2:, 1:-1, 1:-1] - padded[:, :-2, 1:-1, 1:-1]) * 0.5
    slope_z = (padded[:, 1:-1, 2:, 1:-1] - padded[:, 1:-1, :-2, 1:-1]) * 0.5
    return jnp.sum(cell_loss(center, slope_x, slope_y, slope_z)) / (NX * NY * NZ)

def gelu_slope(pre_act):
    normal_cdf = 0.5 * (1.0 + lax.erf(pre_act * (1.0 / math.sqrt(2.0))))
    density = jnp.exp(-0.5 * pre_act * pre_act) * (1.0 / math.sqrt(2.0 * math.pi))
    return normal_cdf + pre_act * density

def reference(field_in, spectral_weight, point_weight, point_bias, out_weight, out_bias):
    forward_table, inverse_table = x_tables(NX, MX)
    channels = field_in.shape[0]
    block_ids = jnp.arange(N_GY, dtype=jnp.int32)

    def x_block(block_id):
        part_in = lax.dynamic_slice_in_dim(field_in, block_id * CY, CY, 1).astype(jnp.float32)
        products = jnp.einsum('cyzx,xpk->yzkpc', part_in, forward_table.astype(jnp.float32))
        return products.reshape(CY, NZ, MX, 2 * channels).astype(jnp.bfloat16)
    x_modes = lax.map(x_block, block_ids).reshape(NY, NZ, MX, 2 * channels)
    modes_in = to_modes(x_modes, math.sqrt(MX * MY * MZ / (NX * NY * NZ)))
    modes_out = mix_modes(modes_in, spectral_weight)
    y_back = from_modes(modes_out)

    def dense_block(block_id):
        part_in = lax.dynamic_slice_in_dim(field_in, block_id * CY, CY, 1).astype(jnp.float32)
        part_modes = lax.dynamic_slice_in_dim(y_back, block_id * CY, CY, 0).astype(jnp.float32)
        spectral = jnp.einsum('yzkpc,pkx->cyzx', part_modes.reshape(CY, NZ, MX, 2, channels), inverse_table.astype(jnp.float32))
        pointwise = jnp.einsum('cyzx,co->oyzx', part_in, point_weight.astype(jnp.float32))
        pre_act = spectral + pointwise + point_bias[:, None, None, None]
        hidden = jax.nn.gelu(pre_act, approximate=False).astype(jnp.bfloat16)
        return (part_in, pre_act, hidden)

    def field_block(block_id):
        part_in, pre_act, hidden = dense_block(block_id)
        return jnp.einsum('cyzx,cb->byzx', hidden.astype(jnp.float32), out_weight.astype(jnp.float32)) + out_bias[:, None, None, None]
    b_field = jnp.transpose(lax.map(field_block, block_ids), (1, 0, 2, 3, 4)).reshape(3, NY, NZ, NX)
    loss_value, pullback = jax.vjp(loss_total, b_field)
    grad_b = pullback(jnp.ones_like(loss_value))[0]

    def grad_block(block_id):
        part_in, pre_act, hidden = dense_block(block_id)
        grad_part = lax.dynamic_slice_in_dim(grad_b, block_id * CY, CY, 1)
        weights_f = out_weight.astype(jnp.float32)
        grad_hidden = jnp.zeros_like(pre_act)
        for component in range(3):
            grad_hidden = grad_hidden + weights_f[:, component][:, None, None, None] * grad_part[component][None]
        grad_pre = (grad_hidden * gelu_slope(pre_act)).astype(jnp.bfloat16)
        grad_pre_f = grad_pre.astype(jnp.float32)
        out_part = jnp.einsum('cyzx,byzx->cb', hidden.astype(jnp.float32), grad_part, precision=lax.Precision.HIGHEST)
        out_bias_part = lax.optimization_barrier(jnp.sum(grad_part, axis=(1, 2, 3)))
        point_part = jnp.einsum('iyzx,oyzx->io', part_in, grad_pre_f)
        point_bias_part = lax.optimization_barrier(jnp.sum(grad_pre_f, axis=(1, 2, 3)))
        products = jnp.einsum('cyzx,xpk->yzkpc', grad_pre_f, forward_table.astype(jnp.float32))
        x_part = products.reshape(CY, NZ, MX, 2 * channels).astype(jnp.bfloat16)
        return (point_part, point_bias_part, out_part, out_bias_part, x_part)
    point_parts, point_bias_parts, out_parts, out_bias_parts, x_parts = lax.map(grad_block, block_ids)
    grad_modes = to_modes(x_parts.reshape(NY, NZ, MX, 2 * channels), 1.0)
    grad_spectral = weight_grad(modes_in, grad_modes)
    return (loss_value, grad_spectral, lax.optimization_barrier(jnp.sum(point_parts, axis=0)), lax.optimization_barrier(jnp.sum(point_bias_parts, axis=0)), lax.optimization_barrier(jnp.sum(out_parts, axis=0)), lax.optimization_barrier(jnp.sum(out_bias_parts, axis=0)))
```

```python
import functools
import math

import jax
import jax.numpy as jnp
from jax import lax
from jax.experimental import pallas as pl
from jax.experimental.pallas import tpu as pltpu
from jax.sharding import PartitionSpec as P

F32 = jnp.float32
BF16 = jnp.bfloat16
CORES = 2
LANES = 128
VMEM_LIMIT = 56 * 1024 * 1024
PARTS = 4


def params():
    return pltpu.CompilerParams(
        vmem_limit_bytes=VMEM_LIMIT, dimension_semantics=("arbitrary",)
    )


def whole(shape):
    return pl.BlockSpec(shape, lambda i: (0,) * len(shape), pipeline_mode=pl.Buffered(1))


ANY = pl.BlockSpec(memory_space=pl.ANY)


def cost(flops, moved):
    return pl.CostEstimate(flops=flops, bytes_accessed=moved, transcendentals=0)


def dot(a, b):
    return jnp.dot(a, b, preferred_element_type=F32)


def frequencies(mode_index, mode_total):
    return jnp.where(mode_index < mode_total // 2, mode_index, mode_index - mode_total)


def twiddle(product, length):
    phases = (product % length).astype(F32) * (2.0 * math.pi / length)
    return jnp.cos(phases).astype(BF16).astype(F32), jnp.sin(phases).astype(BF16).astype(F32)


def with_halo(block, sides, width):
    for axis, dim in sides:
        count = lax.axis_size(axis)
        forward = [(i, i + 1) for i in range(count - 1)]
        backward = [(target, source) for source, target in forward]
        low = lax.ppermute(
            lax.slice_in_dim(block, block.shape[dim] - width, None, axis=dim), axis, forward
        )
        high = lax.ppermute(lax.slice_in_dim(block, 0, width, axis=dim), axis, backward)
        block = jnp.concatenate([low, block, high], axis=dim)
    return block


class Layout:
    def __init__(self, field_in, spectral_weight):
        self.channels, self.rows, self.depth, self.width = field_in.shape
        self.kz, self.ky, self.mx = spectral_weight.shape[:3]
        self.n_gy, self.n_gz = lax.axis_size("gy"), lax.axis_size("gz")
        self.chips = self.n_gy // CORES
        self.ny, self.nz = self.rows * self.n_gy, self.depth * self.n_gz
        self.my, self.mz = self.ky * self.n_gy, self.kz * self.n_gz
        self.cells = self.rows * self.depth
        self.modes = self.my * self.mz
        self.pack = LANES // self.mx
        self.groups = self.channels // self.pack
        self.own = self.ky * self.kz
        self.band = min(LANES // self.depth, self.rows)
        self.blocks = self.rows // self.band
        self.step = min(LANES // self.rows, self.kz)
        self.tile = min(16, self.depth)
        self.gy, self.gz = lax.axis_index("gy"), lax.axis_index("gz")
        self.y0 = self.gy * self.rows
        self.z0 = self.gz * self.depth

    def mode_numbers(self):
        core, chip = self.gy % CORES, self.gy // CORES
        h = jnp.arange(CORES, dtype=jnp.int32) ^ core
        f = jnp.arange(self.chips, dtype=jnp.int32) ^ chip
        e = jnp.arange(self.n_gz, dtype=jnp.int32) ^ self.gz
        ky = (f[None, :, None] * CORES + h[:, None, None]) * self.ky
        ky = ky + jnp.arange(self.ky, dtype=jnp.int32)
        kz = e[:, None] * self.kz + jnp.arange(self.kz, dtype=jnp.int32)
        return frequencies(ky, self.my), frequencies(kz, self.mz)

    def grid_tables(self):
        ky, kz = self.mode_numbers()
        ky, kz = ky.reshape(self.my), kz.reshape(self.mz)
        y_cells = self.y0 + jnp.arange(self.rows, dtype=jnp.int32)
        z_cells = self.z0 + jnp.arange(self.depth, dtype=jnp.int32)
        y_both = jnp.stack(twiddle(ky[:, None] * y_cells, self.ny))
        y_both = y_both.reshape(2, self.my, self.blocks, self.band)
        z_both = jnp.stack(twiddle(kz[:, None] * z_cells, self.nz))
        band, step = jnp.eye(self.band, dtype=F32), jnp.eye(self.step, dtype=F32)
        z_modes, y_modes = self.mz * self.band, self.my * self.step
        z_cells, y_cells = self.band * self.depth, self.blocks * self.step * self.band
        z_forward = jnp.einsum("pkz,ab->kapbz", z_both, band)
        y_forward = jnp.einsum("pknb,st->kspntb", y_both, step)
        z_back = jnp.einsum("pkz,ab->azpkb", z_both, band)
        y_back = jnp.einsum("pknb,st->nsbpkt", y_both, step)
        return (
            z_forward.reshape(z_modes, 2 * z_cells).astype(BF16),
            y_forward.reshape(y_modes, 2 * y_cells).astype(BF16),
            y_back.reshape(y_cells, 2 * y_modes).astype(BF16),
            z_back.reshape(z_cells, 2 * z_modes).astype(BF16),
        )

    def x_tables(self):
        k = frequencies(jnp.arange(self.mx, dtype=jnp.int32), self.mx)
        cos, sin = twiddle(jnp.arange(self.width, dtype=jnp.int32)[:, None] * k, self.width)
        table = jnp.stack([cos, -sin], axis=1)
        eye = jnp.eye(self.pack, dtype=F32)
        forward = table[None, :, :, None, :] * eye[:, None, None, :, None]
        forward = forward.reshape(self.pack * self.width, 2 * LANES).astype(BF16)
        flipped = jnp.transpose(table, (1, 2, 0))
        inverse = flipped[:, None, :, None, :] * eye[None, :, None, :, None]
        inverse = inverse.reshape(2 * LANES, self.pack * self.width).astype(BF16)
        return forward, inverse


def turn(values, sign):
    real, imag = values[:, :LANES], values[:, LANES:]
    return jnp.concatenate([imag, -real] if sign > 0 else [-imag, real], axis=1)


def z_transform(x_modes, table_ref, part_ref, n):
    x_modes = x_modes.astype(BF16)
    rhs = jnp.concatenate([x_modes, turn(x_modes, 1)], axis=0)
    modes = dot(table_ref[...], rhs).astype(BF16)
    steps, _, _, size, _ = part_ref.shape
    part_ref[:, 0, n] = modes.reshape(steps, size, 2 * LANES)
    part_ref[:, 1, n] = turn(modes, 1).reshape(steps, size, 2 * LANES)


def y_transform(table_ref, part_ref, own_ref, send_ref):
    half = table_ref.shape[0] // 2
    steps, _, blocks, size, _ = part_ref.shape
    chips = own_ref.shape[1]
    rows = half // chips
    per = steps // own_ref.shape[0]
    for q in range(steps):
        modes = dot(table_ref[...], part_ref[q].reshape(2 * blocks * size, 2 * LANES))
        modes = modes.astype(BF16)
        here = pl.ds(q % per * rows, rows)
        own_ref[q // per, :, 0, here] = modes[:half].reshape(chips, rows, 2 * LANES)
        send_ref[q // per, :, 0, here] = modes[half:].reshape(chips, rows, 2 * LANES)


def modes_kernel(n_after, field_ref, x_ref, z_ref, y_ref, *refs):
    own_ref, send_ref, part_ref = refs[n_after:]
    pack, rows, depth, width = field_ref.shape
    blocks = part_ref.shape[2]
    band = rows // blocks
    for n in range(blocks):
        cells = [
            field_ref[c, n * band : (n + 1) * band].reshape(band * depth, width)
            for c in range(pack)
        ]
        z_transform(dot(jnp.concatenate(cells, axis=1), x_ref[...]), z_ref, part_ref, n)
    y_transform(y_ref, part_ref, own_ref, send_ref)


def mode_blocks(lay, count):
    shape = (lay.n_gz, lay.chips, count, lay.own, 2 * LANES)
    spec = pl.BlockSpec((lay.n_gz, lay.chips, 1, lay.own, 2 * LANES), lambda i: (0, 0, i, 0, 0))
    return jax.ShapeDtypeStruct(shape, BF16), spec


def part_scratch(lay):
    size = lay.step * lay.band
    return pltpu.VMEM((lay.mz // lay.step, 2, lay.blocks, size, 2 * LANES), BF16)


def forward_modes(lay, field_in, x_table, tables, first, count, after=()):
    out, spec = mode_blocks(lay, count)
    block = (lay.pack, lay.rows, lay.depth, lay.width)
    volume = lay.pack * lay.cells * lay.width
    return pl.pallas_call(
        functools.partial(modes_kernel, len(after)),
        grid=(count,),
        in_specs=[
            pl.BlockSpec(block, lambda i: (first + i, 0, 0, 0)),
            whole(x_table.shape),
            whole(tables[0].shape),
            whole(tables[1].shape),
        ]
        + [ANY] * len(after),
        out_specs=[spec, spec],
        out_shape=[out, out],
        scratch_shapes=[part_scratch(lay)],
        compiler_params=params(),
        cost_estimate=cost(count * volume * 2 * 2 * LANES, count * volume * 3),
        name="forward_modes",
    )(field_in, x_table, tables[0], tables[1], *after)


def exchange(value, axis, distance):
    count = lax.axis_size(axis)
    return lax.ppermute(value, axis, [(i, i ^ distance) for i in range(count)])


def sum_cores(own, send):
    return (own.astype(F32) + exchange(send, "gy", 1).astype(F32)).astype(BF16)


def sum_depth(lay, both):
    total = both[0].astype(F32)
    for d in range(1, lay.n_gz):
        total = total + exchange(both[d], "gz", d).astype(F32)
    return total.astype(BF16)


def sum_chips(lay, column, factor):
    total = column[0].astype(F32)
    for d in range(1, lay.chips):
        total = total + exchange(column[d], "gy", d * CORES).astype(F32)
    return (total * factor).astype(BF16)


def spread_chips(lay, mine):
    return jnp.stack([mine] + [exchange(mine, "gy", d * CORES) for d in range(1, lay.chips)])


def spread_depth(lay, column):
    return [column] + [exchange(column, "gz", d) for d in range(1, lay.n_gz)]


def by_mode(lay, modes):
    count = modes.shape[0]
    split = modes.reshape(
        count, lay.kz // lay.step, lay.ky, lay.step, 2, lay.pack, lay.mx
    )
    return jnp.transpose(split, (1, 3, 2, 4, 6, 0, 5)).reshape(
        lay.kz, lay.ky, 2 * lay.mx, count * lay.pack
    )


def by_group(lay, modes):
    split = modes.reshape(
        lay.kz // lay.step, lay.step, lay.ky, lay.mx, 2, lay.groups, lay.pack
    )
    return jnp.transpose(split, (5, 0, 2, 1, 4, 6, 3)).reshape(
        lay.groups, lay.own, 2 * LANES
    )


def mix_kernel(modes_ref, weight_ref, *refs):
    out_ref = refs[-1]
    count, channels, wide = weight_ref.shape[2:]
    modes = modes_ref[0, 0]
    per = wide // channels
    modes = jnp.concatenate([modes] * per, axis=1)
    shape = modes.shape
    row = lax.broadcasted_iota(jnp.int32, shape, 0) % count
    owner = lax.broadcasted_iota(jnp.int32, shape, 1) // channels
    zero = jnp.zeros_like(modes)
    spread = [jnp.where(row == owner + n * per, modes, zero) for n in range(count // per)]
    mixed = dot(jnp.concatenate(spread, axis=1), weight_ref[0, 0].reshape(count * channels, wide))
    real, imag = mixed[:count], mixed[count:]
    turned = jnp.concatenate([-imag[:, channels:], imag[:, :channels]], axis=1)
    out_ref[0, 0] = (real + turned).astype(BF16)


def mode_spec(lay, shape):
    return pl.BlockSpec((1, 1) + shape, lambda i: (i // lay.ky, i % lay.ky) + (0,) * len(shape))


def mix_modes(lay, modes_in, spectral_weight, after=()):
    shape = (lay.mx, 2 * lay.channels)
    return pl.pallas_call(
        mix_kernel,
        grid=(lay.own,),
        in_specs=[mode_spec(lay, modes_in.shape[2:]), mode_spec(lay, spectral_weight.shape[2:])]
        + [ANY] * len(after),
        out_specs=mode_spec(lay, shape),
        out_shape=jax.ShapeDtypeStruct((lay.kz, lay.ky) + shape, BF16),
        compiler_params=params(),
        cost_estimate=cost(spectral_weight.size * 8, spectral_weight.size * 2),
        name="mix_modes",
    )(modes_in, spectral_weight, *after)


def pointwise_kernel(tile, n_after, field_ref, weight_ref, *refs):
    out_ref, blocks_ref = refs[n_after:]
    channels, rows, depth, width = field_ref.shape
    count = out_ref.shape[0]

    @pl.when(pl.program_id(0) == 0)
    def _():
        shape = (tile * channels, tile * channels)
        split = lax.broadcasted_iota(jnp.int32, (shape[0], channels), 0) // tile
        split = (split == lax.broadcasted_iota(jnp.int32, (shape[0], channels), 1)).astype(BF16)
        wide = dot(split[: count * tile, :count], weight_ref[...]).astype(BF16)
        wide = lax.dot_general(
            wide, split, (((1,), (1,)), ((), ())), preferred_element_type=F32
        )
        row = lax.broadcasted_iota(jnp.int32, wide.shape, 0) % tile
        column = lax.broadcasted_iota(jnp.int32, wide.shape, 1) % tile
        blocks_ref[...] = jnp.where(row == column, wide, 0.0).astype(BF16)

    for y in range(rows):
        for z in range(0, depth, tile):
            cells = field_ref[:, y, z : z + tile, :].reshape(channels * tile, width)
            mixed = dot(blocks_ref[...], cells).astype(BF16)
            out_ref[:, y, z : z + tile, :] = mixed.reshape(count, tile, width)


def pointwise(lay, field_in, weight, after=()):
    span = 2
    count = weight.shape[0]
    size = lay.channels * lay.tile
    return pl.pallas_call(
        functools.partial(pointwise_kernel, lay.tile, len(after)),
        grid=(lay.rows // span,),
        in_specs=[
            pl.BlockSpec((lay.channels, span, lay.depth, lay.width), lambda i: (0, i, 0, 0)),
            whole(weight.shape),
        ]
        + [ANY] * len(after),
        out_specs=pl.BlockSpec((count, span, lay.depth, lay.width), lambda i: (0, i, 0, 0)),
        out_shape=jax.ShapeDtypeStruct((count,) + field_in.shape[1:], BF16),
        scratch_shapes=[pltpu.VMEM((count * lay.tile, size), BF16)],
        compiler_params=params(),
        cost_estimate=cost(2 * size * count * lay.cells * lay.width, 3 * field_in.size),
        name="pointwise",
    )(field_in, weight, *after)


def gelu_and_slope(v):
    bell = jnp.exp(v * v * -0.5)
    t = 1.0 / (1.0 + jnp.abs(v) * (0.3275911 / math.sqrt(2.0)))
    poly = 0.5 * 1.061405429
    for coefficient in (-1.453152027, 1.421413741, -0.284496736, 0.254829592):
        poly = poly * t + 0.5 * coefficient
    tail = poly * t * bell
    cdf = jnp.where(v >= 0.0, 1.0 - tail, tail)
    return v * cdf, cdf + v * (bell * (1.0 / math.sqrt(2.0 * math.pi)))


def dense_kernel(first, n_pieces, n_after, *refs):
    pieces = refs[:n_pieces]
    y_ref, z_ref, x_ref, point_ref, bias_ref, mix_ref, b_in_ref = refs[n_pieces : n_pieces + 7]
    hidden_ref, slope_ref, b_ref, part_ref = refs[n_pieces + 7 + n_after :]
    pack, rows, depth, width = point_ref.shape
    blocks, _, steps, size, _ = part_ref.shape
    band = rows // blocks
    tile = mix_ref.shape[2] // pack
    step = pl.program_id(0)

    @pl.when(step == 0)
    def _():
        b_ref[...] = b_in_ref[...]

    depths = n_pieces // CORES
    per = steps // depths
    for q in range(steps):
        chunks = []
        for h in range(CORES):
            piece = pieces[h * depths + q // per]
            rows_here = piece.shape[2] // per
            here = pl.ds(q % per * rows_here, rows_here)
            chunks.append(piece[:, 0, here].reshape(piece.shape[0] * rows_here, 2 * LANES))
        modes = jnp.concatenate(chunks, axis=0)
        back = dot(y_ref[...], jnp.concatenate([modes, turn(modes, -1)], axis=0)).astype(BF16)
        part_ref[:, 0, q] = back.reshape(blocks, size, 2 * LANES)
        part_ref[:, 1, q] = turn(back, -1).reshape(blocks, size, 2 * LANES)
    channel = (first + step) * pack

    def body(n, carry):
        here = pl.ds(n * band, band)
        cells = dot(z_ref[...], part_ref[n].reshape(2 * steps * size, 2 * LANES)).astype(BF16)
        hiddens = []
        for c in range(pack):
            value = dot(cells, x_ref[:, c * width : (c + 1) * width])
            value = value.reshape(band, depth, width)
            value = value + (point_ref[c, here].astype(F32) + bias_ref[channel + c])
            hidden, slope = gelu_and_slope(value)
            hiddens.append(hidden.astype(BF16))
            hidden_ref[c, here] = hiddens[c]
            slope_ref[c, here] = slope.astype(BF16)
        for y in range(band):
            for z in range(0, depth, tile):
                cells = jnp.concatenate([h[y, z : z + tile] for h in hiddens], axis=0)
                added = dot(mix_ref[0], cells).reshape(3, tile, width)
                b_ref[:, n * band + y, z : z + tile] += added
        return carry

    lax.fori_loop(0, blocks, body, 0)


def dense(lay, pieces, tables, x_table, point, bias, mixers, b_in, first, count, after=()):
    size = (lay.chips, 1, lay.own, 2 * LANES)
    block = (lay.pack, lay.rows, lay.depth, lay.width)
    part = pl.BlockSpec(block, lambda i: (i, 0, 0, 0))
    kept = jax.ShapeDtypeStruct((count * lay.pack,) + block[1:], BF16)
    volume = lay.pack * lay.cells * lay.width
    steps = lay.mz // lay.step
    return pl.pallas_call(
        functools.partial(dense_kernel, first, len(pieces), len(after)),
        grid=(count,),
        in_specs=[pl.BlockSpec(size, lambda i: (0, i, 0, 0)) for _ in pieces]
        + [
            whole(tables[2].shape),
            whole(tables[3].shape),
            whole(x_table.shape),
            part,
            pl.BlockSpec(memory_space=pltpu.SMEM),
            pl.BlockSpec((1,) + mixers.shape[1:], lambda i: (first + i, 0, 0)),
            whole(b_in.shape),
        ]
        + [ANY] * len(after),
        out_specs=[part, part, whole(b_in.shape)],
        out_shape=[kept, kept, jax.ShapeDtypeStruct(b_in.shape, F32)],
        scratch_shapes=[
            pltpu.VMEM((lay.blocks, 2, steps, lay.step * lay.band, 2 * LANES), BF16)
        ],
        compiler_params=params(),
        cost_estimate=cost(count * volume * 2 * 6 * LANES, count * volume * 24),
        name="dense",
    )(*pieces, tables[2], tables[3], x_table, point, bias, mixers, b_in, *after)


def stencil_kernel(total_y, total_z, origin_ref, b_ref, grad_ref, sums_ref, gy_ref, rest_ref):
    _, rows_wide, depth_wide, width = b_ref.shape
    rows, depth = grad_ref.shape[1:3]
    shape = (depth_wide, width)
    lane = lax.broadcasted_iota(jnp.int32, shape, 1)
    z_cell = origin_ref[1] + lax.broadcasted_iota(jnp.int32, shape, 0) - 2
    z_inside = (z_cell >= 0) & (z_cell < total_z)
    z_own = lax.broadcasted_iota(jnp.int32, shape, 0)
    z_own = (z_own >= 2) & (z_own < depth + 2)
    scale = 1.0 / (total_y * total_z * width)

    def next_x(v):
        return jnp.where(lane == width - 1, 0.0, pltpu.roll(v, width - 1, 1))

    def last_x(v):
        return jnp.where(lane == 0, 0.0, pltpu.roll(v, 1, 1))

    def next_z(v):
        return pltpu.roll(v, depth_wide - 1, 0)

    def last_z(v):
        return pltpu.roll(v, 1, 0)

    def terms(n, loss):
        b = [b_ref[a, n + 1] for a in range(3)]
        dx = [(next_x(v) - last_x(v)) * 0.5 for v in b]
        dy = [(b_ref[a, n + 2] - b_ref[a, n]) * 0.5 for a in range(3)]
        dz = [(next_z(v) - last_z(v)) * 0.5 for v in b]
        jx = dy[2] - dz[1]
        jy = dz[0] - dx[2]
        jz = dx[1] - dy[0]
        fx = jy * b[2] - jz * b[1]
        fy = jz * b[0] - jx * b[2]
        fz = jx * b[1] - jy * b[0]
        q = dx[0] + dy[1] + dz[2]
        strength = b[0] * b[0] + b[1] * b[1] + b[2] * b[2] + 1.0
        inverse = 1.0 / strength
        ratio = (fx * fx + fy * fy + fz * fz) * inverse
        y_cell = origin_ref[0] + n - 1
        y_inside = (y_cell >= 0) & (y_cell < total_y)
        own = z_own & (n >= 1) & (n <= rows)
        loss = loss + jnp.where(own, ratio + q * q, 0.0)
        weight = jnp.where(z_inside & y_inside, 2.0 * scale, 0.0)
        inverse = inverse * weight
        pull = ratio * inverse
        fx, fy, fz = fx * inverse, fy * inverse, fz * inverse
        q = q * weight
        cx = b[1] * fz - b[2] * fy
        cy = b[2] * fx - b[0] * fz
        cz = b[0] * fy - b[1] * fx
        db = [
            fy * jz - fz * jy - pull * b[0],
            fz * jx - fx * jz - pull * b[1],
            fx * jy - fy * jx - pull * b[2],
        ]
        gx = [q, cz, -cy]
        gy = [-cz, q, cx]
        gz = [cy, -cx, q]
        for a in range(3):
            gy_ref[a, n] = gy[a]
            back = last_x(gx[a]) - next_x(gx[a]) + last_z(gz[a]) - next_z(gz[a])
            rest_ref[a, n] = db[a] + back * 0.5
        return loss

    loss = lax.fori_loop(0, rows + 2, terms, jnp.zeros(shape, F32))

    def combine(n, sums):
        done = []
        for a in range(3):
            grad = rest_ref[a, n + 1] + (gy_ref[a, n] - gy_ref[a, n + 2]) * 0.5
            grad = grad[2 : depth + 2]
            grad_ref[a, n] = grad
            done.append(sums[a] + grad)
        return tuple(done)

    sums = lax.fori_loop(0, rows, combine, (jnp.zeros((depth, width), F32),) * 3)
    sums_ref[...] = jnp.zeros_like(sums_ref)
    for a in range(3):
        sums_ref[a : a + 1, :] = jnp.sum(sums[a], axis=0, keepdims=True)
    sums_ref[3:4, :] = jnp.sum(loss, axis=0, keepdims=True)


def stencil(lay, b_field):
    padded = with_halo(b_field, (("gy", 1), ("gz", 2)), 2)
    padded = jnp.pad(padded, ((0, 0), (0, 0), (0, 4), (0, 0)))
    origin = jnp.stack([lay.y0, lay.z0]).astype(jnp.int32)
    wide = (3, lay.rows + 2, padded.shape[2], lay.width)
    return pl.pallas_call(
        functools.partial(stencil_kernel, lay.ny, lay.nz),
        in_specs=[
            pl.BlockSpec(memory_space=pltpu.SMEM),
            pl.BlockSpec(memory_space=pltpu.VMEM),
        ],
        out_specs=[pl.BlockSpec(memory_space=pltpu.VMEM)] * 2,
        out_shape=[
            jax.ShapeDtypeStruct(b_field.shape, F32),
            jax.ShapeDtypeStruct((8, lay.width), F32),
        ],
        scratch_shapes=[pltpu.VMEM(wide, F32), pltpu.VMEM(wide, F32)],
        compiler_params=pltpu.CompilerParams(vmem_limit_bytes=VMEM_LIMIT),
        name="stencil",
    )(origin, padded)


def grad_kernel(first, n_after, weight_ref, hidden_ref, slope_ref, grad_ref, x_ref, z_ref, y_ref,
                *refs):
    pre_ref, own_ref, send_ref, sums_ref, part_ref = refs[n_after:]
    pack, rows, depth, width = hidden_ref.shape
    blocks = part_ref.shape[2]
    band = rows // blocks
    channel = (first + pl.program_id(0)) * pack

    def fold(v):
        return jnp.sum(v.reshape(-1, 8, width), axis=0)

    def body(n, sums):
        here = pl.ds(n * band, band)
        grads = [grad_ref[b, here] for b in range(3)]
        done, pres = [], []
        for c in range(pack):
            w = [weight_ref[channel + c, b] for b in range(3)]
            mixed = grads[0] * w[0] + grads[1] * w[1] + grads[2] * w[2]
            pre = (mixed * slope_ref[c, here].astype(F32)).astype(BF16)
            pre_ref[c, here] = pre
            pres.append(pre.reshape(band * depth, width))
            hidden = hidden_ref[c, here].astype(F32)
            for b in range(3):
                done.append(sums[3 * c + b] + fold(hidden * grads[b]))
        total = dot(jnp.concatenate(pres, axis=1), x_ref[...])
        done.append(sums[3 * pack] + fold(total))
        z_transform(total, z_ref, part_ref, n)
        return tuple(done)

    start = (jnp.zeros((8, width), F32),) * (3 * pack) + (jnp.zeros((8, 2 * LANES), F32),)
    sums = lax.fori_loop(0, blocks, body, start)
    sums_ref[...] = jnp.zeros_like(sums_ref)
    for n in range(3 * pack + 1):
        sums_ref[0, n : n + 1, :] = jnp.sum(sums[n], axis=0, keepdims=True)
    y_transform(y_ref, part_ref, own_ref, send_ref)


def grad_modes(lay, hidden, slope, grad_b, x_table, tables, weights, first, count, after=()):
    out, spec = mode_blocks(lay, count)
    block = (lay.pack, lay.rows, lay.depth, lay.width)
    part = pl.BlockSpec(block, lambda i: (i, 0, 0, 0))
    volume = lay.pack * lay.cells * lay.width
    lines = -(-(3 * lay.pack + 1) // 8) * 8
    return pl.pallas_call(
        functools.partial(grad_kernel, first, len(after)),
        grid=(count,),
        in_specs=[
            pl.BlockSpec(memory_space=pltpu.SMEM),
            part,
            part,
            whole(grad_b.shape),
            whole(x_table.shape),
            whole(tables[0].shape),
            whole(tables[1].shape),
        ]
        + [ANY] * len(after),
        out_specs=[
            part,
            spec,
            spec,
            pl.BlockSpec((1, lines, lay.width), lambda i: (i, 0, 0)),
        ],
        out_shape=[
            jax.ShapeDtypeStruct(hidden.shape, BF16),
            out,
            out,
            jax.ShapeDtypeStruct((count, lines, lay.width), F32),
        ],
        scratch_shapes=[part_scratch(lay)],
        compiler_params=params(),
        cost_estimate=cost(count * volume * 2 * 2 * LANES, count * volume * 10),
        name="grad_modes",
    )(weights, hidden, slope, grad_b, x_table, tables[0], tables[1], *after)


def point_kernel(tile, n_after, field_ref, grad_ref, *refs):
    out_ref, acc_ref = refs[n_after:]
    channels, rows, depth, width = field_ref.shape
    count = grad_ref.shape[0]
    step = pl.program_id(0)

    @pl.when(step == 0)
    def _():
        acc_ref[...] = jnp.zeros_like(acc_ref)

    total = 0.0
    for y in range(rows):
        for z in range(0, depth, tile):
            left = field_ref[:, y, z : z + tile, :].reshape(channels * tile, width)
            right = grad_ref[:, y, z : z + tile, :].reshape(count * tile, width)
            total = total + lax.dot_general(
                left, right, (((1,), (1,)), ((), ())), preferred_element_type=F32
            )
    acc_ref[...] += total

    @pl.when(step == pl.num_programs(0) - 1)
    def _():
        def pick(n):
            owner = lax.broadcasted_iota(jnp.int32, (n, n * tile), 1) // tile
            return (owner == lax.broadcasted_iota(jnp.int32, (n, n * tile), 0)).astype(F32)

        row = lax.broadcasted_iota(jnp.int32, acc_ref.shape, 0)
        column = lax.broadcasted_iota(jnp.int32, acc_ref.shape, 1)
        kept = jnp.where(row % tile == column % tile, acc_ref[...], 0.0)
        half = jnp.dot(
            pick(channels), kept, precision=lax.Precision.HIGHEST, preferred_element_type=F32
        )
        out_ref[...] = lax.dot_general(
            half,
            pick(count),
            (((1,), (1,)), ((), ())),
            precision=lax.Precision.HIGHEST,
            preferred_element_type=F32,
        )


def point_grad(lay, field_in, grad_pre, after=()):
    span = 4

    def block(count):
        return pl.BlockSpec((count, span, lay.depth, lay.width), lambda i: (0, i, 0, 0))

    count = grad_pre.shape[0]
    size = lay.channels * lay.tile
    return pl.pallas_call(
        functools.partial(point_kernel, lay.tile, len(after)),
        grid=(lay.rows // span,),
        in_specs=[block(lay.channels), block(count)] + [ANY] * len(after),
        out_specs=pl.BlockSpec((lay.channels, count), lambda i: (0, 0)),
        out_shape=jax.ShapeDtypeStruct((lay.channels, count), F32),
        scratch_shapes=[pltpu.VMEM((size, count * lay.tile), F32)],
        compiler_params=params(),
        cost_estimate=cost(2 * size * count * lay.cells * lay.width, 3 * field_in.size),
        name="point_grad",
    )(field_in, grad_pre, *after)


def outer_kernel(modes_ref, grads_ref, out_ref):
    count, channels, wide = out_ref.shape[2:]
    right = grads_ref[0, 0]
    turned = jnp.concatenate([right[:, channels:], -right[:, :channels]], axis=1)
    rows = jnp.concatenate([right, turned], axis=0)
    row = lax.broadcasted_iota(jnp.int32, rows.shape, 0) % count
    zero = jnp.zeros_like(rows)
    for k in range(0, count, 2):
        pair = [jnp.where(row == k + n, rows, zero) for n in range(2)]
        out = dot(modes_ref[0, 0], jnp.concatenate(pair, axis=1))
        out_ref[0, 0, k] = out[:, :wide]
        out_ref[0, 0, k + 1] = out[:, wide:]


def weight_grad(lay, modes_in, grads):
    columns = jnp.transpose(modes_in, (0, 1, 3, 2))
    rows = jnp.concatenate([grads[:, :, : lay.mx], grads[:, :, lay.mx :]], axis=-1)
    tile = (lay.mx, lay.channels, 2 * lay.channels)
    shape = (lay.kz, lay.ky) + tile
    return pl.pallas_call(
        outer_kernel,
        grid=(lay.own,),
        in_specs=[mode_spec(lay, columns.shape[2:]), mode_spec(lay, rows.shape[2:])],
        out_specs=mode_spec(lay, tile),
        out_shape=jax.ShapeDtypeStruct(shape, F32),
        compiler_params=params(),
        cost_estimate=cost(math.prod(shape) * 4, math.prod(shape) * 4),
        name="weight_grad",
    )(columns, rows)


def sum_everywhere(value, axes):
    for axis in axes:
        count = lax.axis_size(axis)
        d = 1
        while d < count:
            value = value + lax.ppermute(value, axis, [(i, i ^ d) for i in range(count)])
            d *= 2
    return value


def on_device(field_in, spectral_weight, point_weight, point_bias, out_weight, out_bias):
    lay = Layout(field_in, spectral_weight)
    tables = lay.grid_tables()
    x_table, x_back = lay.x_tables()
    weights = out_weight.astype(F32)
    per = lay.groups // PARTS
    parts = range(PARTS)
    scale = math.sqrt(lay.mx * lay.my * lay.mz / (lay.width * lay.ny * lay.nz))
    share = lay.channels // PARTS

    def point(n, after):
        return pointwise(lay, field_in, point_weight.T[n * share : (n + 1) * share], after)

    both, column, modes, points = [], [], [], []
    for n in parts:
        own, send = forward_modes(
            lay, field_in, x_table, tables, n * per, per, after=both[n - 2 : n - 1] if n > 1 else ()
        )
        both.append(sum_cores(own, send))
    for n in parts:
        column.append(sum_depth(lay, both[n]))
        modes.append(sum_chips(lay, column[n], scale))
    points.append(point(0, both[-1:]))
    points.append(point(1, column[:1]))
    points.append(point(2, column[1:2]))
    modes_in = by_mode(lay, jnp.concatenate(modes))
    mixed = mix_modes(lay, modes_in, spectral_weight, after=points)
    mine = by_group(
        lay, mixed.reshape(lay.kz, lay.ky, lay.mx, 2, lay.groups, lay.pack)
    )
    points.append(point(3, [mine]))

    b_field = jnp.broadcast_to(
        out_bias[:, None, None, None], (3, lay.rows, lay.depth, lay.width)
    ).astype(F32)
    eye = jnp.eye(lay.tile, dtype=BF16)
    mixers = jnp.einsum("gcb,zy->gbzcy", out_weight.reshape(lay.groups, lay.pack, 3), eye)
    mixers = mixers.reshape(lay.groups, 3 * lay.tile, lay.pack * lay.tile)
    hiddens, slopes = [], []
    columns = [spread_chips(lay, mine[n * per : (n + 1) * per]) for n in parts]
    for n in parts:
        pieces = spread_depth(lay, columns[n])
        pieces = pieces + [exchange(piece, "gy", 1) for piece in pieces]
        hidden, slope, b_field = dense(
            lay, pieces, tables, x_back, points[n], point_bias, mixers, b_field, n * per, per,
            after=columns[n + 1 : n + 2] + points[3:],
        )
        hiddens.append(hidden)
        slopes.append(slope)

    grad_b, edge = stencil(lay, b_field)

    both, column, grads, pres, sums = [], [], [], [], []
    for n in parts:
        pre, own, send, part = grad_modes(
            lay, hiddens[n], slopes[n], grad_b, x_table, tables, weights, n * per, per,
            after=both[n - 2 : n - 1] + column[n - 3 : n - 2] if n > 1 else (),
        )
        both.append(sum_cores(own, send))
        column.append(sum_depth(lay, both[n]))
        grads.append(sum_chips(lay, column[n], 1.0))
        pres.append(pre)
        sums.append(part)
    point_parts = [point_grad(lay, field_in, pres[0], both[2:3] + column[1:2])]
    point_parts.append(point_grad(lay, field_in, pres[1], both[3:4] + column[2:3]))
    point_parts.append(point_grad(lay, field_in, pres[2], column[3:4]))
    point_parts.append(point_grad(lay, field_in, pres[3]))
    sums = jnp.concatenate(sums)
    outs = jnp.sum(sums[:, : 3 * lay.pack], axis=-1).reshape(3 * lay.channels)
    bias = sums[:, 3 * lay.pack, :LANES].reshape(lay.groups, lay.pack, lay.mx)[..., 0]
    ends = jnp.sum(edge, axis=-1)
    square = lay.channels * lay.channels
    flat = jnp.concatenate(
        [
            jnp.concatenate(point_parts, axis=1).reshape(square),
            outs,
            bias.reshape(lay.channels),
            ends[:4],
        ]
    )
    flat = jnp.pad(flat, (0, -flat.shape[0] % 1024)).reshape(-1, LANES)
    flat = sum_everywhere(flat, ("gy", "gz")).reshape(-1)
    after = square + 3 * lay.channels
    ends = flat[after + lay.channels : after + lay.channels + 4]
    grad_spectral = weight_grad(lay, modes_in, by_mode(lay, jnp.concatenate(grads)))
    return (
        ends[3] / (lay.width * lay.ny * lay.nz),
        grad_spectral,
        flat[:square].reshape(lay.channels, lay.channels),
        flat[after : after + lay.channels],
        flat[square:after].reshape(lay.channels, 3),
        ends[:3],
    )


def solution(mesh):
    return jax.shard_map(
        on_device,
        mesh=mesh,
        in_specs=(P(None, "gy", "gz", None), P("gz", "gy", None, None, None), P(), P(), P(), P()),
        out_specs=(P(), P("gz", "gy", None, None, None), P(), P(), P(), P()),
        check_vma=False,
    )
```

```python
import functools
import math

import jax
import jax.numpy as jnp
from jax import lax
from jax.experimental import pallas as pl
from jax.experimental.pallas import tpu as pltpu
from jax.sharding import PartitionSpec as P

F32 = jnp.float32
BF16 = jnp.bfloat16
CORES = 2
LANES = 128
VMEM_LIMIT = 56 * 1024 * 1024
PARTS = 2
CHUNK = 256


def params():
    return pltpu.CompilerParams(
        vmem_limit_bytes=VMEM_LIMIT, dimension_semantics=("arbitrary",)
    )


def whole(shape):
    return pl.BlockSpec(shape, lambda i: (0,) * len(shape), pipeline_mode=pl.Buffered(1))


ANY = pl.BlockSpec(memory_space=pl.ANY)


def cost(flops, moved):
    return pl.CostEstimate(flops=flops, bytes_accessed=moved, transcendentals=0)


def dot(a, b):
    return jnp.dot(a, b, preferred_element_type=F32)


def frequencies(mode_index, mode_total):
    return jnp.where(mode_index < mode_total // 2, mode_index, mode_index - mode_total)


def twiddle(product, length):
    phases = (product % length).astype(F32) * (2.0 * math.pi / length)
    return jnp.cos(phases).astype(BF16).astype(F32), jnp.sin(phases).astype(BF16).astype(F32)


def halo(lay, block):
    sizes = {"gy": lay.n_gy, "gz": lay.n_gz}

    def cut(dim, step):
        count = block.shape[dim]
        return slice(None) if step == 0 else slice(count - 2, count) if step > 0 else slice(0, 2)

    def moved(y_step, z_step):
        pairs = [
            (y * lay.n_gz + z, (y + y_step) * lay.n_gz + z + z_step)
            for y in range(sizes["gy"])
            for z in range(sizes["gz"])
            if 0 <= y + y_step < sizes["gy"] and 0 <= z + z_step < sizes["gz"]
        ]
        return lax.ppermute(block[:, cut(1, y_step), cut(2, z_step)], ("gy", "gz"), pairs)

    steps = [(1, 0), (-1, 0), (0, 1), (0, -1), (1, 1), (1, -1), (-1, 1), (-1, -1)]
    return [moved(*step) for step in steps]


class Layout:
    def __init__(self, field_in, spectral_weight):
        self.channels, self.rows, self.depth, self.width = field_in.shape
        self.kz, self.ky, self.mx = spectral_weight.shape[:3]
        self.n_gy, self.n_gz = lax.axis_size("gy"), lax.axis_size("gz")
        self.chips = self.n_gy // CORES
        self.ny, self.nz = self.rows * self.n_gy, self.depth * self.n_gz
        self.my, self.mz = self.ky * self.n_gy, self.kz * self.n_gz
        self.cells = self.rows * self.depth
        self.modes = self.my * self.mz
        self.pack = LANES // self.mx
        self.groups = self.channels // self.pack
        self.own = self.ky * self.kz
        self.band = min(LANES // self.depth, self.rows)
        self.blocks = self.rows // self.band
        self.step = min(LANES // self.rows, self.kz)
        self.tile = 8
        self.gy, self.gz = lax.axis_index("gy"), lax.axis_index("gz")
        self.y0 = self.gy * self.rows
        self.z0 = self.gz * self.depth

    def grid_table(self, mode, cell, first, length, same):
        real, imag = twiddle(mode * (first + cell[0]), length)
        return jnp.where(same, jnp.where(cell[1] == 0, real, imag), 0.0).astype(BF16)

    def grid_tables(self):
        core, chip = self.gy % CORES, self.gy // CORES

        def iotas(rows, columns):
            shape = (rows, columns)
            row = lax.broadcasted_iota(jnp.int32, shape, 0)
            return row, lax.broadcasted_iota(jnp.int32, shape, 1)

        def kz(n):
            return frequencies(((n // self.kz) ^ self.gz) * self.kz + n % self.kz, self.mz)

        def ky(n):
            h, f = n // (self.chips * self.ky), n // self.ky % self.chips
            return frequencies(((f ^ chip) * CORES + (h ^ core)) * self.ky + n % self.ky, self.my)

        band, step, depth = self.band, self.step, self.depth
        z_modes, y_modes = self.mz * band, self.my * step
        z_cells, y_cells = band * depth, self.blocks * step * band
        m, c = iotas(z_modes, 2 * z_cells)
        z_forward = self.grid_table(
            kz(m // band), (c % depth, c // z_cells), self.z0, self.nz,
            m % band == c // depth % band,
        )
        c, m = iotas(z_cells, 2 * z_modes)
        z_back = self.grid_table(
            kz(m % z_modes // band), (c % depth, m // z_modes), self.z0, self.nz,
            m % band == c // depth,
        )

        def row_of(c):
            return c // (step * band) % self.blocks * band + c % band

        m, c = iotas(y_modes, 2 * y_cells)
        y_forward = self.grid_table(
            ky(m // step), (row_of(c), c // y_cells), self.y0, self.ny,
            m % step == c // band % step,
        )
        c, m = iotas(y_cells, 2 * y_modes)
        y_back = self.grid_table(
            ky(m % y_modes // step), (row_of(c), m // y_modes), self.y0, self.ny,
            m % step == c // band % step,
        )
        return z_forward, y_forward, y_back, z_back

    def x_tables(self):
        shape = (self.width, 2 * LANES)
        x = lax.broadcasted_iota(jnp.int32, shape, 0)
        lane = lax.broadcasted_iota(jnp.int32, shape, 1)
        cos, sin = twiddle(x * frequencies(lane % self.mx, self.mx), self.width)
        table = jnp.where(lane < LANES, cos, -sin).astype(BF16)
        owner = lane % LANES // self.mx
        forward = [jnp.where(owner == c, table, 0) for c in range(self.pack)]
        lane, x = (lax.broadcasted_iota(jnp.int32, shape[::-1], d) for d in range(2))
        cos, sin = twiddle(x * frequencies(lane % self.mx, self.mx), self.width)
        table = jnp.where(lane < LANES, cos, -sin).astype(BF16)
        owner = lane % LANES // self.mx
        inverse = [jnp.where(owner == c, table, 0) for c in range(self.pack)]
        return jnp.concatenate(forward, axis=0), jnp.concatenate(inverse, axis=1)


def turn(values, sign):
    real, imag = values[:, :LANES], values[:, LANES:]
    return jnp.concatenate([imag, -real] if sign > 0 else [-imag, real], axis=1)


def z_transform(x_modes, table_ref, part_ref, n):
    x_modes = x_modes.astype(BF16)
    rhs = jnp.concatenate([x_modes, turn(x_modes, 1)], axis=0)
    modes = dot(table_ref[...], rhs).astype(BF16)
    steps, _, _, size, _ = part_ref.shape
    part_ref[:, 0, n] = modes.reshape(steps, size, 2 * LANES)
    part_ref[:, 1, n] = turn(modes, 1).reshape(steps, size, 2 * LANES)


def y_transform(table_ref, part_ref, own_ref, send_ref):
    half = table_ref.shape[0] // 2
    steps, _, blocks, size, _ = part_ref.shape
    chips = own_ref.shape[1]
    rows = half // chips
    per = steps // own_ref.shape[0]
    for q in range(steps):
        modes = dot(table_ref[...], part_ref[q].reshape(2 * blocks * size, 2 * LANES))
        modes = modes.astype(BF16)
        here = pl.ds(q % per * rows, rows)
        own_ref[q // per, :, 0, here] = modes[:half].reshape(chips, rows, 2 * LANES)
        send_ref[q // per, :, 0, here] = modes[half:].reshape(chips, rows, 2 * LANES)


def x_transform(source_ref, x_ref):
    pack, rows, depth, width = source_ref.shape
    cells = [source_ref[c].reshape(rows * depth, width) for c in range(pack)]
    return dot(jnp.concatenate(cells, axis=1), x_ref[...])


def modes_kernel(n_after, field_ref, x_ref, z_ref, y_ref, *refs):
    own_ref, send_ref, part_ref = refs[n_after:]
    total = x_transform(field_ref, x_ref)
    blocks = part_ref.shape[2]
    size = total.shape[0] // blocks
    for n in range(blocks):
        z_transform(total[n * size : (n + 1) * size], z_ref, part_ref, n)
    y_transform(y_ref, part_ref, own_ref, send_ref)


def mode_blocks(lay, count):
    shape = (lay.n_gz, lay.chips, count, lay.own, 2 * LANES)
    spec = pl.BlockSpec((lay.n_gz, lay.chips, 1, lay.own, 2 * LANES), lambda i: (0, 0, i, 0, 0))
    return jax.ShapeDtypeStruct(shape, BF16), spec


def part_scratch(lay):
    size = lay.step * lay.band
    return pltpu.VMEM((lay.mz // lay.step, 2, lay.blocks, size, 2 * LANES), BF16)


def forward_modes(lay, field_in, x_table, tables, first, count, after=()):
    out, spec = mode_blocks(lay, count)
    block = (lay.pack, lay.rows, lay.depth, lay.width)
    volume = lay.pack * lay.cells * lay.width
    return pl.pallas_call(
        functools.partial(modes_kernel, len(after)),
        grid=(count,),
        in_specs=[
            pl.BlockSpec(block, lambda i: (first + i, 0, 0, 0)),
            whole(x_table.shape),
            whole(tables[0].shape),
            whole(tables[1].shape),
        ]
        + [ANY] * len(after),
        out_specs=[spec, spec],
        out_shape=[out, out],
        scratch_shapes=[part_scratch(lay)],
        compiler_params=params(),
        cost_estimate=cost(count * volume * 2 * 2 * LANES, count * volume * 3),
        name="forward_modes",
    )(field_in, x_table, tables[0], tables[1], *after)


def exchange(value, axis, distance):
    count = lax.axis_size(axis)
    return lax.ppermute(value, axis, [(i, i ^ distance) for i in range(count)])


def sum_kernel(n_in, n_out, factor, *refs):
    total = refs[0][...].astype(F32)
    for ref in refs[1:n_in]:
        total = total + ref[...].astype(F32)
    total = (total * factor).astype(BF16)
    for n, out_ref in enumerate(refs[-n_out:]):
        out_ref[...] = total[n] if n_out > 1 else total


def sum_blocks(values, split, factor=1.0, after=()):
    shape = values[0].shape
    out = shape[1:] if split else shape
    count = shape[-3]

    def spec(sizes):
        lead = len(sizes) - 3
        block = sizes[:lead] + (1,) + sizes[lead + 1 :]
        return pl.BlockSpec(block, lambda i: (0,) * lead + (i, 0, 0))

    n_out = shape[0] if split else 1
    total = math.prod(shape)
    outs = pl.pallas_call(
        functools.partial(sum_kernel, len(values), n_out, factor),
        grid=(count,),
        in_specs=[spec(shape)] * len(values) + [ANY] * len(after),
        out_specs=[spec(out)] * n_out,
        out_shape=[jax.ShapeDtypeStruct(out, BF16)] * n_out,
        compiler_params=params(),
        cost_estimate=cost(total * len(values), total * 2 * (len(values) + 1)),
        name="sum_blocks",
    )(*values, *after)
    return list(outs)


def from_cores(own, send, after=()):
    return sum_blocks([own, exchange(send, "gy", 1)], True, after=after)


def from_depth(blocks, after=()):
    return sum_blocks(
        blocks[:1] + [exchange(block, "gz", d) for d, block in enumerate(blocks) if d], True,
        after=after,
    )


def from_chips(blocks, factor, after=()):
    got = [exchange(block, "gy", d * CORES) for d, block in enumerate(blocks) if d]
    return sum_blocks(blocks[:1] + got, False, factor, after)[0]


def stack_kernel(n_in, *refs):
    for n in range(n_in):
        refs[-1][n] = refs[n][...]


def stack_blocks(values, after=()):
    shape = values[0].shape
    count = shape[-3]

    def spec(sizes):
        lead = len(sizes) - 3
        block = sizes[:lead] + (1,) + sizes[lead + 1 :]
        return pl.BlockSpec(block, lambda i: (0,) * lead + (i, 0, 0))

    out = (len(values),) + shape
    return pl.pallas_call(
        functools.partial(stack_kernel, len(values)),
        grid=(count,),
        in_specs=[spec(shape)] * len(values) + [ANY] * len(after),
        out_specs=spec(out),
        out_shape=jax.ShapeDtypeStruct(out, BF16),
        compiler_params=params(),
        cost_estimate=cost(math.prod(out), 4 * math.prod(out)),
        name="stack_blocks",
    )(*values, *after)


def spread_chips(lay, mine):
    return stack_blocks([mine] + [exchange(mine, "gy", d * CORES) for d in range(1, lay.chips)])


def spread_depth(lay, column, after=()):
    pieces = [column] + [exchange(column, "gz", d) for d in range(1, lay.n_gz)]
    return stack_blocks(pieces, after)


def by_mode(lay, modes):
    count = modes.shape[0]
    split = modes.reshape(
        count, lay.kz // lay.step, lay.ky, lay.step, 2, lay.pack, lay.mx
    )
    return jnp.transpose(split, (1, 3, 2, 4, 6, 0, 5)).reshape(
        lay.kz, lay.ky, 2 * lay.mx, count * lay.pack
    )


def by_group(lay, modes):
    split = modes.reshape(
        lay.kz // lay.step, lay.step, lay.ky, lay.mx, 2, lay.groups, lay.pack
    )
    return jnp.transpose(split, (5, 0, 2, 1, 4, 6, 3)).reshape(
        lay.groups, lay.own, 2 * LANES
    )


def mix_kernel(modes_ref, weight_ref, *refs):
    out_ref = refs[-1]
    pair, count, channels, wide = weight_ref.shape[1:]
    per = wide // channels
    spread = []
    for a in range(pair):
        modes = jnp.concatenate([modes_ref[0, a]] * per, axis=1)
        row = lax.broadcasted_iota(jnp.int32, modes.shape, 0) % count
        owner = lax.broadcasted_iota(jnp.int32, modes.shape, 1) // channels
        zero = jnp.zeros_like(modes)
        parts = [jnp.where(row == owner + n * per, modes, zero) for n in range(count // per)]
        spread.append(jnp.concatenate(parts, axis=1))
    weights = [weight_ref[0, a].reshape(count * channels, wide) for a in range(pair)]
    mixed = dot(jnp.concatenate(spread, axis=0), jnp.concatenate(weights, axis=1))
    for a in range(pair):
        own = mixed[2 * count * a : 2 * count * (a + 1), wide * a : wide * (a + 1)]
        real, imag = own[:count], own[count:]
        turned = jnp.concatenate([-imag[:, channels:], imag[:, :channels]], axis=1)
        out_ref[0, a] = (real + turned).astype(BF16)


def mode_spec(lay, shape):
    per = lay.ky // 2
    return pl.BlockSpec((1, 2) + shape, lambda i: (i // per, i % per) + (0,) * len(shape))


def mix_modes(lay, modes_in, spectral_weight, after=()):
    shape = (lay.mx, 2 * lay.channels)
    return pl.pallas_call(
        mix_kernel,
        grid=(lay.own // 2,),
        in_specs=[mode_spec(lay, modes_in.shape[2:]), mode_spec(lay, spectral_weight.shape[2:])]
        + [ANY] * len(after),
        out_specs=mode_spec(lay, shape),
        out_shape=jax.ShapeDtypeStruct((lay.kz, lay.ky) + shape, BF16),
        compiler_params=params(),
        cost_estimate=cost(spectral_weight.size * 8, spectral_weight.size * 2),
        name="mix_modes",
    )(modes_in, spectral_weight, *after)


def pointwise_kernel(tile, field_ref, weight_ref, bias_ref, *refs):
    out_ref, blocks_ref, shift_ref = refs[-3:]
    channels, rows, depth, width = field_ref.shape

    @pl.when(pl.program_id(0) == 0)
    def _():
        shape = (tile * channels, channels)
        split = lax.broadcasted_iota(jnp.int32, shape, 0) // tile
        split = split == lax.broadcasted_iota(jnp.int32, shape, 1)
        shift = jnp.sum(jnp.where(split, bias_ref[...], 0.0), axis=1, keepdims=True)
        shift_ref[...] = jnp.broadcast_to(shift, shift_ref.shape)
        split = split.astype(BF16)
        wide = dot(split, weight_ref[...]).astype(BF16)
        wide = lax.dot_general(
            wide, split, (((1,), (1,)), ((), ())), preferred_element_type=F32
        )
        row = lax.broadcasted_iota(jnp.int32, wide.shape, 0) % tile
        column = lax.broadcasted_iota(jnp.int32, wide.shape, 1) % tile
        blocks_ref[...] = jnp.where(row == column, wide, 0.0).astype(BF16)

    for y in range(rows):
        for z in range(0, depth, tile):
            cells = field_ref[:, y, z : z + tile, :].reshape(channels * tile, width)
            mixed = (dot(blocks_ref[...], cells) + shift_ref[...]).astype(BF16)
            out_ref[:, y, z : z + tile, :] = mixed.reshape(channels, tile, width)


def pointwise(lay, field_in, weight, bias, first, count, done=None, after=()):
    span = 2
    size = lay.channels * lay.tile
    given = [] if done is None else [done]
    block = pl.BlockSpec(
        (lay.channels, span, lay.depth, lay.width), lambda i: (0, first // span + i, 0, 0)
    )
    return pl.pallas_call(
        functools.partial(pointwise_kernel, lay.tile),
        grid=(count // span,),
        in_specs=[block, whole(weight.shape), whole(bias.shape)]
        + [ANY] * (len(given) + len(after)),
        out_specs=block,
        out_shape=jax.ShapeDtypeStruct(field_in.shape, BF16),
        scratch_shapes=[pltpu.VMEM((size, size), BF16), pltpu.VMEM((size, lay.width), F32)],
        input_output_aliases={3: 0} if given else {},
        compiler_params=params(),
        cost_estimate=cost(
            2 * size * lay.channels * count * lay.depth * lay.width,
            4 * lay.channels * count * lay.depth * lay.width,
        ),
        name="pointwise",
    )(field_in, weight, bias, *given, *after)


def gelu_and_slope(v):
    bell = jnp.exp2(v * v * (-0.5 * math.log2(math.e)))
    base = 1.0 + jnp.abs(v) * (0.3275911 / math.sqrt(2.0))
    t = pl.reciprocal(base, approx=True)
    poly = 0.5 * 1.061405429
    for coefficient in (-1.453152027, 1.421413741, -0.284496736, 0.254829592):
        poly = poly * t + 0.5 * coefficient
    tail = poly * t * bell
    cdf = jnp.where(v >= 0.0, 1.0 - tail, tail)
    return v * cdf, cdf + v * (bell * (1.0 / math.sqrt(2.0 * math.pi)))


def dense_kernel(
    first, own_ref, other_ref, y_ref, z_ref, x_ref, point_ref, weight_ref, b_in_ref, *refs
):
    hidden_ref, slope_ref, b_ref, part_ref, even_ref, odd_ref = refs[-6:]
    pack, rows, depth, width = point_ref.shape
    blocks, _, steps, size, _ = part_ref.shape
    band = rows // blocks
    step = pl.program_id(0)

    @pl.when(step == 0)
    def _():
        b_ref[...] = b_in_ref[...]

    depths, chips = own_ref.shape[:2]
    per = steps // depths
    rows_here = own_ref.shape[3] // per
    for q in range(steps):
        here = pl.ds(q % per * rows_here, rows_here)
        chunks = [
            piece[q // per, :, 0, here].reshape(chips * rows_here, 2 * LANES)
            for piece in (own_ref, other_ref)
        ]
        modes = jnp.concatenate(chunks, axis=0)
        back = dot(y_ref[...], jnp.concatenate([modes, turn(modes, -1)], axis=0)).astype(BF16)
        part_ref[:, 0, q] = back.reshape(blocks, size, 2 * LANES)
        part_ref[:, 1, q] = turn(back, -1).reshape(blocks, size, 2 * LANES)
    channel = (first + step) * pack

    per = even_ref.shape[0] // (band * depth)
    span = per * band
    count = rows // span

    def spectral(out_ref, n):
        cells = [
            dot(z_ref[...], part_ref[n * per + m].reshape(2 * steps * size, 2 * LANES))
            for m in range(per)
        ]
        out_ref[...] = dot(jnp.concatenate(cells, axis=0).astype(BF16), x_ref[...])

    def activate(spectral_ref, n):
        for m in range(span):
            y = n * span + m
            parts = [b_ref[b, y] for b in range(3)]
            for c in range(pack):
                value = spectral_ref[m * depth : (m + 1) * depth, c * width : (c + 1) * width]
                value = value + point_ref[c, y].astype(F32)
                hidden, slope = gelu_and_slope(value)
                hidden = hidden.astype(BF16)
                hidden_ref[c, y] = hidden
                slope_ref[c, y] = slope.astype(BF16)
                hidden = hidden.astype(F32)
                parts = [parts[b] + hidden * weight_ref[channel + c, b] for b in range(3)]
            for b in range(3):
                b_ref[b, y] = parts[b]

    spectral(even_ref, 0)
    if count == 1:
        activate(even_ref, 0)
        return

    def body(m, carry):
        spectral(odd_ref, 2 * m + 1)
        activate(even_ref, 2 * m)
        spectral(even_ref, jnp.minimum(2 * m + 2, count - 1))
        activate(odd_ref, 2 * m + 1)
        return carry

    lax.fori_loop(0, count // 2, body, 0)


def dense(lay, own, other, tables, x_table, point, weights, b_in, first, count, after=()):
    size = (lay.n_gz, lay.chips, 1, lay.own, 2 * LANES)
    modes = pl.BlockSpec(size, lambda i: (0, 0, i, 0, 0))
    block = (lay.pack, lay.rows, lay.depth, lay.width)
    part = pl.BlockSpec(block, lambda i: (i, 0, 0, 0))
    kept = jax.ShapeDtypeStruct((count * lay.pack,) + block[1:], BF16)
    volume = lay.pack * lay.cells * lay.width
    steps = lay.mz // lay.step
    return pl.pallas_call(
        functools.partial(dense_kernel, first),
        grid=(count,),
        in_specs=[
            modes,
            modes,
            whole(tables[2].shape),
            whole(tables[3].shape),
            whole(x_table.shape),
            pl.BlockSpec(block, lambda i: (first + i, 0, 0, 0)),
            pl.BlockSpec(memory_space=pltpu.SMEM),
            whole(b_in.shape),
        ]
        + [ANY] * len(after),
        out_specs=[part, part, whole(b_in.shape)],
        out_shape=[kept, kept, jax.ShapeDtypeStruct(b_in.shape, F32)],
        scratch_shapes=[
            pltpu.VMEM((lay.blocks, 2, steps, lay.step * lay.band, 2 * LANES), BF16),
            pltpu.VMEM((CHUNK, lay.pack * lay.width), F32),
            pltpu.VMEM((CHUNK, lay.pack * lay.width), F32),
        ],
        compiler_params=params(),
        cost_estimate=cost(count * volume * 2 * 6 * LANES, count * volume * 24),
        name="dense",
    )(own, other, tables[2], tables[3], x_table, point, weights, b_in, *after)


def stencil_kernel(total_y, total_z, origin_ref, field_ref, *refs):
    halos, (grad_ref, sums_ref, b_ref, gy_ref, rest_ref) = refs[:8], refs[8:]
    _, rows_wide, depth_wide, width = b_ref.shape
    rows, depth = grad_ref.shape[1:3]
    low_y, high_y = pl.ds(0, 2), pl.ds(rows + 2, 2)
    low_z, high_z = pl.ds(0, 2), pl.ds(depth + 2, 2)
    mid_y, mid_z = pl.ds(2, rows), pl.ds(2, depth)
    b_ref[:, :, depth + 4 :] = jnp.zeros_like(b_ref[:, :, depth + 4 :])
    b_ref[:, mid_y, mid_z] = field_ref[...]
    places = [
        (low_y, mid_z), (high_y, mid_z), (mid_y, low_z), (mid_y, high_z),
        (low_y, low_z), (low_y, high_z), (high_y, low_z), (high_y, high_z),
    ]
    for ref, (y, z) in zip(halos, places):
        b_ref[:, y, z] = ref[...]
    shape = (depth_wide, width)
    lane = lax.broadcasted_iota(jnp.int32, shape, 1)
    z_cell = origin_ref[1] + lax.broadcasted_iota(jnp.int32, shape, 0) - 2
    z_inside = (z_cell >= 0) & (z_cell < total_z)
    z_own = lax.broadcasted_iota(jnp.int32, shape, 0)
    z_own = (z_own >= 2) & (z_own < depth + 2)
    scale = 1.0 / (total_y * total_z * width)

    def next_x(v):
        return jnp.where(lane == width - 1, 0.0, pltpu.roll(v, width - 1, 1))

    def last_x(v):
        return jnp.where(lane == 0, 0.0, pltpu.roll(v, 1, 1))

    def next_z(v):
        return pltpu.roll(v, depth_wide - 1, 0)

    def last_z(v):
        return pltpu.roll(v, 1, 0)

    def terms(n, loss):
        b = [b_ref[a, n + 1] for a in range(3)]
        dx = [(next_x(v) - last_x(v)) * 0.5 for v in b]
        dy = [(b_ref[a, n + 2] - b_ref[a, n]) * 0.5 for a in range(3)]
        dz = [(next_z(v) - last_z(v)) * 0.5 for v in b]
        jx = dy[2] - dz[1]
        jy = dz[0] - dx[2]
        jz = dx[1] - dy[0]
        fx = jy * b[2] - jz * b[1]
        fy = jz * b[0] - jx * b[2]
        fz = jx * b[1] - jy * b[0]
        q = dx[0] + dy[1] + dz[2]
        strength = b[0] * b[0] + b[1] * b[1] + b[2] * b[2] + 1.0
        inverse = 1.0 / strength
        ratio = (fx * fx + fy * fy + fz * fz) * inverse
        y_cell = origin_ref[0] + n - 1
        y_inside = (y_cell >= 0) & (y_cell < total_y)
        own = z_own & (n >= 1) & (n <= rows)
        loss = loss + jnp.where(own, ratio + q * q, 0.0)
        weight = jnp.where(z_inside & y_inside, 2.0 * scale, 0.0)
        inverse = inverse * weight
        pull = ratio * inverse
        fx, fy, fz = fx * inverse, fy * inverse, fz * inverse
        q = q * weight
        cx = b[1] * fz - b[2] * fy
        cy = b[2] * fx - b[0] * fz
        cz = b[0] * fy - b[1] * fx
        db = [
            fy * jz - fz * jy - pull * b[0],
            fz * jx - fx * jz - pull * b[1],
            fx * jy - fy * jx - pull * b[2],
        ]
        gx = [q, cz, -cy]
        gy = [-cz, q, cx]
        gz = [cy, -cx, q]
        for a in range(3):
            gy_ref[a, n] = gy[a]
            back = last_x(gx[a]) - next_x(gx[a]) + last_z(gz[a]) - next_z(gz[a])
            rest_ref[a, n] = db[a] + back * 0.5
        return loss

    loss = lax.fori_loop(0, rows + 2, terms, jnp.zeros(shape, F32))

    def combine(n, sums):
        done = []
        for a in range(3):
            grad = rest_ref[a, n + 1] + (gy_ref[a, n] - gy_ref[a, n + 2]) * 0.5
            grad = grad[2 : depth + 2]
            grad_ref[a, n] = grad
            done.append(sums[a] + grad)
        return tuple(done)

    sums = lax.fori_loop(0, rows, combine, (jnp.zeros((depth, width), F32),) * 3)
    sums_ref[...] = jnp.zeros_like(sums_ref)
    for a in range(3):
        sums_ref[a : a + 1, :] = jnp.sum(sums[a], axis=0, keepdims=True)
    sums_ref[3:4, :] = jnp.sum(loss, axis=0, keepdims=True)


def stencil(lay, b_field):
    halos = halo(lay, b_field)
    origin = jnp.stack([lay.y0, lay.z0]).astype(jnp.int32)
    wide = (3, lay.rows + 2, lay.depth + 8, lay.width)
    return pl.pallas_call(
        functools.partial(stencil_kernel, lay.ny, lay.nz),
        in_specs=[
            pl.BlockSpec(memory_space=pltpu.SMEM),
        ]
        + [pl.BlockSpec(memory_space=pltpu.VMEM)] * 9,
        out_specs=[pl.BlockSpec(memory_space=pltpu.VMEM)] * 2,
        out_shape=[
            jax.ShapeDtypeStruct(b_field.shape, F32),
            jax.ShapeDtypeStruct((8, lay.width), F32),
        ],
        scratch_shapes=[
            pltpu.VMEM((3, lay.rows + 4) + wide[2:], F32),
            pltpu.VMEM(wide, F32),
            pltpu.VMEM(wide, F32),
        ],
        compiler_params=pltpu.CompilerParams(vmem_limit_bytes=VMEM_LIMIT),
        name="stencil",
    )(origin, b_field, *halos)


def grad_kernel(first, n_after, weight_ref, hidden_ref, slope_ref, grad_ref, x_ref, z_ref, y_ref,
                *refs):
    pre_ref, own_ref, send_ref, sums_ref, part_ref = refs[n_after:]
    pack, rows, depth, width = hidden_ref.shape
    blocks = part_ref.shape[2]
    band = rows // blocks
    channel = (first + pl.program_id(0)) * pack

    def fold(v):
        return jnp.sum(v.reshape(-1, 8, width), axis=0)

    per = max(CHUNK // (band * depth), 1)
    span = per * band
    count = rows // span

    def slopes(n):
        sums = [0.0] * (3 * pack)
        for y in range(n * span, (n + 1) * span):
            grads = [grad_ref[b, y] for b in range(3)]
            for c in range(pack):
                w = [weight_ref[channel + c, b] for b in range(3)]
                mixed = grads[0] * w[0] + grads[1] * w[1] + grads[2] * w[2]
                pre_ref[c, y] = (mixed * slope_ref[c, y].astype(F32)).astype(BF16)
                hidden = hidden_ref[c, y].astype(F32)
                for b in range(3):
                    sums[3 * c + b] = sums[3 * c + b] + fold(hidden * grads[b])
        return sums

    def transform(n):
        total = x_transform(pre_ref.at[:, n * span : (n + 1) * span], x_ref)
        for m in range(per):
            here = total[m * band * depth : (m + 1) * band * depth]
            z_transform(here, z_ref, part_ref, n * per + m)
        return fold(total)

    parts = [slopes(0)]
    totals = []
    for n in range(1, count):
        parts.append(slopes(n))
        totals.append(transform(n - 1))
    totals.append(transform(count - 1))
    sums = [sum(column[1:], column[0]) for column in zip(*parts)]
    sums.append(sum(totals[1:], totals[0]))
    sums_ref[...] = jnp.zeros_like(sums_ref)
    for n, part in enumerate(sums):
        sums_ref[0, n : n + 1, :] = jnp.sum(part, axis=0, keepdims=True)
    y_transform(y_ref, part_ref, own_ref, send_ref)


def grad_modes(lay, hidden, slope, grad_b, x_table, tables, weights, first, count, after=()):
    out, spec = mode_blocks(lay, count)
    block = (lay.pack, lay.rows, lay.depth, lay.width)
    part = pl.BlockSpec(block, lambda i: (i, 0, 0, 0))
    volume = lay.pack * lay.cells * lay.width
    lines = -(-(3 * lay.pack + 1) // 8) * 8
    return pl.pallas_call(
        functools.partial(grad_kernel, first, len(after)),
        grid=(count,),
        in_specs=[
            pl.BlockSpec(memory_space=pltpu.SMEM),
            part,
            part,
            whole(grad_b.shape),
            whole(x_table.shape),
            whole(tables[0].shape),
            whole(tables[1].shape),
        ]
        + [ANY] * len(after),
        out_specs=[
            part,
            spec,
            spec,
            pl.BlockSpec((1, lines, lay.width), lambda i: (i, 0, 0)),
        ],
        out_shape=[
            jax.ShapeDtypeStruct(hidden.shape, BF16),
            out,
            out,
            jax.ShapeDtypeStruct((count, lines, lay.width), F32),
        ],
        scratch_shapes=[part_scratch(lay)],
        compiler_params=params(),
        cost_estimate=cost(count * volume * 2 * 2 * LANES, count * volume * 10),
        name="grad_modes",
    )(weights, hidden, slope, grad_b, x_table, tables[0], tables[1], *after)


def point_kernel(tile, n_after, field_ref, grad_ref, *refs):
    out_ref, acc_ref = refs[n_after:]
    channels, rows, depth, width = field_ref.shape
    count = grad_ref.shape[0]
    step = pl.program_id(0)

    @pl.when(step == 0)
    def _():
        acc_ref[...] = jnp.zeros_like(acc_ref)

    left, right = [], []
    for y in range(rows):
        for z in range(0, depth, tile):
            left.append(field_ref[:, y, z : z + tile, :].reshape(channels * tile, width))
            right.append(grad_ref[:, y, z : z + tile, :].reshape(count * tile, width))
    acc_ref[...] += lax.dot_general(
        jnp.concatenate(left, axis=1),
        jnp.concatenate(right, axis=1),
        (((1,), (1,)), ((), ())),
        preferred_element_type=F32,
    )

    @pl.when(step == pl.num_programs(0) - 1)
    def _():
        def pick(n):
            owner = lax.broadcasted_iota(jnp.int32, (n, n * tile), 1) // tile
            return (owner == lax.broadcasted_iota(jnp.int32, (n, n * tile), 0)).astype(F32)

        row = lax.broadcasted_iota(jnp.int32, acc_ref.shape, 0)
        column = lax.broadcasted_iota(jnp.int32, acc_ref.shape, 1)
        kept = jnp.where(row % tile == column % tile, acc_ref[...], 0.0)
        half = jnp.dot(
            pick(channels), kept, precision=lax.Precision.HIGHEST, preferred_element_type=F32
        )
        out_ref[...] = lax.dot_general(
            half,
            pick(count),
            (((1,), (1,)), ((), ())),
            precision=lax.Precision.HIGHEST,
            preferred_element_type=F32,
        )


def point_grad(lay, field_in, grad_pre, after=()):
    span = 4

    def block(count):
        return pl.BlockSpec((count, span, lay.depth, lay.width), lambda i: (0, i, 0, 0))

    count = grad_pre.shape[0]
    size = lay.channels * lay.tile
    return pl.pallas_call(
        functools.partial(point_kernel, lay.tile, len(after)),
        grid=(lay.rows // span,),
        in_specs=[block(lay.channels), block(count)] + [ANY] * len(after),
        out_specs=pl.BlockSpec((lay.channels, count), lambda i: (0, 0)),
        out_shape=jax.ShapeDtypeStruct((lay.channels, count), F32),
        scratch_shapes=[pltpu.VMEM((size, count * lay.tile), F32)],
        compiler_params=params(),
        cost_estimate=cost(2 * size * count * lay.cells * lay.width, 3 * field_in.size),
        name="point_grad",
    )(field_in, grad_pre, *after)


def join_kernel(n_in, *refs):
    refs[-1][...] = jnp.concatenate([ref[...] for ref in refs[:n_in]], axis=1)


def join(values, after=()):
    vmem = pl.BlockSpec(memory_space=pltpu.VMEM)
    rows = values[0].shape[0]
    out = (rows, sum(value.shape[1] for value in values))
    return pl.pallas_call(
        functools.partial(join_kernel, len(values)),
        in_specs=[vmem] * len(values) + [ANY] * len(after),
        out_specs=vmem,
        out_shape=jax.ShapeDtypeStruct(out, values[0].dtype),
        name="join",
    )(*values, *after)


def outer_kernel(modes_ref, grads_ref, out_ref):
    pair, count, channels, wide = out_ref.shape[1:]
    columns = jnp.concatenate([modes_ref[0, a] for a in range(pair)], axis=1)
    rows = []
    for a in range(pair):
        right = grads_ref[0, a]
        turned = jnp.concatenate([right[:, channels:], -right[:, :channels]], axis=1)
        right = jnp.concatenate([right, turned], axis=0)
        zero = jnp.zeros_like(right)
        rows.append(jnp.concatenate([right if n == a else zero for n in range(pair)], axis=1))
    rows = jnp.concatenate(rows, axis=0)
    owner = lax.broadcasted_iota(jnp.int32, columns.shape, 1) % count
    zero = jnp.zeros_like(columns)
    some = 8
    for k in range(0, count, some):
        left = [jnp.where(owner == k + n, columns, zero) for n in range(some)]
        out = dot(jnp.concatenate(left, axis=0), rows)
        for a in range(pair):
            here = out[:, wide * a : wide * (a + 1)]
            out_ref[0, a, k : k + some] = here.reshape(some, channels, wide)


def weight_grad(lay, modes_in, grads):
    columns = jnp.transpose(modes_in, (0, 1, 3, 2))
    rows = jnp.concatenate([grads[:, :, : lay.mx], grads[:, :, lay.mx :]], axis=-1)
    tile = (lay.mx, lay.channels, 2 * lay.channels)
    shape = (lay.kz, lay.ky) + tile
    return pl.pallas_call(
        outer_kernel,
        grid=(lay.own // 2,),
        in_specs=[mode_spec(lay, columns.shape[2:]), mode_spec(lay, rows.shape[2:])],
        out_specs=mode_spec(lay, tile),
        out_shape=jax.ShapeDtypeStruct(shape, F32),
        compiler_params=params(),
        cost_estimate=cost(math.prod(shape) * 4, math.prod(shape) * 4),
        name="weight_grad",
    )(columns, rows)


def on_device(field_in, spectral_weight, point_weight, point_bias, out_weight, out_bias):
    lay = Layout(field_in, spectral_weight)
    tables = lay.grid_tables()
    x_table, x_back = lay.x_tables()
    weights = out_weight.astype(F32)
    per = lay.groups // PARTS
    parts = range(PARTS)
    scale = math.sqrt(lay.mx * lay.my * lay.mz / (lay.width * lay.ny * lay.nz))
    half = lay.rows // 2

    def point(n, done, after):
        bias = point_bias.reshape(1, lay.channels)
        return pointwise(lay, field_in, point_weight.T, bias, n * half, half, done, after)

    both, column = [], []
    for n in parts:
        own, send = forward_modes(
            lay, field_in, x_table, tables, n * per, per, after=[b[0] for b in both[n - 1 : n]]
        )
        both.append(from_cores(own, send))
    column.append(from_depth(both[0], both[1][:1]))
    done = point(0, None, column[0][:1])
    column.append(from_depth(both[1], [done]))
    modes = [from_chips(column[0], scale, [done])]
    done = point(1, done, column[1][:1] + modes)
    modes.append(from_chips(column[1], scale, [done]))
    modes_in = by_mode(lay, jnp.concatenate(modes))
    mixed = mix_modes(lay, modes_in, spectral_weight, after=[done])
    mine = by_group(lay, mixed.reshape(lay.kz, lay.ky, lay.mx, 2, lay.groups, lay.pack))

    b_field = jnp.broadcast_to(
        out_bias[:, None, None, None], (3, lay.rows, lay.depth, lay.width)
    ).astype(F32)
    hiddens, slopes = [], []
    columns = [spread_chips(lay, mine[n * per : (n + 1) * per]) for n in parts]
    for n in parts:
        own = spread_depth(lay, columns[n], columns[n + 1 : n + 2] if n == 0 else [b_field])
        hidden, slope, b_field = dense(
            lay, own, exchange(own, "gy", 1), tables, x_back, done, weights, b_field,
            n * per, per,
        )
        hiddens.append(hidden)
        slopes.append(slope)

    grad_b, edge = stencil(lay, b_field)

    both, column, pres, sums = [], [], [], []
    for n in parts:
        pre, own, send, part = grad_modes(
            lay, hiddens[n], slopes[n], grad_b, x_table, tables, weights, n * per, per,
            after=[b[0] for b in both[n - 1 : n]],
        )
        both.append(from_cores(own, send))
        pres.append(pre)
        sums.append(part)
    column.append(from_depth(both[0], both[1][:1]))
    point_parts = [point_grad(lay, field_in, pres[0], column[0][:1])]
    column.append(from_depth(both[1], point_parts[:1]))
    grads = [from_chips(column[0], 1.0, point_parts)]
    point_parts.append(point_grad(lay, field_in, pres[1], column[1][:1] + grads))
    grads.append(from_chips(column[1], 1.0, point_parts[1:]))
    sums = jnp.concatenate(sums)
    outs = jnp.sum(sums[:, : 3 * lay.pack], axis=-1).reshape(3 * lay.channels)
    bias = sums[:, 3 * lay.pack, :LANES].reshape(lay.groups, lay.pack, lay.mx)[..., 0]
    ends = jnp.sum(edge, axis=-1)
    square = lay.channels * lay.channels
    flat = jnp.concatenate(
        [
            join(point_parts, grads[-1:]).reshape(square),
            outs,
            bias.reshape(lay.channels),
            ends[:4],
        ]
    )
    flat = jnp.pad(flat, (0, -flat.shape[0] % 1024)).reshape(-1, LANES)
    flat = jnp.sum(lax.all_gather(flat, ("gy", "gz")), axis=0).reshape(-1)
    after = square + 3 * lay.channels
    ends = flat[after + lay.channels : after + lay.channels + 4]
    grad_spectral = weight_grad(lay, modes_in, by_mode(lay, jnp.concatenate(grads)))
    return (
        ends[3] / (lay.width * lay.ny * lay.nz),
        grad_spectral,
        flat[:square].reshape(lay.channels, lay.channels),
        flat[after : after + lay.channels],
        flat[square:after].reshape(lay.channels, 3),
        ends[:3],
    )


def solution(mesh):
    return jax.shard_map(
        on_device,
        mesh=mesh,
        in_specs=(P(None, "gy", "gz", None), P("gz", "gy", None, None, None), P(), P(), P(), P()),
        out_specs=(P(), P("gz", "gy", None, None, None), P(), P(), P(), P()),
        check_vma=False,
    )
```

```python
import functools
import math

import jax
import jax.numpy as jnp
from jax import lax
from jax.experimental import pallas as pl
from jax.experimental.pallas import tpu as pltpu
from jax.sharding import PartitionSpec as P

F32 = jnp.float32
BF16 = jnp.bfloat16
CORES = 2
LANES = 128
VMEM_LIMIT = 56 * 1024 * 1024
CHUNK = 256


def params():
    return pltpu.CompilerParams(
        vmem_limit_bytes=VMEM_LIMIT, dimension_semantics=("arbitrary",)
    )


def whole(shape):
    return pl.BlockSpec(shape, lambda i: (0,) * len(shape), pipeline_mode=pl.Buffered(1))


ANY = pl.BlockSpec(memory_space=pl.ANY)


def cost(flops, moved):
    return pl.CostEstimate(flops=flops, bytes_accessed=moved, transcendentals=0)


def dot(a, b):
    return jnp.dot(a, b, preferred_element_type=F32)


def frequencies(mode_index, mode_total):
    return jnp.where(mode_index < mode_total // 2, mode_index, mode_index - mode_total)


def twiddle(product, length):
    phases = (product % length).astype(F32) * (2.0 * math.pi / length)
    return jnp.cos(phases).astype(BF16).astype(F32), jnp.sin(phases).astype(BF16).astype(F32)


def halo(block):
    def moved(value, axis, step):
        count = lax.axis_size(axis)
        pairs = [(n, n + step) for n in range(count) if 0 <= n + step < count]
        return lax.ppermute(value, axis, pairs)

    low = moved(block[:, -2:], "gy", 1)
    high = moved(block[:, :2], "gy", -1)
    ends = [
        jnp.concatenate([part[:, :, cut] for part in (low, block, high)], axis=1)
        for cut in (slice(-2, None), slice(0, 2))
    ]
    return [low, high, moved(ends[0], "gz", 1), moved(ends[1], "gz", -1)]


class Layout:
    def __init__(self, field_in, spectral_weight):
        self.channels, self.rows, self.depth, self.width = field_in.shape
        self.kz, self.ky, self.mx = spectral_weight.shape[:3]
        self.n_gy, self.n_gz = lax.axis_size("gy"), lax.axis_size("gz")
        self.chips = self.n_gy // CORES
        self.ny, self.nz = self.rows * self.n_gy, self.depth * self.n_gz
        self.my, self.mz = self.ky * self.n_gy, self.kz * self.n_gz
        self.cells = self.rows * self.depth
        self.modes = self.my * self.mz
        self.pack = LANES // self.mx
        self.groups = self.channels // self.pack
        self.own = self.ky * self.kz
        self.band = min(LANES // self.depth, self.rows)
        self.blocks = self.rows // self.band
        self.step = min(LANES // self.rows, self.kz)
        self.tile = 8
        self.gy, self.gz = lax.axis_index("gy"), lax.axis_index("gz")
        self.y0 = self.gy * self.rows
        self.z0 = self.gz * self.depth

    def grid_table(self, mode, cell, first, length, same):
        real, imag = twiddle(mode * (first + cell[0]), length)
        return jnp.where(same, jnp.where(cell[1] == 0, real, imag), 0.0).astype(BF16)

    def grid_tables(self):
        core, chip = self.gy % CORES, self.gy // CORES

        def iotas(rows, columns):
            shape = (rows, columns)
            row = lax.broadcasted_iota(jnp.int32, shape, 0)
            return row, lax.broadcasted_iota(jnp.int32, shape, 1)

        def kz(n):
            return frequencies(((n // self.kz) ^ self.gz) * self.kz + n % self.kz, self.mz)

        def ky(n):
            h, f = n // (self.chips * self.ky), n // self.ky % self.chips
            return frequencies(((f ^ chip) * CORES + (h ^ core)) * self.ky + n % self.ky, self.my)

        band, step, depth = self.band, self.step, self.depth
        z_modes, y_modes = self.mz * band, self.my * step
        z_cells, y_cells = band * depth, self.blocks * step * band
        m, c = iotas(z_modes, 2 * z_cells)
        z_forward = self.grid_table(
            kz(m // band), (c % depth, c // z_cells), self.z0, self.nz,
            m % band == c // depth % band,
        )
        c, m = iotas(z_cells, 2 * z_modes)
        z_back = self.grid_table(
            kz(m % z_modes // band), (c % depth, m // z_modes), self.z0, self.nz,
            m % band == c // depth,
        )

        def row_of(c):
            return c // (step * band) % self.blocks * band + c % band

        m, c = iotas(y_modes, 2 * y_cells)
        y_forward = self.grid_table(
            ky(m // step), (row_of(c), c // y_cells), self.y0, self.ny,
            m % step == c // band % step,
        )
        c, m = iotas(y_cells, 2 * y_modes)
        y_back = self.grid_table(
            ky(m % y_modes // step), (row_of(c), m // y_modes), self.y0, self.ny,
            m % step == c // band % step,
        )
        return z_forward, y_forward, y_back, z_back

    def x_tables(self):
        shape = (self.width, 2 * LANES)
        x = lax.broadcasted_iota(jnp.int32, shape, 0)
        lane = lax.broadcasted_iota(jnp.int32, shape, 1)
        cos, sin = twiddle(x * frequencies(lane % self.mx, self.mx), self.width)
        table = jnp.where(lane < LANES, cos, -sin).astype(BF16)
        owner = lane % LANES // self.mx
        forward = [jnp.where(owner == c, table, 0) for c in range(self.pack)]
        lane, x = (lax.broadcasted_iota(jnp.int32, shape[::-1], d) for d in range(2))
        cos, sin = twiddle(x * frequencies(lane % self.mx, self.mx), self.width)
        table = jnp.where(lane < LANES, cos, -sin).astype(BF16)
        owner = lane % LANES // self.mx
        inverse = [jnp.where(owner == c, table, 0) for c in range(self.pack)]
        return jnp.concatenate(forward, axis=0), jnp.concatenate(inverse, axis=1)


def turn(values, sign):
    real, imag = values[:, :LANES], values[:, LANES:]
    return jnp.concatenate([imag, -real] if sign > 0 else [-imag, real], axis=1)


def z_transform(x_modes, table_ref, part_ref, n):
    x_modes = x_modes.astype(BF16)
    rhs = jnp.concatenate([x_modes, turn(x_modes, 1)], axis=0)
    modes = dot(table_ref[...], rhs).astype(BF16)
    steps, _, _, size, _ = part_ref.shape
    part_ref[:, 0, n] = modes.reshape(steps, size, 2 * LANES)
    part_ref[:, 1, n] = turn(modes, 1).reshape(steps, size, 2 * LANES)


def y_transform(table_ref, part_ref, own_ref, send_ref):
    half = table_ref.shape[0] // 2
    steps, _, blocks, size, _ = part_ref.shape
    chips = own_ref.shape[1]
    rows = half // chips
    per = steps // own_ref.shape[0]
    for q in range(steps):
        modes = dot(table_ref[...], part_ref[q].reshape(2 * blocks * size, 2 * LANES))
        modes = modes.astype(BF16)
        here = pl.ds(q % per * rows, rows)
        own_ref[q // per, :, 0, here] = modes[:half].reshape(chips, rows, 2 * LANES)
        send_ref[q // per, :, 0, here] = modes[half:].reshape(chips, rows, 2 * LANES)


def x_transform(source_ref, x_ref):
    pack, rows, depth, width = source_ref.shape
    cells = [source_ref[c].reshape(rows * depth, width) for c in range(pack)]
    return dot(jnp.concatenate(cells, axis=1), x_ref[...])


def modes_kernel(n_after, field_ref, x_ref, z_ref, y_ref, *refs):
    own_ref, send_ref, part_ref = refs[n_after:]
    total = x_transform(field_ref, x_ref)
    blocks = part_ref.shape[2]
    size = total.shape[0] // blocks
    for n in range(blocks):
        z_transform(total[n * size : (n + 1) * size], z_ref, part_ref, n)
    y_transform(y_ref, part_ref, own_ref, send_ref)


def mode_blocks(lay, count):
    shape = (lay.n_gz, lay.chips, count, lay.own, 2 * LANES)
    spec = pl.BlockSpec((lay.n_gz, lay.chips, 1, lay.own, 2 * LANES), lambda i: (0, 0, i, 0, 0))
    return jax.ShapeDtypeStruct(shape, BF16), spec


def part_scratch(lay):
    size = lay.step * lay.band
    return pltpu.VMEM((lay.mz // lay.step, 2, lay.blocks, size, 2 * LANES), BF16)


def forward_modes(lay, field_in, x_table, tables, first, count, after=()):
    out, spec = mode_blocks(lay, count)
    block = (lay.pack, lay.rows, lay.depth, lay.width)
    volume = lay.pack * lay.cells * lay.width
    return pl.pallas_call(
        functools.partial(modes_kernel, len(after)),
        grid=(count,),
        in_specs=[
            pl.BlockSpec(block, lambda i: (first + i, 0, 0, 0)),
            whole(x_table.shape),
            whole(tables[0].shape),
            whole(tables[1].shape),
        ]
        + [ANY] * len(after),
        out_specs=[spec, spec],
        out_shape=[out, out],
        scratch_shapes=[part_scratch(lay)],
        compiler_params=params(),
        cost_estimate=cost(count * volume * 2 * 2 * LANES, count * volume * 3),
        name="forward_modes",
    )(field_in, x_table, tables[0], tables[1], *after)


def exchange(value, axis, distance):
    count = lax.axis_size(axis)
    return lax.ppermute(value, axis, [(i, i ^ distance) for i in range(count)])


def sum_kernel(n_in, n_out, factor, *refs):
    rows = refs[0].shape[1]
    chunk = math.gcd(rows, 256)

    def body(n, carry):
        here = pl.ds(pl.multiple_of(n * chunk, chunk), chunk)
        for m, out_ref in enumerate(refs[-n_out:]):
            total = refs[0][m, here].astype(F32)
            for ref in refs[1:n_in]:
                total = total + ref[m, here].astype(F32)
            out_ref[here] = (total * factor).astype(out_ref.dtype)
        return carry

    lax.fori_loop(0, rows // chunk, body, 0)


VMEM = pl.BlockSpec(memory_space=pltpu.VMEM)


def sum_blocks(values, split, factor=1.0, after=(), weight=2):
    shape = values[0].shape
    n_out = shape[0] if split else 1
    rows = math.prod(shape[:-1]) // n_out
    values = [value.reshape(n_out, rows, shape[-1]) for value in values]
    outs = pl.pallas_call(
        functools.partial(sum_kernel, len(values), n_out, factor),
        in_specs=[VMEM] * len(values) + [ANY] * len(after),
        out_specs=[VMEM] * n_out,
        out_shape=[jax.ShapeDtypeStruct((rows, shape[-1]), values[0].dtype)] * n_out,
        compiler_params=pltpu.CompilerParams(vmem_limit_bytes=VMEM_LIMIT),
        cost_estimate=cost(math.prod(shape) * len(values), math.prod(shape) * weight * len(values)),
        name="sum_blocks",
    )(*values, *after)
    return [out.reshape(shape[1:] if split else shape) for out in outs]


def core_kernel(own_ref, other_ref, *refs):
    count = own_ref.shape[0]
    for n, out_ref in enumerate(refs[len(refs) - count :]):
        out_ref[0] = (own_ref[n, 0].astype(F32) + other_ref[n, 0].astype(F32)).astype(BF16)


def from_cores(lay, own, other, half, after=()):
    size = lay.groups // 2
    tail = (size, lay.own, 2 * LANES)
    given = pl.BlockSpec((lay.n_gz, 1) + tail, lambda i: (0, i, half, 0, 0))
    return list(
        pl.pallas_call(
            core_kernel,
            grid=(lay.chips,),
            in_specs=[given, given] + [ANY] * len(after),
            out_specs=[pl.BlockSpec((1,) + tail, lambda i: (i, 0, 0, 0))] * lay.n_gz,
            out_shape=[jax.ShapeDtypeStruct((lay.chips,) + tail, BF16)] * lay.n_gz,
            compiler_params=params(),
            cost_estimate=cost(own.size // 2, own.size * 3),
            name="core_sums",
        )(own, other, *after)
    )


def sum_all(lay, own, send, factor, work):
    other = exchange(send, "gy", 1)
    early = from_cores(lay, own, other, 0)
    done = work(0, early[:1])
    early = to_depth(early)
    late = to_depth(from_cores(lay, own, other, 1, [done, early[1]]))
    done = work(1, late[:1])
    early = sum_blocks(early, True, after=[done])
    done = work(2, early[:1])
    first = from_chips(early, factor, [done])
    late = sum_blocks(late, True, after=[first])
    return [first, from_chips(late, factor)]


def to_depth(blocks):
    return blocks[:1] + [exchange(block, "gz", d) for d, block in enumerate(blocks) if d]


def from_chips(blocks, factor, after=()):
    got = [exchange(block, "gy", d * CORES) for d, block in enumerate(blocks) if d]
    return sum_blocks(blocks[:1] + got, False, factor, after)[0]


def stack_kernel(n_in, *refs):
    out_ref, sems = refs[-2:]
    copies = [pltpu.make_async_copy(refs[n], out_ref.at[n], sems.at[n]) for n in range(n_in)]
    for copy in copies:
        copy.start()
    for copy in copies:
        copy.wait()


def stack_blocks(values, after=()):
    out = (len(values),) + values[0].shape
    return pl.pallas_call(
        functools.partial(stack_kernel, len(values)),
        in_specs=[ANY] * (len(values) + len(after)),
        out_specs=ANY,
        out_shape=jax.ShapeDtypeStruct(out, values[0].dtype),
        scratch_shapes=[pltpu.SemaphoreType.DMA((len(values),))],
        cost_estimate=cost(math.prod(out), 4 * math.prod(out)),
        name="stack_blocks",
    )(*values, *after)


def spread_chips(lay, mine):
    return stack_blocks([mine] + [exchange(mine, "gy", d * CORES) for d in range(1, lay.chips)])


def spread_depth(lay, column, after=()):
    pieces = [column] + [exchange(column, "gz", d) for d in range(1, lay.n_gz)]
    return stack_blocks(pieces, after)


def by_mode(lay, modes):
    count = modes.shape[0]
    split = modes.reshape(
        count, lay.kz // lay.step, lay.ky, lay.step, 2, lay.pack, lay.mx
    )
    return jnp.transpose(split, (1, 3, 2, 4, 6, 0, 5)).reshape(
        lay.kz, lay.ky, 2 * lay.mx, count * lay.pack
    )


def by_group(lay, modes):
    split = modes.reshape(
        lay.kz // lay.step, lay.step, lay.ky, lay.mx, 2, lay.groups, lay.pack
    )
    return jnp.transpose(split, (5, 0, 2, 1, 4, 6, 3)).reshape(
        lay.groups, lay.own, 2 * LANES
    )


def mix_kernel(modes_ref, weight_ref, *refs):
    out_ref = refs[-1]
    pair, count, channels, wide = weight_ref.shape[1:]
    per = wide // channels
    spread = []
    for a in range(pair):
        modes = jnp.concatenate([modes_ref[0, a]] * per, axis=1)
        row = lax.broadcasted_iota(jnp.int32, modes.shape, 0) % count
        owner = lax.broadcasted_iota(jnp.int32, modes.shape, 1) // channels
        zero = jnp.zeros_like(modes)
        parts = [jnp.where(row == owner + n * per, modes, zero) for n in range(count // per)]
        spread.append(jnp.concatenate(parts, axis=1))
    weights = [weight_ref[0, a].reshape(count * channels, wide) for a in range(pair)]
    mixed = dot(jnp.concatenate(spread, axis=0), jnp.concatenate(weights, axis=1))
    for a in range(pair):
        own = mixed[2 * count * a : 2 * count * (a + 1), wide * a : wide * (a + 1)]
        real, imag = own[:count], own[count:]
        turned = jnp.concatenate([-imag[:, channels:], imag[:, :channels]], axis=1)
        out_ref[0, a] = (real + turned).astype(BF16)


def mode_spec(lay, shape):
    per = lay.ky // 2
    return pl.BlockSpec((1, 2) + shape, lambda i: (i // per, i % per) + (0,) * len(shape))


def mix_modes(lay, modes_in, spectral_weight, after=()):
    shape = (lay.mx, 2 * lay.channels)
    return pl.pallas_call(
        mix_kernel,
        grid=(lay.own // 2,),
        in_specs=[mode_spec(lay, modes_in.shape[2:]), mode_spec(lay, spectral_weight.shape[2:])]
        + [ANY] * len(after),
        out_specs=mode_spec(lay, shape),
        out_shape=jax.ShapeDtypeStruct((lay.kz, lay.ky) + shape, BF16),
        compiler_params=params(),
        cost_estimate=cost(spectral_weight.size * 8, spectral_weight.size * 2),
        name="mix_modes",
    )(modes_in, spectral_weight, *after)


def pointwise_kernel(tile, field_ref, weight_ref, bias_ref, *refs):
    out_ref, blocks_ref, shift_ref = refs[-3:]
    channels, rows, depth, width = field_ref.shape

    @pl.when(pl.program_id(0) == 0)
    def _():
        shape = (tile * channels, channels)
        split = lax.broadcasted_iota(jnp.int32, shape, 0) // tile
        split = split == lax.broadcasted_iota(jnp.int32, shape, 1)
        shift = jnp.sum(jnp.where(split, bias_ref[...], 0.0), axis=1, keepdims=True)
        shift_ref[...] = jnp.broadcast_to(shift, shift_ref.shape)
        split = split.astype(BF16)
        wide = dot(split, weight_ref[...]).astype(BF16)
        wide = lax.dot_general(
            wide, split, (((1,), (1,)), ((), ())), preferred_element_type=F32
        )
        row = lax.broadcasted_iota(jnp.int32, wide.shape, 0) % tile
        column = lax.broadcasted_iota(jnp.int32, wide.shape, 1) % tile
        blocks_ref[...] = jnp.where(row == column, wide, 0.0).astype(BF16)

    for y in range(rows):
        for z in range(0, depth, tile):
            cells = field_ref[:, y, z : z + tile, :].reshape(channels * tile, width)
            mixed = (dot(blocks_ref[...], cells) + shift_ref[...]).astype(BF16)
            out_ref[:, y, z : z + tile, :] = mixed.reshape(channels, tile, width)


def pointwise(lay, field_in, weight, bias, first, count, done=None, after=()):
    span = 2
    size = lay.channels * lay.tile
    given = [] if done is None else [done]
    block = pl.BlockSpec(
        (lay.channels, span, lay.depth, lay.width), lambda i: (0, first // span + i, 0, 0)
    )
    return pl.pallas_call(
        functools.partial(pointwise_kernel, lay.tile),
        grid=(count // span,),
        in_specs=[block, whole(weight.shape), whole(bias.shape)]
        + [ANY] * (len(given) + len(after)),
        out_specs=block,
        out_shape=jax.ShapeDtypeStruct(field_in.shape, BF16),
        scratch_shapes=[pltpu.VMEM((size, size), BF16), pltpu.VMEM((size, lay.width), F32)],
        input_output_aliases={3: 0} if given else {},
        compiler_params=params(),
        cost_estimate=cost(
            2 * size * lay.channels * count * lay.depth * lay.width,
            4 * lay.channels * count * lay.depth * lay.width,
        ),
        name="pointwise",
    )(field_in, weight, bias, *given, *after)


def gelu_and_slope(v):
    bell = jnp.exp2(v * v * (-0.5 * math.log2(math.e)))
    base = 1.0 + jnp.abs(v) * (0.3275911 / math.sqrt(2.0))
    t = pl.reciprocal(base, approx=True)
    poly = 0.5 * 1.061405429
    for coefficient in (-1.453152027, 1.421413741, -0.284496736, 0.254829592):
        poly = poly * t + 0.5 * coefficient
    tail = poly * t * bell
    cdf = jnp.where(v >= 0.0, 1.0 - tail, tail)
    return v * cdf, cdf + v * (bell * (1.0 / math.sqrt(2.0 * math.pi)))


def dense_kernel(
    first, own_ref, other_ref, y_ref, z_ref, x_ref, point_ref, weight_ref, b_in_ref, *refs
):
    hidden_ref, slope_ref, b_ref, part_ref, even_ref, odd_ref = refs[-6:]
    pack, rows, depth, width = point_ref.shape
    blocks, _, steps, size, _ = part_ref.shape
    band = rows // blocks
    step = pl.program_id(0)

    @pl.when(step == 0)
    def _():
        b_ref[...] = b_in_ref[...]

    depths, chips = own_ref.shape[:2]
    per = steps // depths
    rows_here = own_ref.shape[3] // per
    for q in range(steps):
        here = pl.ds(q % per * rows_here, rows_here)
        chunks = [
            piece[q // per, :, 0, here].reshape(chips * rows_here, 2 * LANES)
            for piece in (own_ref, other_ref)
        ]
        modes = jnp.concatenate(chunks, axis=0)
        back = dot(y_ref[...], jnp.concatenate([modes, turn(modes, -1)], axis=0)).astype(BF16)
        part_ref[:, 0, q] = back.reshape(blocks, size, 2 * LANES)
        part_ref[:, 1, q] = turn(back, -1).reshape(blocks, size, 2 * LANES)
    channel = (first + step) * pack

    per = even_ref.shape[0] // (band * depth)
    span = per * band
    count = rows // span

    def spectral(out_ref, n):
        cells = [
            dot(z_ref[...], part_ref[n * per + m].reshape(2 * steps * size, 2 * LANES))
            for m in range(per)
        ]
        out_ref[...] = dot(jnp.concatenate(cells, axis=0).astype(BF16), x_ref[...])

    def activate(spectral_ref, n):
        for m in range(span):
            y = n * span + m
            parts = [b_ref[b, y] for b in range(3)]
            for c in range(pack):
                value = spectral_ref[m * depth : (m + 1) * depth, c * width : (c + 1) * width]
                value = value + point_ref[c, y].astype(F32)
                hidden, slope = gelu_and_slope(value)
                hidden = hidden.astype(BF16)
                hidden_ref[c, y] = hidden
                slope_ref[c, y] = slope.astype(BF16)
                hidden = hidden.astype(F32)
                parts = [parts[b] + hidden * weight_ref[channel + c, b] for b in range(3)]
            for b in range(3):
                b_ref[b, y] = parts[b]

    spectral(even_ref, 0)
    if count == 1:
        activate(even_ref, 0)
        return

    def body(m, carry):
        spectral(odd_ref, 2 * m + 1)
        activate(even_ref, 2 * m)
        spectral(even_ref, jnp.minimum(2 * m + 2, count - 1))
        activate(odd_ref, 2 * m + 1)
        return carry

    lax.fori_loop(0, count // 2, body, 0)


def dense(lay, own, other, tables, x_table, point, weights, b_in, first, count, kept=()):
    size = (lay.n_gz, lay.chips, 1, lay.own, 2 * LANES)
    modes = pl.BlockSpec(size, lambda i: (0, 0, i, 0, 0))
    block = (lay.pack, lay.rows, lay.depth, lay.width)
    part = pl.BlockSpec(block, lambda i: (first + i, 0, 0, 0))
    out = jax.ShapeDtypeStruct(point.shape, BF16)
    volume = lay.pack * lay.cells * lay.width
    steps = lay.mz // lay.step
    return pl.pallas_call(
        functools.partial(dense_kernel, first),
        grid=(count,),
        in_specs=[
            modes,
            modes,
            whole(tables[2].shape),
            whole(tables[3].shape),
            whole(x_table.shape),
            part,
            pl.BlockSpec(memory_space=pltpu.SMEM),
            whole(b_in.shape),
        ]
        + [ANY] * len(kept),
        out_specs=[part, part, whole(b_in.shape)],
        out_shape=[out, out, jax.ShapeDtypeStruct(b_in.shape, F32)],
        input_output_aliases={8 + n: n for n in range(len(kept))},
        scratch_shapes=[
            pltpu.VMEM((lay.blocks, 2, steps, lay.step * lay.band, 2 * LANES), BF16),
            pltpu.VMEM((CHUNK, lay.pack * lay.width), F32),
            pltpu.VMEM((CHUNK, lay.pack * lay.width), F32),
        ],
        compiler_params=params(),
        cost_estimate=cost(count * volume * 2 * 6 * LANES, count * volume * 24),
        name="dense",
    )(own, other, tables[2], tables[3], x_table, point, weights, b_in, *kept)


def stencil_kernel(total_y, total_z, origin_ref, field_ref, *refs):
    halos, (grad_ref, sums_ref, b_ref, gy_ref, rest_ref) = refs[:4], refs[4:]
    _, rows_wide, depth_wide, width = b_ref.shape
    rows, depth = grad_ref.shape[1:3]
    low_y, high_y = pl.ds(0, 2), pl.ds(rows + 2, 2)
    low_z, high_z = pl.ds(0, 2), pl.ds(depth + 2, 2)
    mid_y, mid_z = pl.ds(2, rows), pl.ds(2, depth)
    b_ref[:, :, depth + 4 :] = jnp.zeros_like(b_ref[:, :, depth + 4 :])
    b_ref[:, mid_y, mid_z] = field_ref[...]
    all_y = pl.ds(0, rows_wide)
    places = [(low_y, mid_z), (high_y, mid_z), (all_y, low_z), (all_y, high_z)]
    for ref, (y, z) in zip(halos, places):
        b_ref[:, y, z] = ref[...]
    shape = (depth_wide, width)
    lane = lax.broadcasted_iota(jnp.int32, shape, 1)
    z_cell = origin_ref[1] + lax.broadcasted_iota(jnp.int32, shape, 0) - 2
    z_inside = (z_cell >= 0) & (z_cell < total_z)
    z_own = lax.broadcasted_iota(jnp.int32, shape, 0)
    z_own = (z_own >= 2) & (z_own < depth + 2)
    scale = 1.0 / (total_y * total_z * width)

    def next_x(v):
        return jnp.where(lane == width - 1, 0.0, pltpu.roll(v, width - 1, 1))

    def last_x(v):
        return jnp.where(lane == 0, 0.0, pltpu.roll(v, 1, 1))

    def next_z(v):
        return pltpu.roll(v, depth_wide - 1, 0)

    def last_z(v):
        return pltpu.roll(v, 1, 0)

    def terms(n, loss):
        b = [b_ref[a, n + 1] for a in range(3)]
        dx = [(next_x(v) - last_x(v)) * 0.5 for v in b]
        dy = [(b_ref[a, n + 2] - b_ref[a, n]) * 0.5 for a in range(3)]
        dz = [(next_z(v) - last_z(v)) * 0.5 for v in b]
        jx = dy[2] - dz[1]
        jy = dz[0] - dx[2]
        jz = dx[1] - dy[0]
        fx = jy * b[2] - jz * b[1]
        fy = jz * b[0] - jx * b[2]
        fz = jx * b[1] - jy * b[0]
        q = dx[0] + dy[1] + dz[2]
        strength = b[0] * b[0] + b[1] * b[1] + b[2] * b[2] + 1.0
        inverse = 1.0 / strength
        ratio = (fx * fx + fy * fy + fz * fz) * inverse
        y_cell = origin_ref[0] + n - 1
        y_inside = (y_cell >= 0) & (y_cell < total_y)
        own = z_own & (n >= 1) & (n <= rows)
        loss = loss + jnp.where(own, ratio + q * q, 0.0)
        weight = jnp.where(z_inside & y_inside, 2.0 * scale, 0.0)
        inverse = inverse * weight
        pull = ratio * inverse
        fx, fy, fz = fx * inverse, fy * inverse, fz * inverse
        q = q * weight
        cx = b[1] * fz - b[2] * fy
        cy = b[2] * fx - b[0] * fz
        cz = b[0] * fy - b[1] * fx
        db = [
            fy * jz - fz * jy - pull * b[0],
            fz * jx - fx * jz - pull * b[1],
            fx * jy - fy * jx - pull * b[2],
        ]
        gx = [q, cz, -cy]
        gy = [-cz, q, cx]
        gz = [cy, -cx, q]
        for a in range(3):
            gy_ref[a, n] = gy[a]
            back = last_x(gx[a]) - next_x(gx[a]) + last_z(gz[a]) - next_z(gz[a])
            rest_ref[a, n] = db[a] + back * 0.5
        return loss

    loss = lax.fori_loop(0, rows + 2, terms, jnp.zeros(shape, F32))

    def combine(n, sums):
        done = []
        for a in range(3):
            grad = rest_ref[a, n + 1] + (gy_ref[a, n] - gy_ref[a, n + 2]) * 0.5
            grad = grad[2 : depth + 2]
            grad_ref[a, n] = grad
            done.append(sums[a] + grad)
        return tuple(done)

    sums = lax.fori_loop(0, rows, combine, (jnp.zeros((depth, width), F32),) * 3)
    sums_ref[...] = jnp.zeros_like(sums_ref)
    for a in range(3):
        sums_ref[a : a + 1, :] = jnp.sum(sums[a], axis=0, keepdims=True)
    sums_ref[3:4, :] = jnp.sum(loss, axis=0, keepdims=True)


def stencil(lay, b_field):
    halos = halo(b_field)
    origin = jnp.stack([lay.y0, lay.z0]).astype(jnp.int32)
    wide = (3, lay.rows + 2, lay.depth + 8, lay.width)
    return pl.pallas_call(
        functools.partial(stencil_kernel, lay.ny, lay.nz),
        in_specs=[
            pl.BlockSpec(memory_space=pltpu.SMEM),
        ]
        + [VMEM] * 5,
        out_specs=[pl.BlockSpec(memory_space=pltpu.VMEM)] * 2,
        out_shape=[
            jax.ShapeDtypeStruct(b_field.shape, F32),
            jax.ShapeDtypeStruct((8, lay.width), F32),
        ],
        scratch_shapes=[
            pltpu.VMEM((3, lay.rows + 4) + wide[2:], F32),
            pltpu.VMEM(wide, F32),
            pltpu.VMEM(wide, F32),
        ],
        compiler_params=pltpu.CompilerParams(vmem_limit_bytes=VMEM_LIMIT),
        name="stencil",
    )(origin, b_field, *halos)


def grad_kernel(first, n_after, weight_ref, hidden_ref, slope_ref, grad_ref, x_ref, z_ref, y_ref,
                *refs):
    pre_ref, own_ref, send_ref, sums_ref, part_ref = refs[n_after:]
    pack, rows, depth, width = hidden_ref.shape
    blocks = part_ref.shape[2]
    band = rows // blocks
    channel = (first + pl.program_id(0)) * pack

    def fold(v):
        return jnp.sum(v.reshape(-1, 8, width), axis=0)

    per = max(CHUNK // (band * depth), 1)
    span = per * band
    count = rows // span

    def slopes(n):
        sums = [0.0] * (3 * pack)
        for y in range(n * span, (n + 1) * span):
            grads = [grad_ref[b, y] for b in range(3)]
            for c in range(pack):
                w = [weight_ref[channel + c, b] for b in range(3)]
                mixed = grads[0] * w[0] + grads[1] * w[1] + grads[2] * w[2]
                pre_ref[c, y] = (mixed * slope_ref[c, y].astype(F32)).astype(BF16)
                hidden = hidden_ref[c, y].astype(F32)
                for b in range(3):
                    sums[3 * c + b] = sums[3 * c + b] + fold(hidden * grads[b])
        return sums

    def transform(n):
        total = x_transform(pre_ref.at[:, n * span : (n + 1) * span], x_ref)
        for m in range(per):
            here = total[m * band * depth : (m + 1) * band * depth]
            z_transform(here, z_ref, part_ref, n * per + m)
        return fold(total)

    parts = [slopes(0)]
    totals = []
    for n in range(1, count):
        parts.append(slopes(n))
        totals.append(transform(n - 1))
    totals.append(transform(count - 1))
    sums = [sum(column[1:], column[0]) for column in zip(*parts)]
    sums.append(sum(totals[1:], totals[0]))
    sums_ref[...] = jnp.zeros_like(sums_ref)
    for n, part in enumerate(sums):
        sums_ref[0, n : n + 1, :] = jnp.sum(part, axis=0, keepdims=True)
    y_transform(y_ref, part_ref, own_ref, send_ref)


def grad_modes(lay, hidden, slope, grad_b, x_table, tables, weights, first, count, after=()):
    out, spec = mode_blocks(lay, count)
    block = (lay.pack, lay.rows, lay.depth, lay.width)
    part = pl.BlockSpec(block, lambda i: (i, 0, 0, 0))
    given = pl.BlockSpec(block, lambda i: (first + i, 0, 0, 0))
    volume = lay.pack * lay.cells * lay.width
    lines = -(-(3 * lay.pack + 1) // 8) * 8
    return pl.pallas_call(
        functools.partial(grad_kernel, first, len(after)),
        grid=(count,),
        in_specs=[
            pl.BlockSpec(memory_space=pltpu.SMEM),
            given,
            given,
            whole(grad_b.shape),
            whole(x_table.shape),
            whole(tables[0].shape),
            whole(tables[1].shape),
        ]
        + [ANY] * len(after),
        out_specs=[
            part,
            spec,
            spec,
            pl.BlockSpec((1, lines, lay.width), lambda i: (i, 0, 0)),
        ],
        out_shape=[
            jax.ShapeDtypeStruct((count * lay.pack,) + block[1:], BF16),
            out,
            out,
            jax.ShapeDtypeStruct((count, lines, lay.width), F32),
        ],
        scratch_shapes=[part_scratch(lay)],
        compiler_params=params(),
        cost_estimate=cost(count * volume * 2 * 2 * LANES, count * volume * 10),
        name="grad_modes",
    )(weights, hidden, slope, grad_b, x_table, tables[0], tables[1], *after)


def point_kernel(tile, n_after, field_ref, grad_ref, *refs):
    out_ref, acc_ref = refs[n_after:]
    channels, rows, depth, width = field_ref.shape
    count = grad_ref.shape[0]
    step = pl.program_id(0)

    @pl.when(step == 0)
    def _():
        acc_ref[...] = jnp.zeros_like(acc_ref)

    left, right = [], []
    for y in range(rows):
        for z in range(0, depth, tile):
            left.append(field_ref[:, y, z : z + tile, :].reshape(channels * tile, width))
            right.append(grad_ref[:, y, z : z + tile, :].reshape(count * tile, width))
    acc_ref[...] += lax.dot_general(
        jnp.concatenate(left, axis=1),
        jnp.concatenate(right, axis=1),
        (((1,), (1,)), ((), ())),
        preferred_element_type=F32,
    )

    @pl.when(step == pl.num_programs(0) - 1)
    def _():
        def pick(n):
            owner = lax.broadcasted_iota(jnp.int32, (n, n * tile), 1) // tile
            return (owner == lax.broadcasted_iota(jnp.int32, (n, n * tile), 0)).astype(F32)

        row = lax.broadcasted_iota(jnp.int32, acc_ref.shape, 0)
        column = lax.broadcasted_iota(jnp.int32, acc_ref.shape, 1)
        kept = jnp.where(row % tile == column % tile, acc_ref[...], 0.0)
        half = jnp.dot(
            pick(channels), kept, precision=lax.Precision.HIGHEST, preferred_element_type=F32
        )
        out_ref[...] = lax.dot_general(
            half,
            pick(count),
            (((1,), (1,)), ((), ())),
            precision=lax.Precision.HIGHEST,
            preferred_element_type=F32,
        )


def point_grad(lay, field_in, grad_pre, first, rows, after=()):
    span = math.gcd(4, rows)

    def block(count):
        size = (count, span, lay.depth, lay.width)
        return pl.BlockSpec(size, lambda i: (0, first // span + i, 0, 0))

    count = grad_pre.shape[0]
    size = lay.channels * lay.tile
    return pl.pallas_call(
        functools.partial(point_kernel, lay.tile, len(after)),
        grid=(rows // span,),
        in_specs=[block(lay.channels), block(count)] + [ANY] * len(after),
        out_specs=pl.BlockSpec((lay.channels, count), lambda i: (0, 0)),
        out_shape=jax.ShapeDtypeStruct((lay.channels, count), F32),
        scratch_shapes=[pltpu.VMEM((size, count * lay.tile), F32)],
        compiler_params=params(),
        cost_estimate=cost(2 * size * count * lay.cells * lay.width, 3 * field_in.size),
        name="point_grad",
    )(field_in, grad_pre, *after)


def outer_kernel(modes_ref, grads_ref, *refs):
    out_ref = refs[-1]
    pair, count, channels, wide = out_ref.shape[1:]
    columns = jnp.concatenate([modes_ref[0, a] for a in range(pair)], axis=1)
    rows = []
    for a in range(pair):
        right = grads_ref[0, a]
        turned = jnp.concatenate([right[:, channels:], -right[:, :channels]], axis=1)
        right = jnp.concatenate([right, turned], axis=0)
        zero = jnp.zeros_like(right)
        rows.append(jnp.concatenate([right if n == a else zero for n in range(pair)], axis=1))
    rows = jnp.concatenate(rows, axis=0)
    owner = lax.broadcasted_iota(jnp.int32, columns.shape, 1) % count
    zero = jnp.zeros_like(columns)
    some = 8
    for k in range(0, count, some):
        left = [jnp.where(owner == k + n, columns, zero) for n in range(some)]
        out = dot(jnp.concatenate(left, axis=0), rows)
        for a in range(pair):
            here = out[:, wide * a : wide * (a + 1)]
            out_ref[0, a, k : k + some] = here.reshape(some, channels, wide)


def weight_grad(lay, columns, rows, half, done=(), after=()):
    tile = (lay.mx, lay.channels, 2 * lay.channels)
    shape = (lay.kz, lay.ky) + tile
    per = lay.ky // 2
    first = half * lay.kz // 2

    def spec(block):
        return pl.BlockSpec(
            (1, 2) + block, lambda i: (first + i // per, i % per) + (0,) * len(block)
        )

    return pl.pallas_call(
        outer_kernel,
        grid=(lay.own // 4,),
        in_specs=[spec(columns.shape[2:]), spec(rows.shape[2:])]
        + [ANY] * (len(done) + len(after)),
        out_specs=spec(tile),
        out_shape=jax.ShapeDtypeStruct(shape, F32),
        input_output_aliases={2: 0} if done else {},
        compiler_params=params(),
        cost_estimate=cost(math.prod(shape) * 2, math.prod(shape) * 2),
        name="weight_grad",
    )(columns, rows, *done, *after)


def on_device(field_in, spectral_weight, point_weight, point_bias, out_weight, out_bias):
    lay = Layout(field_in, spectral_weight)
    tables = lay.grid_tables()
    x_table, x_back = lay.x_tables()
    weights = out_weight.astype(F32)
    scale = math.sqrt(lay.mx * lay.my * lay.mz / (lay.width * lay.ny * lay.nz))
    cuts = [0, lay.rows // 4, lay.rows * 5 // 8, lay.rows]

    def point(n, done, after):
        bias = point_bias.reshape(1, lay.channels)
        first, count = cuts[n], cuts[n + 1] - cuts[n]
        return pointwise(lay, field_in, point_weight.T, bias, first, count, done, after)

    own, send = forward_modes(lay, field_in, x_table, tables, 0, lay.groups)
    points = [None]

    def point_part(n, after):
        points.append(point(n, points[-1], after))
        return points[-1]

    modes = sum_all(lay, own, send, scale, point_part)
    done = points[-1]
    modes_in = by_mode(lay, jnp.concatenate(modes))
    mixed = mix_modes(lay, modes_in, spectral_weight, after=[done])
    mine = by_group(lay, mixed.reshape(lay.kz, lay.ky, lay.mx, 2, lay.groups, lay.pack))

    b_field = jnp.broadcast_to(
        out_bias[:, None, None, None], (3, lay.rows, lay.depth, lay.width)
    ).astype(F32)
    first = max(lay.groups * 5 // 16, 1)
    columns = [spread_chips(lay, mine[:first]), spread_chips(lay, mine[first:])]
    own = spread_depth(lay, columns[0], columns[1:])
    *kept, b_field = dense(
        lay, own, exchange(own, "gy", 1), tables, x_back, done, weights, b_field, 0, first
    )
    own = spread_depth(lay, columns[1], [b_field])
    hidden, slope, b_field = dense(
        lay, own, exchange(own, "gy", 1), tables, x_back, done, weights, b_field,
        first, lay.groups - first, kept,
    )

    grad_b, edge = stencil(lay, b_field)

    pre, own, send, sums = grad_modes(
        lay, hidden, slope, grad_b, x_table, tables, weights, 0, lay.groups
    )
    point_parts = []

    def grad_part(n, after):
        count = cuts[n + 1] - cuts[n]
        point_parts.append(point_grad(lay, field_in, pre, cuts[n], count, after))
        return point_parts[-1]

    grads = sum_all(lay, own, send, 1.0, grad_part)
    outs = jnp.sum(sums[:, : 3 * lay.pack], axis=-1).reshape(3 * lay.channels)
    bias = sums[:, 3 * lay.pack, :LANES].reshape(lay.groups, lay.pack, lay.mx)[..., 0]
    ends = jnp.sum(edge, axis=-1)
    square = lay.channels * lay.channels
    flat = jnp.concatenate(
        [
            sum_blocks(point_parts, False, 1.0, grads[-1:])[0].reshape(square),
            outs,
            bias.reshape(lay.channels),
            ends[:4],
        ]
    )
    flat = jnp.pad(flat, (0, -flat.shape[0] % 1024)).reshape(-1, LANES)
    rows = by_mode(lay, jnp.concatenate(grads))
    rows = jnp.concatenate([rows[:, :, : lay.mx], rows[:, :, lay.mx :]], axis=-1)
    columns = jnp.transpose(modes_in, (0, 1, 3, 2))

    def gathered(axis, steps, after):
        return sum_blocks([flat] + [exchange(flat, axis, d) for d in steps], False, 1.0, after)[0]

    flat = gathered("gz", range(1, lay.n_gz), [rows])
    grad_spectral = weight_grad(lay, columns, rows, 0, after=[flat])
    flat = gathered("gy", range(CORES, lay.n_gy, CORES), [grad_spectral])
    grad_spectral = weight_grad(lay, columns, rows, 1, [grad_spectral], [flat])
    flat = gathered("gy", [1], [grad_spectral]).reshape(-1)
    after = square + 3 * lay.channels
    ends = flat[after + lay.channels : after + lay.channels + 4]
    return (
        ends[3] / (lay.width * lay.ny * lay.nz),
        grad_spectral,
        flat[:square].reshape(lay.channels, lay.channels),
        flat[after : after + lay.channels],
        flat[square:after].reshape(lay.channels, 3),
        ends[:3],
    )


def solution(mesh):
    return jax.shard_map(
        on_device,
        mesh=mesh,
        in_specs=(P(None, "gy", "gz", None), P("gz", "gy", None, None, None), P(), P(), P(), P()),
        out_specs=(P(), P("gz", "gy", None, None, None), P(), P(), P(), P()),
        check_vma=False,
    )
```

```python
import functools
import math

import jax
import jax.numpy as jnp
from jax import lax
from jax.experimental import pallas as pl
from jax.experimental.pallas import tpu as pltpu
from jax.sharding import PartitionSpec as P

F32 = jnp.float32
BF16 = jnp.bfloat16
CORES = 2
LANES = 128
VMEM_LIMIT = 56 * 1024 * 1024
CHUNK = 256


def params():
    return pltpu.CompilerParams(
        vmem_limit_bytes=VMEM_LIMIT, dimension_semantics=("arbitrary",)
    )


def whole(shape):
    return pl.BlockSpec(shape, lambda i: (0,) * len(shape), pipeline_mode=pl.Buffered(1))


ANY = pl.BlockSpec(memory_space=pl.ANY)


def cost(flops, moved):
    return pl.CostEstimate(flops=flops, bytes_accessed=moved, transcendentals=0)


def dot(a, b):
    return jnp.dot(a, b, preferred_element_type=F32)


def frequencies(mode_index, mode_total):
    return jnp.where(mode_index < mode_total // 2, mode_index, mode_index - mode_total)


def twiddle(product, length):
    phases = (product % length).astype(F32) * (2.0 * math.pi / length)
    return jnp.cos(phases).astype(BF16).astype(F32), jnp.sin(phases).astype(BF16).astype(F32)


def halo(block):
    def moved(value, axis, step):
        count = lax.axis_size(axis)
        pairs = [(n, n + step) for n in range(count) if 0 <= n + step < count]
        return lax.ppermute(value, axis, pairs)

    low = moved(block[:, -2:], "gy", 1)
    high = moved(block[:, :2], "gy", -1)
    ends = [
        jnp.concatenate([part[:, :, cut] for part in (low, block, high)], axis=1)
        for cut in (slice(-2, None), slice(0, 2))
    ]
    return [low, high, moved(ends[0], "gz", 1), moved(ends[1], "gz", -1)]


class Layout:
    def __init__(self, field_in, spectral_weight):
        self.channels, self.rows, self.depth, self.width = field_in.shape
        self.kz, self.ky, self.mx = spectral_weight.shape[:3]
        self.n_gy, self.n_gz = lax.axis_size("gy"), lax.axis_size("gz")
        self.chips = self.n_gy // CORES
        self.ny, self.nz = self.rows * self.n_gy, self.depth * self.n_gz
        self.my, self.mz = self.ky * self.n_gy, self.kz * self.n_gz
        self.cells = self.rows * self.depth
        self.modes = self.my * self.mz
        self.pack = LANES // self.mx
        self.groups = self.channels // self.pack
        self.own = self.ky * self.kz
        self.band = min(LANES // self.depth, self.rows)
        self.blocks = self.rows // self.band
        self.step = min(LANES // self.rows, self.kz)
        self.tile = 8
        self.gy, self.gz = lax.axis_index("gy"), lax.axis_index("gz")
        self.y0 = self.gy * self.rows
        self.z0 = self.gz * self.depth

    def grid_table(self, mode, cell, first, length, same):
        real, imag = twiddle(mode * (first + cell[0]), length)
        return jnp.where(same, jnp.where(cell[1] == 0, real, imag), 0.0).astype(BF16)

    def grid_tables(self):
        core, chip = self.gy % CORES, self.gy // CORES

        def iotas(rows, columns):
            shape = (rows, columns)
            row = lax.broadcasted_iota(jnp.int32, shape, 0)
            return row, lax.broadcasted_iota(jnp.int32, shape, 1)

        def kz(n):
            return frequencies(((n // self.kz) ^ self.gz) * self.kz + n % self.kz, self.mz)

        def ky(n):
            h, f = n // (self.chips * self.ky), n // self.ky % self.chips
            return frequencies(((f ^ chip) * CORES + (h ^ core)) * self.ky + n % self.ky, self.my)

        band, step, depth = self.band, self.step, self.depth
        z_modes, y_modes = self.mz * band, self.my * step
        z_cells, y_cells = band * depth, self.blocks * step * band
        m, c = iotas(z_modes, 2 * z_cells)
        z_forward = self.grid_table(
            kz(m // band), (c % depth, c // z_cells), self.z0, self.nz,
            m % band == c // depth % band,
        )
        c, m = iotas(z_cells, 2 * z_modes)
        z_back = self.grid_table(
            kz(m % z_modes // band), (c % depth, m // z_modes), self.z0, self.nz,
            m % band == c // depth,
        )

        def row_of(c):
            return c // (step * band) % self.blocks * band + c % band

        m, c = iotas(y_modes, 2 * y_cells)
        y_forward = self.grid_table(
            ky(m // step), (row_of(c), c // y_cells), self.y0, self.ny,
            m % step == c // band % step,
        )
        c, m = iotas(y_cells, 2 * y_modes)
        y_back = self.grid_table(
            ky(m % y_modes // step), (row_of(c), m // y_modes), self.y0, self.ny,
            m % step == c // band % step,
        )
        return z_forward, y_forward, y_back, z_back

    def x_tables(self):
        shape = (self.width, 2 * LANES)
        x = lax.broadcasted_iota(jnp.int32, shape, 0)
        lane = lax.broadcasted_iota(jnp.int32, shape, 1)
        cos, sin = twiddle(x * frequencies(lane % self.mx, self.mx), self.width)
        table = jnp.where(lane < LANES, cos, -sin).astype(BF16)
        owner = lane % LANES // self.mx
        forward = [jnp.where(owner == c, table, 0) for c in range(self.pack)]
        lane, x = (lax.broadcasted_iota(jnp.int32, shape[::-1], d) for d in range(2))
        cos, sin = twiddle(x * frequencies(lane % self.mx, self.mx), self.width)
        table = jnp.where(lane < LANES, cos, -sin).astype(BF16)
        owner = lane % LANES // self.mx
        inverse = [jnp.where(owner == c, table, 0) for c in range(self.pack)]
        return jnp.concatenate(forward, axis=0), jnp.concatenate(inverse, axis=1)


def turn(values, sign):
    real, imag = values[:, :LANES], values[:, LANES:]
    return jnp.concatenate([imag, -real] if sign > 0 else [-imag, real], axis=1)


def z_transform(x_modes, table_ref, part_ref, n):
    x_modes = x_modes.astype(BF16)
    rhs = jnp.concatenate([x_modes, turn(x_modes, 1)], axis=0)
    modes = dot(table_ref[...], rhs).astype(BF16)
    steps, _, _, size, _ = part_ref.shape
    part_ref[:, 0, n] = modes.reshape(steps, size, 2 * LANES)
    part_ref[:, 1, n] = turn(modes, 1).reshape(steps, size, 2 * LANES)


def y_transform(table_ref, part_ref, own_ref, send_ref):
    half = table_ref.shape[0] // 2
    steps, _, blocks, size, _ = part_ref.shape
    chips = own_ref.shape[1]
    rows = half // chips
    per = steps // own_ref.shape[0]
    for q in range(steps):
        modes = dot(table_ref[...], part_ref[q].reshape(2 * blocks * size, 2 * LANES))
        modes = modes.astype(BF16)
        here = pl.ds(q % per * rows, rows)
        own_ref[q // per, :, 0, here] = modes[:half].reshape(chips, rows, 2 * LANES)
        send_ref[q // per, :, 0, here] = modes[half:].reshape(chips, rows, 2 * LANES)


def x_transform(source_ref, x_ref):
    pack, rows, depth, width = source_ref.shape
    cells = [source_ref[c].reshape(rows * depth, width) for c in range(pack)]
    return dot(jnp.concatenate(cells, axis=1), x_ref[...])


def modes_kernel(n_after, field_ref, x_ref, z_ref, y_ref, *refs):
    own_ref, send_ref, part_ref = refs[n_after:]
    total = x_transform(field_ref, x_ref)
    blocks = part_ref.shape[2]
    size = total.shape[0] // blocks
    for n in range(blocks):
        z_transform(total[n * size : (n + 1) * size], z_ref, part_ref, n)
    y_transform(y_ref, part_ref, own_ref, send_ref)


def mode_blocks(lay, count):
    shape = (lay.n_gz, lay.chips, count, lay.own, 2 * LANES)
    spec = pl.BlockSpec((lay.n_gz, lay.chips, 1, lay.own, 2 * LANES), lambda i: (0, 0, i, 0, 0))
    return jax.ShapeDtypeStruct(shape, BF16), spec


def part_scratch(lay):
    size = lay.step * lay.band
    return pltpu.VMEM((lay.mz // lay.step, 2, lay.blocks, size, 2 * LANES), BF16)


def forward_modes(lay, field_in, x_table, tables, first, count, after=()):
    out, spec = mode_blocks(lay, count)
    block = (lay.pack, lay.rows, lay.depth, lay.width)
    volume = lay.pack * lay.cells * lay.width
    return pl.pallas_call(
        functools.partial(modes_kernel, len(after)),
        grid=(count,),
        in_specs=[
            pl.BlockSpec(block, lambda i: (first + i, 0, 0, 0)),
            whole(x_table.shape),
            whole(tables[0].shape),
            whole(tables[1].shape),
        ]
        + [ANY] * len(after),
        out_specs=[spec, spec],
        out_shape=[out, out],
        scratch_shapes=[part_scratch(lay)],
        compiler_params=params(),
        cost_estimate=cost(count * volume * 2 * 2 * LANES, count * volume * 3),
        name="forward_modes",
    )(field_in, x_table, tables[0], tables[1], *after)


def exchange(value, axis, distance):
    count = lax.axis_size(axis)
    return lax.ppermute(value, axis, [(i, i ^ distance) for i in range(count)])


def sum_kernel(n_in, n_out, factor, *refs):
    rows = refs[0].shape[1]
    chunk = math.gcd(rows, 256)

    def body(n, carry):
        here = pl.ds(pl.multiple_of(n * chunk, chunk), chunk)
        for m, out_ref in enumerate(refs[-n_out:]):
            total = refs[0][m, here].astype(F32)
            for ref in refs[1:n_in]:
                total = total + ref[m, here].astype(F32)
            out_ref[here] = (total * factor).astype(out_ref.dtype)
        return carry

    lax.fori_loop(0, rows // chunk, body, 0)


VMEM = pl.BlockSpec(memory_space=pltpu.VMEM)


def sum_blocks(values, split, factor=1.0, after=(), weight=2):
    shape = values[0].shape
    n_out = shape[0] if split else 1
    rows = math.prod(shape[:-1]) // n_out
    values = [value.reshape(n_out, rows, shape[-1]) for value in values]
    outs = pl.pallas_call(
        functools.partial(sum_kernel, len(values), n_out, factor),
        in_specs=[VMEM] * len(values) + [ANY] * len(after),
        out_specs=[VMEM] * n_out,
        out_shape=[jax.ShapeDtypeStruct((rows, shape[-1]), values[0].dtype)] * n_out,
        compiler_params=pltpu.CompilerParams(vmem_limit_bytes=VMEM_LIMIT),
        cost_estimate=cost(math.prod(shape) * len(values), math.prod(shape) * weight * len(values)),
        name="sum_blocks",
    )(*values, *after)
    return [out.reshape(shape[1:] if split else shape) for out in outs]


def core_kernel(own_ref, other_ref, *refs):
    count = own_ref.shape[0]
    half = refs[0].shape[1]
    for n in range(count):
        total = (own_ref[n, 0].astype(F32) + other_ref[n, 0].astype(F32)).astype(BF16)
        refs[n][0] = total[:half]
        refs[count + n][0] = total[half:]


def from_cores(lay, own, other):
    tail = (lay.own, 2 * LANES)
    half = lay.groups // 2
    given = pl.BlockSpec((lay.n_gz, 1, lay.groups) + tail, lambda i: (0, i, 0, 0, 0))
    outs = pl.pallas_call(
        core_kernel,
        grid=(lay.chips,),
        in_specs=[given, given],
        out_specs=[pl.BlockSpec((1, half) + tail, lambda i: (i, 0, 0, 0))] * (2 * lay.n_gz),
        out_shape=[jax.ShapeDtypeStruct((lay.chips, half) + tail, BF16)] * (2 * lay.n_gz),
        compiler_params=params(),
        cost_estimate=cost(own.size, own.size * 6),
        name="core_sums",
    )(own, other)
    return list(outs[: lay.n_gz]), list(outs[lay.n_gz :])


def sum_all(lay, own, send, factor, work):
    early, late = from_cores(lay, own, exchange(send, "gy", 1))
    done = work(0, early[:1])
    early = sum_blocks(to_depth(early), True, after=[done])
    done = work(1, early[:1])
    first = from_chips(early, factor, [done])
    late = sum_blocks(to_depth(late), True, after=[first])
    return [first, from_chips(late, factor)]


def to_depth(blocks):
    return blocks[:1] + [exchange(block, "gz", d) for d, block in enumerate(blocks) if d]


def from_chips(blocks, factor, after=()):
    got = [exchange(block, "gy", d * CORES) for d, block in enumerate(blocks) if d]
    return sum_blocks(blocks[:1] + got, False, factor, after)[0]


def stack_kernel(n_in, *refs):
    rows = refs[0].shape[0]
    chunk = math.gcd(rows, 256)

    def body(n, carry):
        here = pl.ds(pl.multiple_of(n * chunk, chunk), chunk)
        for m in range(n_in):
            refs[-1][m, here] = refs[m][here]
        return carry

    lax.fori_loop(0, rows // chunk, body, 0)


def stack_blocks(values, after=()):
    shape = values[0].shape
    flat = [value.reshape(-1, shape[-1]) for value in values]
    out = (len(values),) + flat[0].shape
    stacked = pl.pallas_call(
        functools.partial(stack_kernel, len(values)),
        in_specs=[VMEM] * len(values) + [ANY] * len(after),
        out_specs=VMEM,
        out_shape=jax.ShapeDtypeStruct(out, values[0].dtype),
        compiler_params=pltpu.CompilerParams(vmem_limit_bytes=VMEM_LIMIT),
        cost_estimate=cost(math.prod(out), 4 * math.prod(out)),
        name="stack_blocks",
    )(*flat, *after)
    return stacked.reshape((len(values),) + shape)


def spread_chips(lay, mine):
    return stack_blocks([mine] + [exchange(mine, "gy", d * CORES) for d in range(1, lay.chips)])


def spread_depth(lay, column, after=()):
    pieces = [column] + [exchange(column, "gz", d) for d in range(1, lay.n_gz)]
    return stack_blocks(pieces, after)


def by_mode(lay, modes):
    count = modes.shape[0]
    split = modes.reshape(
        count, lay.kz // lay.step, lay.ky, lay.step, 2, lay.pack, lay.mx
    )
    return jnp.transpose(split, (1, 3, 2, 4, 6, 0, 5)).reshape(
        lay.kz, lay.ky, 2 * lay.mx, count * lay.pack
    )


def by_group(lay, modes):
    split = modes.reshape(
        lay.kz // lay.step, lay.step, lay.ky, lay.mx, 2, lay.groups, lay.pack
    )
    return jnp.transpose(split, (5, 0, 2, 1, 4, 6, 3)).reshape(
        lay.groups, lay.own, 2 * LANES
    )


def mix_kernel(modes_ref, weight_ref, *refs):
    out_ref = refs[-1]
    pair, count, channels, wide = weight_ref.shape[1:]
    per = wide // channels
    spread = []
    for a in range(pair):
        modes = jnp.concatenate([modes_ref[0, a]] * per, axis=1)
        row = lax.broadcasted_iota(jnp.int32, modes.shape, 0) % count
        owner = lax.broadcasted_iota(jnp.int32, modes.shape, 1) // channels
        zero = jnp.zeros_like(modes)
        parts = [jnp.where(row == owner + n * per, modes, zero) for n in range(count // per)]
        spread.append(jnp.concatenate(parts, axis=1))
    weights = [weight_ref[0, a].reshape(count * channels, wide) for a in range(pair)]
    mixed = dot(jnp.concatenate(spread, axis=0), jnp.concatenate(weights, axis=1))
    for a in range(pair):
        own = mixed[2 * count * a : 2 * count * (a + 1), wide * a : wide * (a + 1)]
        real, imag = own[:count], own[count:]
        turned = jnp.concatenate([-imag[:, channels:], imag[:, :channels]], axis=1)
        out_ref[0, a] = (real + turned).astype(BF16)


def mode_spec(lay, shape):
    per = lay.ky // 2
    return pl.BlockSpec((1, 2) + shape, lambda i: (i // per, i % per) + (0,) * len(shape))


def mix_modes(lay, modes_in, spectral_weight, after=()):
    shape = (lay.mx, 2 * lay.channels)
    return pl.pallas_call(
        mix_kernel,
        grid=(lay.own // 2,),
        in_specs=[mode_spec(lay, modes_in.shape[2:]), mode_spec(lay, spectral_weight.shape[2:])]
        + [ANY] * len(after),
        out_specs=mode_spec(lay, shape),
        out_shape=jax.ShapeDtypeStruct((lay.kz, lay.ky) + shape, BF16),
        compiler_params=params(),
        cost_estimate=cost(spectral_weight.size * 8, spectral_weight.size * 2),
        name="mix_modes",
    )(modes_in, spectral_weight, *after)


def pointwise_kernel(tile, field_ref, weight_ref, bias_ref, *refs):
    out_ref, blocks_ref, shift_ref = refs[-3:]
    channels, rows, depth, width = field_ref.shape

    @pl.when(pl.program_id(0) == 0)
    def _():
        shape = (tile * channels, channels)
        split = lax.broadcasted_iota(jnp.int32, shape, 0) // tile
        split = split == lax.broadcasted_iota(jnp.int32, shape, 1)
        shift = jnp.sum(jnp.where(split, bias_ref[...], 0.0), axis=1, keepdims=True)
        shift_ref[...] = jnp.broadcast_to(shift, shift_ref.shape)
        split = split.astype(BF16)
        wide = dot(split, weight_ref[...]).astype(BF16)
        wide = lax.dot_general(
            wide, split, (((1,), (1,)), ((), ())), preferred_element_type=F32
        )
        row = lax.broadcasted_iota(jnp.int32, wide.shape, 0) % tile
        column = lax.broadcasted_iota(jnp.int32, wide.shape, 1) % tile
        blocks_ref[...] = jnp.where(row == column, wide, 0.0).astype(BF16)

    for y in range(rows):
        for z in range(0, depth, tile):
            cells = field_ref[:, y, z : z + tile, :].reshape(channels * tile, width)
            mixed = (dot(blocks_ref[...], cells) + shift_ref[...]).astype(BF16)
            out_ref[:, y, z : z + tile, :] = mixed.reshape(channels, tile, width)


def pointwise(lay, field_in, weight, bias, first, count, done=None, after=()):
    span = 2
    size = lay.channels * lay.tile
    given = [] if done is None else [done]
    block = pl.BlockSpec(
        (lay.channels, span, lay.depth, lay.width), lambda i: (0, first // span + i, 0, 0)
    )
    return pl.pallas_call(
        functools.partial(pointwise_kernel, lay.tile),
        grid=(count // span,),
        in_specs=[block, whole(weight.shape), whole(bias.shape)]
        + [ANY] * (len(given) + len(after)),
        out_specs=block,
        out_shape=jax.ShapeDtypeStruct(field_in.shape, BF16),
        scratch_shapes=[pltpu.VMEM((size, size), BF16), pltpu.VMEM((size, lay.width), F32)],
        input_output_aliases={3: 0} if given else {},
        compiler_params=params(),
        cost_estimate=cost(
            2 * size * lay.channels * count * lay.depth * lay.width,
            4 * lay.channels * count * lay.depth * lay.width,
        ),
        name="pointwise",
    )(field_in, weight, bias, *given, *after)


def gelu_and_slope(v):
    bell = jnp.exp2(v * v * (-0.5 * math.log2(math.e)))
    base = 1.0 + jnp.abs(v) * (0.3275911 / math.sqrt(2.0))
    t = pl.reciprocal(base, approx=True)
    poly = 0.5 * 1.061405429
    for coefficient in (-1.453152027, 1.421413741, -0.284496736, 0.254829592):
        poly = poly * t + 0.5 * coefficient
    tail = poly * t * bell
    cdf = jnp.where(v >= 0.0, 1.0 - tail, tail)
    return v * cdf, cdf + v * (bell * (1.0 / math.sqrt(2.0 * math.pi)))


def dense_kernel(
    first, own_ref, other_ref, y_ref, z_ref, x_ref, point_ref, weight_ref, b_in_ref, *refs
):
    hidden_ref, slope_ref, b_ref, part_ref, even_ref, odd_ref = refs[-6:]
    pack, rows, depth, width = point_ref.shape
    blocks, _, steps, size, _ = part_ref.shape
    band = rows // blocks
    step = pl.program_id(0)

    @pl.when(step == 0)
    def _():
        b_ref[...] = b_in_ref[...]

    depths, chips = own_ref.shape[:2]
    per = steps // depths
    rows_here = own_ref.shape[3] // per
    for q in range(steps):
        here = pl.ds(q % per * rows_here, rows_here)
        chunks = [
            piece[q // per, :, 0, here].reshape(chips * rows_here, 2 * LANES)
            for piece in (own_ref, other_ref)
        ]
        modes = jnp.concatenate(chunks, axis=0)
        back = dot(y_ref[...], jnp.concatenate([modes, turn(modes, -1)], axis=0)).astype(BF16)
        part_ref[:, 0, q] = back.reshape(blocks, size, 2 * LANES)
        part_ref[:, 1, q] = turn(back, -1).reshape(blocks, size, 2 * LANES)
    channel = (first + step) * pack

    per = even_ref.shape[0] // (band * depth)
    span = per * band
    count = rows // span

    def spectral(out_ref, n):
        cells = [
            dot(z_ref[...], part_ref[n * per + m].reshape(2 * steps * size, 2 * LANES))
            for m in range(per)
        ]
        out_ref[...] = dot(jnp.concatenate(cells, axis=0).astype(BF16), x_ref[...])

    def activate(spectral_ref, n):
        for m in range(span):
            y = n * span + m
            parts = [b_ref[b, y] for b in range(3)]
            for c in range(pack):
                value = spectral_ref[m * depth : (m + 1) * depth, c * width : (c + 1) * width]
                value = value + point_ref[c, y].astype(F32)
                hidden, slope = gelu_and_slope(value)
                hidden = hidden.astype(BF16)
                hidden_ref[c, y] = hidden
                slope_ref[c, y] = slope.astype(BF16)
                hidden = hidden.astype(F32)
                parts = [parts[b] + hidden * weight_ref[channel + c, b] for b in range(3)]
            for b in range(3):
                b_ref[b, y] = parts[b]

    spectral(even_ref, 0)
    if count == 1:
        activate(even_ref, 0)
        return

    def body(m, carry):
        spectral(odd_ref, 2 * m + 1)
        activate(even_ref, 2 * m)
        spectral(even_ref, jnp.minimum(2 * m + 2, count - 1))
        activate(odd_ref, 2 * m + 1)
        return carry

    lax.fori_loop(0, count // 2, body, 0)


def dense(lay, own, other, tables, x_table, point, weights, b_in, first, count, kept=()):
    size = (lay.n_gz, lay.chips, 1, lay.own, 2 * LANES)
    modes = pl.BlockSpec(size, lambda i: (0, 0, i, 0, 0))
    block = (lay.pack, lay.rows, lay.depth, lay.width)
    part = pl.BlockSpec(block, lambda i: (first + i, 0, 0, 0))
    out = jax.ShapeDtypeStruct(point.shape, BF16)
    volume = lay.pack * lay.cells * lay.width
    steps = lay.mz // lay.step
    return pl.pallas_call(
        functools.partial(dense_kernel, first),
        grid=(count,),
        in_specs=[
            modes,
            modes,
            whole(tables[2].shape),
            whole(tables[3].shape),
            whole(x_table.shape),
            part,
            pl.BlockSpec(memory_space=pltpu.SMEM),
            whole(b_in.shape),
        ]
        + [ANY] * len(kept),
        out_specs=[part, part, whole(b_in.shape)],
        out_shape=[out, out, jax.ShapeDtypeStruct(b_in.shape, F32)],
        input_output_aliases={8 + n: n for n in range(len(kept))},
        scratch_shapes=[
            pltpu.VMEM((lay.blocks, 2, steps, lay.step * lay.band, 2 * LANES), BF16),
            pltpu.VMEM((CHUNK, lay.pack * lay.width), F32),
            pltpu.VMEM((CHUNK, lay.pack * lay.width), F32),
        ],
        compiler_params=params(),
        cost_estimate=cost(count * volume * 2 * 6 * LANES, count * volume * 24),
        name="dense",
    )(own, other, tables[2], tables[3], x_table, point, weights, b_in, *kept)


def stencil_kernel(total_y, total_z, origin_ref, field_ref, *refs):
    halos, (grad_ref, sums_ref, b_ref, gy_ref, rest_ref) = refs[:4], refs[4:]
    _, rows_wide, depth_wide, width = b_ref.shape
    rows, depth = grad_ref.shape[1:3]
    low_y, high_y = pl.ds(0, 2), pl.ds(rows + 2, 2)
    low_z, high_z = pl.ds(0, 2), pl.ds(depth + 2, 2)
    mid_y, mid_z = pl.ds(2, rows), pl.ds(2, depth)
    b_ref[:, :, depth + 4 :] = jnp.zeros_like(b_ref[:, :, depth + 4 :])
    b_ref[:, mid_y, mid_z] = field_ref[...]
    all_y = pl.ds(0, rows_wide)
    places = [(low_y, mid_z), (high_y, mid_z), (all_y, low_z), (all_y, high_z)]
    for ref, (y, z) in zip(halos, places):
        b_ref[:, y, z] = ref[...]
    shape = (depth_wide, width)
    lane = lax.broadcasted_iota(jnp.int32, shape, 1)
    z_cell = origin_ref[1] + lax.broadcasted_iota(jnp.int32, shape, 0) - 2
    z_inside = (z_cell >= 0) & (z_cell < total_z)
    z_own = lax.broadcasted_iota(jnp.int32, shape, 0)
    z_own = (z_own >= 2) & (z_own < depth + 2)
    scale = 1.0 / (total_y * total_z * width)

    def next_x(v):
        return jnp.where(lane == width - 1, 0.0, pltpu.roll(v, width - 1, 1))

    def last_x(v):
        return jnp.where(lane == 0, 0.0, pltpu.roll(v, 1, 1))

    def next_z(v):
        return pltpu.roll(v, depth_wide - 1, 0)

    def last_z(v):
        return pltpu.roll(v, 1, 0)

    def terms(n, loss):
        b = [b_ref[a, n + 1] for a in range(3)]
        dx = [(next_x(v) - last_x(v)) * 0.5 for v in b]
        dy = [(b_ref[a, n + 2] - b_ref[a, n]) * 0.5 for a in range(3)]
        dz = [(next_z(v) - last_z(v)) * 0.5 for v in b]
        jx = dy[2] - dz[1]
        jy = dz[0] - dx[2]
        jz = dx[1] - dy[0]
        fx = jy * b[2] - jz * b[1]
        fy = jz * b[0] - jx * b[2]
        fz = jx * b[1] - jy * b[0]
        q = dx[0] + dy[1] + dz[2]
        strength = b[0] * b[0] + b[1] * b[1] + b[2] * b[2] + 1.0
        inverse = 1.0 / strength
        ratio = (fx * fx + fy * fy + fz * fz) * inverse
        y_cell = origin_ref[0] + n - 1
        y_inside = (y_cell >= 0) & (y_cell < total_y)
        own = z_own & (n >= 1) & (n <= rows)
        loss = loss + jnp.where(own, ratio + q * q, 0.0)
        weight = jnp.where(z_inside & y_inside, 2.0 * scale, 0.0)
        inverse = inverse * weight
        pull = ratio * inverse
        fx, fy, fz = fx * inverse, fy * inverse, fz * inverse
        q = q * weight
        cx = b[1] * fz - b[2] * fy
        cy = b[2] * fx - b[0] * fz
        cz = b[0] * fy - b[1] * fx
        db = [
            fy * jz - fz * jy - pull * b[0],
            fz * jx - fx * jz - pull * b[1],
            fx * jy - fy * jx - pull * b[2],
        ]
        gx = [q, cz, -cy]
        gy = [-cz, q, cx]
        gz = [cy, -cx, q]
        for a in range(3):
            gy_ref[a, n] = gy[a]
            back = last_x(gx[a]) - next_x(gx[a]) + last_z(gz[a]) - next_z(gz[a])
            rest_ref[a, n] = db[a] + back * 0.5
        return loss

    loss = lax.fori_loop(0, rows + 2, terms, jnp.zeros(shape, F32))

    def combine(n, sums):
        done = []
        for a in range(3):
            grad = rest_ref[a, n + 1] + (gy_ref[a, n] - gy_ref[a, n + 2]) * 0.5
            grad = grad[2 : depth + 2]
            grad_ref[a, n] = grad
            done.append(sums[a] + grad)
        return tuple(done)

    sums = lax.fori_loop(0, rows, combine, (jnp.zeros((depth, width), F32),) * 3)
    sums_ref[...] = jnp.zeros_like(sums_ref)
    for a in range(3):
        sums_ref[a : a + 1, :] = jnp.sum(sums[a], axis=0, keepdims=True)
    sums_ref[3:4, :] = jnp.sum(loss, axis=0, keepdims=True)


def stencil(lay, b_field):
    halos = halo(b_field)
    origin = jnp.stack([lay.y0, lay.z0]).astype(jnp.int32)
    wide = (3, lay.rows + 2, lay.depth + 8, lay.width)
    return pl.pallas_call(
        functools.partial(stencil_kernel, lay.ny, lay.nz),
        in_specs=[
            pl.BlockSpec(memory_space=pltpu.SMEM),
        ]
        + [VMEM] * 5,
        out_specs=[pl.BlockSpec(memory_space=pltpu.VMEM)] * 2,
        out_shape=[
            jax.ShapeDtypeStruct(b_field.shape, F32),
            jax.ShapeDtypeStruct((8, lay.width), F32),
        ],
        scratch_shapes=[
            pltpu.VMEM((3, lay.rows + 4) + wide[2:], F32),
            pltpu.VMEM(wide, F32),
            pltpu.VMEM(wide, F32),
        ],
        compiler_params=pltpu.CompilerParams(vmem_limit_bytes=VMEM_LIMIT),
        name="stencil",
    )(origin, b_field, *halos)


def grad_kernel(first, n_after, weight_ref, hidden_ref, slope_ref, grad_ref, x_ref, z_ref, y_ref,
                *refs):
    pre_ref, own_ref, send_ref, sums_ref, part_ref = refs[n_after:]
    pack, rows, depth, width = hidden_ref.shape
    blocks = part_ref.shape[2]
    band = rows // blocks
    channel = (first + pl.program_id(0)) * pack

    def fold(v):
        return jnp.sum(v.reshape(-1, 8, width), axis=0)

    per = max(CHUNK // (band * depth), 1)
    span = per * band
    count = rows // span

    def slopes(n):
        sums = [0.0] * (3 * pack)
        for y in range(n * span, (n + 1) * span):
            grads = [grad_ref[b, y] for b in range(3)]
            for c in range(pack):
                w = [weight_ref[channel + c, b] for b in range(3)]
                mixed = grads[0] * w[0] + grads[1] * w[1] + grads[2] * w[2]
                pre_ref[c, y] = (mixed * slope_ref[c, y].astype(F32)).astype(BF16)
                hidden = hidden_ref[c, y].astype(F32)
                for b in range(3):
                    sums[3 * c + b] = sums[3 * c + b] + fold(hidden * grads[b])
        return sums

    def transform(n):
        total = x_transform(pre_ref.at[:, n * span : (n + 1) * span], x_ref)
        for m in range(per):
            here = total[m * band * depth : (m + 1) * band * depth]
            z_transform(here, z_ref, part_ref, n * per + m)
        return fold(total)

    parts = [slopes(0)]
    totals = []
    for n in range(1, count):
        parts.append(slopes(n))
        totals.append(transform(n - 1))
    totals.append(transform(count - 1))
    sums = [sum(column[1:], column[0]) for column in zip(*parts)]
    sums.append(sum(totals[1:], totals[0]))
    sums_ref[...] = jnp.zeros_like(sums_ref)
    for n, part in enumerate(sums):
        sums_ref[0, n : n + 1, :] = jnp.sum(part, axis=0, keepdims=True)
    y_transform(y_ref, part_ref, own_ref, send_ref)


def grad_modes(lay, hidden, slope, grad_b, x_table, tables, weights, first, count, after=()):
    out, spec = mode_blocks(lay, count)
    block = (lay.pack, lay.rows, lay.depth, lay.width)
    part = pl.BlockSpec(block, lambda i: (i, 0, 0, 0))
    given = pl.BlockSpec(block, lambda i: (first + i, 0, 0, 0))
    volume = lay.pack * lay.cells * lay.width
    lines = -(-(3 * lay.pack + 1) // 8) * 8
    return pl.pallas_call(
        functools.partial(grad_kernel, first, len(after)),
        grid=(count,),
        in_specs=[
            pl.BlockSpec(memory_space=pltpu.SMEM),
            given,
            given,
            whole(grad_b.shape),
            whole(x_table.shape),
            whole(tables[0].shape),
            whole(tables[1].shape),
        ]
        + [ANY] * len(after),
        out_specs=[
            part,
            spec,
            spec,
            pl.BlockSpec((1, lines, lay.width), lambda i: (i, 0, 0)),
        ],
        out_shape=[
            jax.ShapeDtypeStruct((count * lay.pack,) + block[1:], BF16),
            out,
            out,
            jax.ShapeDtypeStruct((count, lines, lay.width), F32),
        ],
        scratch_shapes=[part_scratch(lay)],
        compiler_params=params(),
        cost_estimate=cost(count * volume * 2 * 2 * LANES, count * volume * 10),
        name="grad_modes",
    )(weights, hidden, slope, grad_b, x_table, tables[0], tables[1], *after)


def point_kernel(tile, n_after, field_ref, grad_ref, *refs):
    out_ref, acc_ref = refs[n_after:]
    channels, rows, depth, width = field_ref.shape
    count = grad_ref.shape[0]
    step = pl.program_id(0)

    @pl.when(step == 0)
    def _():
        acc_ref[...] = jnp.zeros_like(acc_ref)

    left, right = [], []
    for y in range(rows):
        for z in range(0, depth, tile):
            left.append(field_ref[:, y, z : z + tile, :].reshape(channels * tile, width))
            right.append(grad_ref[:, y, z : z + tile, :].reshape(count * tile, width))
    acc_ref[...] += lax.dot_general(
        jnp.concatenate(left, axis=1),
        jnp.concatenate(right, axis=1),
        (((1,), (1,)), ((), ())),
        preferred_element_type=F32,
    )

    @pl.when(step == pl.num_programs(0) - 1)
    def _():
        def pick(n):
            owner = lax.broadcasted_iota(jnp.int32, (n, n * tile), 1) // tile
            return (owner == lax.broadcasted_iota(jnp.int32, (n, n * tile), 0)).astype(F32)

        row = lax.broadcasted_iota(jnp.int32, acc_ref.shape, 0)
        column = lax.broadcasted_iota(jnp.int32, acc_ref.shape, 1)
        kept = jnp.where(row % tile == column % tile, acc_ref[...], 0.0)
        half = jnp.dot(
            pick(channels), kept, precision=lax.Precision.HIGHEST, preferred_element_type=F32
        )
        out_ref[...] = lax.dot_general(
            half,
            pick(count),
            (((1,), (1,)), ((), ())),
            precision=lax.Precision.HIGHEST,
            preferred_element_type=F32,
        )


def point_grad(lay, field_in, grad_pre, first, rows, after=()):
    span = math.gcd(4, rows)

    def block(count):
        size = (count, span, lay.depth, lay.width)
        return pl.BlockSpec(size, lambda i: (0, first // span + i, 0, 0))

    count = grad_pre.shape[0]
    size = lay.channels * lay.tile
    return pl.pallas_call(
        functools.partial(point_kernel, lay.tile, len(after)),
        grid=(rows // span,),
        in_specs=[block(lay.channels), block(count)] + [ANY] * len(after),
        out_specs=pl.BlockSpec((lay.channels, count), lambda i: (0, 0)),
        out_shape=jax.ShapeDtypeStruct((lay.channels, count), F32),
        scratch_shapes=[pltpu.VMEM((size, count * lay.tile), F32)],
        compiler_params=params(),
        cost_estimate=cost(2 * size * count * lay.cells * lay.width, 3 * field_in.size),
        name="point_grad",
    )(field_in, grad_pre, *after)


def outer_kernel(modes_ref, grads_ref, *refs):
    out_ref = refs[-1]
    pair, count, channels, wide = out_ref.shape[1:]
    columns = jnp.concatenate([modes_ref[0, a] for a in range(pair)], axis=1)
    rows = []
    for a in range(pair):
        right = grads_ref[0, a]
        turned = jnp.concatenate([right[:, channels:], -right[:, :channels]], axis=1)
        right = jnp.concatenate([right, turned], axis=0)
        zero = jnp.zeros_like(right)
        rows.append(jnp.concatenate([right if n == a else zero for n in range(pair)], axis=1))
    rows = jnp.concatenate(rows, axis=0)
    owner = lax.broadcasted_iota(jnp.int32, columns.shape, 1) % count
    zero = jnp.zeros_like(columns)
    some = 8
    for k in range(0, count, some):
        left = [jnp.where(owner == k + n, columns, zero) for n in range(some)]
        out = dot(jnp.concatenate(left, axis=0), rows)
        for a in range(pair):
            here = out[:, wide * a : wide * (a + 1)]
            out_ref[0, a, k : k + some] = here.reshape(some, channels, wide)


def weight_grad(lay, columns, rows, half, done=(), after=()):
    tile = (lay.mx, lay.channels, 2 * lay.channels)
    shape = (lay.kz, lay.ky) + tile
    per = lay.ky // 2
    first = half * lay.kz // 2

    def spec(block):
        return pl.BlockSpec(
            (1, 2) + block, lambda i: (first + i // per, i % per) + (0,) * len(block)
        )

    return pl.pallas_call(
        outer_kernel,
        grid=(lay.own // 4,),
        in_specs=[spec(columns.shape[2:]), spec(rows.shape[2:])]
        + [ANY] * (len(done) + len(after)),
        out_specs=spec(tile),
        out_shape=jax.ShapeDtypeStruct(shape, F32),
        input_output_aliases={2: 0} if done else {},
        compiler_params=params(),
        cost_estimate=cost(math.prod(shape) * 2, math.prod(shape) * 2),
        name="weight_grad",
    )(columns, rows, *done, *after)


def pack_kernel(n_parts, *refs):
    small_ref, out_ref = refs[n_parts], refs[-1]
    count = refs[0].shape[0]
    total = refs[0][...]
    for ref in refs[1:n_parts]:
        total = total + ref[...]
    out_ref[...] = small_ref[...]
    out_ref[:count, :count] = total


def pack_sums(lay, parts, small, after):
    return pl.pallas_call(
        functools.partial(pack_kernel, len(parts)),
        in_specs=[VMEM] * (len(parts) + 1) + [ANY] * len(after),
        out_specs=VMEM,
        out_shape=jax.ShapeDtypeStruct(small.shape, F32),
        name="pack_sums",
    )(*parts, small, *after)


def unpack_kernel(left_ref, right_ref, *refs):
    ends_ref, point_ref, bias_ref, outs_ref = refs[-4:]
    count = point_ref.shape[0]
    total = left_ref[...] + right_ref[...]
    point_ref[...] = total[:count, :count]
    outs_ref[...] = total[:count, count : count + 3]
    bias_ref[...] = total[count : count + 1, :count]
    ends_ref[...] = total[count + 1 : count + 2, :4]


def unpack_sums(lay, left, right, after):
    shapes = [(1, 4), (lay.channels, lay.channels), (1, lay.channels), (lay.channels, 3)]
    return pl.pallas_call(
        unpack_kernel,
        in_specs=[VMEM] * 2 + [ANY] * len(after),
        out_specs=[VMEM] * 4,
        out_shape=[jax.ShapeDtypeStruct(shape, F32) for shape in shapes],
        name="unpack_sums",
    )(left, right, *after)


def on_device(field_in, spectral_weight, point_weight, point_bias, out_weight, out_bias):
    lay = Layout(field_in, spectral_weight)
    tables = lay.grid_tables()
    x_table, x_back = lay.x_tables()
    weights = out_weight.astype(F32)
    scale = math.sqrt(lay.mx * lay.my * lay.mz / (lay.width * lay.ny * lay.nz))
    cuts = [0, lay.rows * 5 // 8, lay.rows]

    def point(n, done, after):
        bias = point_bias.reshape(1, lay.channels)
        first, count = cuts[n], cuts[n + 1] - cuts[n]
        return pointwise(lay, field_in, point_weight.T, bias, first, count, done, after)

    own, send = forward_modes(lay, field_in, x_table, tables, 0, lay.groups)
    points = [None]

    def point_part(n, after):
        points.append(point(n, points[-1], after))
        return points[-1]

    modes = sum_all(lay, own, send, scale, point_part)
    done = points[-1]
    modes_in = by_mode(lay, jnp.concatenate(modes))
    mixed = mix_modes(lay, modes_in, spectral_weight, after=[done])
    mine = by_group(lay, mixed.reshape(lay.kz, lay.ky, lay.mx, 2, lay.groups, lay.pack))

    b_field = jnp.broadcast_to(
        out_bias[:, None, None, None], (3, lay.rows, lay.depth, lay.width)
    ).astype(F32)
    first = max(lay.groups * 5 // 16, 1)
    columns = [spread_chips(lay, mine[:first]), spread_chips(lay, mine[first:])]
    own = spread_depth(lay, columns[0], columns[1:])
    *kept, b_field = dense(
        lay, own, exchange(own, "gy", 1), tables, x_back, done, weights, b_field, 0, first
    )
    own = spread_depth(lay, columns[1], [b_field])
    hidden, slope, b_field = dense(
        lay, own, exchange(own, "gy", 1), tables, x_back, done, weights, b_field,
        first, lay.groups - first, kept,
    )

    grad_b, edge = stencil(lay, b_field)

    pre, own, send, sums = grad_modes(
        lay, hidden, slope, grad_b, x_table, tables, weights, 0, lay.groups
    )
    point_parts = []

    def grad_part(n, after):
        count = cuts[n + 1] - cuts[n]
        point_parts.append(point_grad(lay, field_in, pre, cuts[n], count, after))
        return point_parts[-1]

    grads = sum_all(lay, own, send, 1.0, grad_part)
    outs = jnp.sum(sums[:, : 3 * lay.pack], axis=-1).reshape(lay.channels, 3)
    bias = sums[:, 3 * lay.pack, :LANES].reshape(lay.groups, lay.pack, lay.mx)[..., 0]
    ends = jnp.sum(edge[:4], axis=-1)
    small = jnp.zeros((lay.channels + 8, LANES), F32)
    small = small.at[: lay.channels, lay.channels : lay.channels + 3].set(outs)
    small = small.at[lay.channels, : lay.channels].set(bias.reshape(lay.channels))
    small = small.at[lay.channels + 1, :4].set(ends)
    flat = pack_sums(lay, point_parts, small, grads[-1:])
    rows = by_mode(lay, jnp.concatenate(grads))
    rows = jnp.concatenate([rows[:, :, : lay.mx], rows[:, :, lay.mx :]], axis=-1)
    columns = jnp.transpose(modes_in, (0, 1, 3, 2))

    def gathered(axis, steps):
        return [flat] + [exchange(flat, axis, d) for d in steps]

    flat = sum_blocks(gathered("gz", range(1, lay.n_gz)), False, 1.0, [rows])[0]
    grad_spectral = weight_grad(lay, columns, rows, 0, after=[flat])
    flat = sum_blocks(gathered("gy", range(CORES, lay.n_gy, CORES)), False, 1.0, [grad_spectral])
    flat = flat[0]
    grad_spectral = weight_grad(lay, columns, rows, 1, [grad_spectral], [flat])
    ends, grad_point, bias, outs = unpack_sums(lay, *gathered("gy", [1]), [grad_spectral])
    return (
        ends[0, 3] / (lay.width * lay.ny * lay.nz),
        grad_spectral,
        grad_point,
        bias.reshape(lay.channels),
        outs,
        ends[0, :3],
    )


def solution(mesh):
    return jax.shard_map(
        on_device,
        mesh=mesh,
        in_specs=(P(None, "gy", "gz", None), P("gz", "gy", None, None, None), P(), P(), P(), P()),
        out_specs=(P(), P("gz", "gy", None, None, None), P(), P(), P(), P()),
        check_vma=False,
    )
```

```python
import functools
import math

import jax
import jax.numpy as jnp
from jax import lax
from jax.experimental import pallas as pl
from jax.experimental.pallas import tpu as pltpu
from jax.sharding import PartitionSpec as P

F32 = jnp.float32
BF16 = jnp.bfloat16
CORES = 2
LANES = 128
VMEM_LIMIT = 56 * 1024 * 1024
CHUNK = 256


def params():
    return pltpu.CompilerParams(
        vmem_limit_bytes=VMEM_LIMIT, dimension_semantics=("arbitrary",)
    )


def whole(shape):
    return pl.BlockSpec(shape, lambda i: (0,) * len(shape), pipeline_mode=pl.Buffered(1))


ANY = pl.BlockSpec(memory_space=pl.ANY)


def cost(flops, moved):
    return pl.CostEstimate(flops=flops, bytes_accessed=moved, transcendentals=0)


def dot(a, b):
    return jnp.dot(a, b, preferred_element_type=F32)


def frequencies(mode_index, mode_total):
    return jnp.where(mode_index < mode_total // 2, mode_index, mode_index - mode_total)


def twiddle(product, length):
    phases = (product % length).astype(F32) * (2.0 * math.pi / length)
    return jnp.cos(phases).astype(BF16).astype(F32), jnp.sin(phases).astype(BF16).astype(F32)


def halo(block):
    def moved(value, axis, step):
        count = lax.axis_size(axis)
        pairs = [(n, n + step) for n in range(count) if 0 <= n + step < count]
        return lax.ppermute(value, axis, pairs)

    low = moved(block[:, -2:], "gy", 1)
    high = moved(block[:, :2], "gy", -1)
    ends = [
        jnp.concatenate([part[:, :, cut] for part in (low, block, high)], axis=1)
        for cut in (slice(-2, None), slice(0, 2))
    ]
    return [low, high, moved(ends[0], "gz", 1), moved(ends[1], "gz", -1)]


class Layout:
    def __init__(self, field_in, spectral_weight):
        self.channels, self.rows, self.depth, self.width = field_in.shape
        self.kz, self.ky, self.mx = spectral_weight.shape[:3]
        self.n_gy, self.n_gz = lax.axis_size("gy"), lax.axis_size("gz")
        self.chips = self.n_gy // CORES
        self.ny, self.nz = self.rows * self.n_gy, self.depth * self.n_gz
        self.my, self.mz = self.ky * self.n_gy, self.kz * self.n_gz
        self.cells = self.rows * self.depth
        self.modes = self.my * self.mz
        self.pack = LANES // self.mx
        self.groups = self.channels // self.pack
        self.own = self.ky * self.kz
        self.band = min(LANES // self.depth, self.rows)
        self.blocks = self.rows // self.band
        self.step = min(LANES // self.rows, self.kz)
        self.tile = 8
        self.gy, self.gz = lax.axis_index("gy"), lax.axis_index("gz")
        self.y0 = self.gy * self.rows
        self.z0 = self.gz * self.depth

    def grid_table(self, mode, cell, first, length, same):
        real, imag = twiddle(mode * (first + cell[0]), length)
        return jnp.where(same, jnp.where(cell[1] == 0, real, imag), 0.0).astype(BF16)

    def grid_tables(self):
        core, chip = self.gy % CORES, self.gy // CORES

        def iotas(rows, columns):
            shape = (rows, columns)
            row = lax.broadcasted_iota(jnp.int32, shape, 0)
            return row, lax.broadcasted_iota(jnp.int32, shape, 1)

        def kz(n):
            return frequencies(((n // self.kz) ^ self.gz) * self.kz + n % self.kz, self.mz)

        def ky(n):
            h, f = n // (self.chips * self.ky), n // self.ky % self.chips
            return frequencies(((f ^ chip) * CORES + (h ^ core)) * self.ky + n % self.ky, self.my)

        band, step, depth = self.band, self.step, self.depth
        z_modes, y_modes = self.mz * band, self.my * step
        z_cells, y_cells = band * depth, self.blocks * step * band
        m, c = iotas(z_modes, 2 * z_cells)
        z_forward = self.grid_table(
            kz(m // band), (c % depth, c // z_cells), self.z0, self.nz,
            m % band == c // depth % band,
        )
        c, m = iotas(z_cells, 2 * z_modes)
        z_back = self.grid_table(
            kz(m % z_modes // band), (c % depth, m // z_modes), self.z0, self.nz,
            m % band == c // depth,
        )

        def row_of(c):
            return c // (step * band) % self.blocks * band + c % band

        m, c = iotas(y_modes, 2 * y_cells)
        y_forward = self.grid_table(
            ky(m // step), (row_of(c), c // y_cells), self.y0, self.ny,
            m % step == c // band % step,
        )
        c, m = iotas(y_cells, 2 * y_modes)
        y_back = self.grid_table(
            ky(m % y_modes // step), (row_of(c), m // y_modes), self.y0, self.ny,
            m % step == c // band % step,
        )
        return z_forward, y_forward, y_back, z_back

    def x_tables(self):
        shape = (self.width, 2 * LANES)
        x = lax.broadcasted_iota(jnp.int32, shape, 0)
        lane = lax.broadcasted_iota(jnp.int32, shape, 1)
        cos, sin = twiddle(x * frequencies(lane % self.mx, self.mx), self.width)
        table = jnp.where(lane < LANES, cos, -sin).astype(BF16)
        owner = lane % LANES // self.mx
        forward = [jnp.where(owner == c, table, 0) for c in range(self.pack)]
        lane, x = (lax.broadcasted_iota(jnp.int32, shape[::-1], d) for d in range(2))
        cos, sin = twiddle(x * frequencies(lane % self.mx, self.mx), self.width)
        table = jnp.where(lane < LANES, cos, -sin).astype(BF16)
        owner = lane % LANES // self.mx
        inverse = [jnp.where(owner == c, table, 0) for c in range(self.pack)]
        return jnp.concatenate(forward, axis=0), jnp.concatenate(inverse, axis=1)


def turn(values, sign):
    real, imag = values[:, :LANES], values[:, LANES:]
    return jnp.concatenate([imag, -real] if sign > 0 else [-imag, real], axis=1)


def z_transform(x_modes, table_ref, part_ref, n):
    x_modes = x_modes.astype(BF16)
    rhs = jnp.concatenate([x_modes, turn(x_modes, 1)], axis=0)
    modes = dot(table_ref[...], rhs).astype(BF16)
    steps, _, _, size, _ = part_ref.shape
    part_ref[:, 0, n] = modes.reshape(steps, size, 2 * LANES)
    part_ref[:, 1, n] = turn(modes, 1).reshape(steps, size, 2 * LANES)


def y_transform(table_ref, part_ref, own_ref, send_ref):
    half = table_ref.shape[0] // 2
    steps, _, blocks, size, _ = part_ref.shape
    chips = own_ref.shape[1]
    rows = half // chips
    per = steps // own_ref.shape[0]
    for q in range(steps):
        modes = dot(table_ref[...], part_ref[q].reshape(2 * blocks * size, 2 * LANES))
        modes = modes.astype(BF16)
        here = pl.ds(q % per * rows, rows)
        own_ref[q // per, :, 0, here] = modes[:half].reshape(chips, rows, 2 * LANES)
        send_ref[q // per, :, 0, here] = modes[half:].reshape(chips, rows, 2 * LANES)


def x_transform(source_ref, x_ref):
    pack, rows, depth, width = source_ref.shape
    cells = [source_ref[c].reshape(rows * depth, width) for c in range(pack)]
    return dot(jnp.concatenate(cells, axis=1), x_ref[...])


def modes_kernel(n_after, field_ref, x_ref, z_ref, y_ref, *refs):
    own_ref, send_ref, part_ref = refs[n_after:]
    total = x_transform(field_ref, x_ref)
    blocks = part_ref.shape[2]
    size = total.shape[0] // blocks
    for n in range(blocks):
        z_transform(total[n * size : (n + 1) * size], z_ref, part_ref, n)
    y_transform(y_ref, part_ref, own_ref, send_ref)


def mode_blocks(lay, count):
    shape = (lay.n_gz, lay.chips, count, lay.own, 2 * LANES)
    spec = pl.BlockSpec((lay.n_gz, lay.chips, 1, lay.own, 2 * LANES), lambda i: (0, 0, i, 0, 0))
    return jax.ShapeDtypeStruct(shape, BF16), spec


def part_scratch(lay):
    size = lay.step * lay.band
    return pltpu.VMEM((lay.mz // lay.step, 2, lay.blocks, size, 2 * LANES), BF16)


def forward_modes(lay, field_in, x_table, tables, first, count, after=()):
    out, spec = mode_blocks(lay, count)
    block = (lay.pack, lay.rows, lay.depth, lay.width)
    volume = lay.pack * lay.cells * lay.width
    return pl.pallas_call(
        functools.partial(modes_kernel, len(after)),
        grid=(count,),
        in_specs=[
            pl.BlockSpec(block, lambda i: (first + i, 0, 0, 0)),
            whole(x_table.shape),
            whole(tables[0].shape),
            whole(tables[1].shape),
        ]
        + [ANY] * len(after),
        out_specs=[spec, spec],
        out_shape=[out, out],
        scratch_shapes=[part_scratch(lay)],
        compiler_params=params(),
        cost_estimate=cost(count * volume * 2 * 2 * LANES, count * volume * 3),
        name="forward_modes",
    )(field_in, x_table, tables[0], tables[1], *after)


def exchange(value, axis, distance):
    count = lax.axis_size(axis)
    return lax.ppermute(value, axis, [(i, i ^ distance) for i in range(count)])


def sum_kernel(n_in, n_out, factor, *refs):
    rows = refs[0].shape[1]
    chunk = math.gcd(rows, 256)

    def body(n, carry):
        here = pl.ds(pl.multiple_of(n * chunk, chunk), chunk)
        for m, out_ref in enumerate(refs[-n_out:]):
            total = refs[0][m, here].astype(F32)
            for ref in refs[1:n_in]:
                total = total + ref[m, here].astype(F32)
            out_ref[here] = (total * factor).astype(out_ref.dtype)
        return carry

    lax.fori_loop(0, rows // chunk, body, 0)


VMEM = pl.BlockSpec(memory_space=pltpu.VMEM)


def sum_blocks(values, split, factor=1.0, after=(), weight=2):
    shape = values[0].shape
    n_out = shape[0] if split else 1
    rows = math.prod(shape[:-1]) // n_out
    values = [value.reshape(n_out, rows, shape[-1]) for value in values]
    outs = pl.pallas_call(
        functools.partial(sum_kernel, len(values), n_out, factor),
        in_specs=[VMEM] * len(values) + [ANY] * len(after),
        out_specs=[VMEM] * n_out,
        out_shape=[jax.ShapeDtypeStruct((rows, shape[-1]), values[0].dtype)] * n_out,
        compiler_params=pltpu.CompilerParams(vmem_limit_bytes=VMEM_LIMIT),
        cost_estimate=cost(math.prod(shape) * len(values), math.prod(shape) * weight * len(values)),
        name="sum_blocks",
    )(*values, *after)
    return [out.reshape(shape[1:] if split else shape) for out in outs]


def core_kernel(own_ref, other_ref, *refs):
    count = own_ref.shape[0]
    cut = refs[0].shape[1]
    for n in range(count):
        total = (own_ref[n, 0].astype(F32) + other_ref[n, 0].astype(F32)).astype(BF16)
        refs[n][0] = total[:cut]
        refs[count + n][0] = total[cut:]


def from_cores(lay, own, other):
    tail = (lay.own, 2 * LANES)
    cut = max(lay.groups * 5 // 8, 1)
    given = pl.BlockSpec((lay.n_gz, 1, lay.groups) + tail, lambda i: (0, i, 0, 0, 0))
    sizes = [cut] * lay.n_gz + [lay.groups - cut] * lay.n_gz
    outs = pl.pallas_call(
        core_kernel,
        grid=(lay.chips,),
        in_specs=[given, given],
        out_specs=[pl.BlockSpec((1, size) + tail, lambda i: (i, 0, 0, 0)) for size in sizes],
        out_shape=[jax.ShapeDtypeStruct((lay.chips, size) + tail, BF16) for size in sizes],
        compiler_params=params(),
        cost_estimate=cost(own.size, own.size * 6),
        name="core_sums",
    )(own, other)
    return list(outs[: lay.n_gz]), list(outs[lay.n_gz :])


def sum_all(lay, own, send, factor, work, last=()):
    early, late = from_cores(lay, own, exchange(send, "gy", 1))
    done = work(0, early[:1])
    early = sum_blocks(to_depth(early), True, after=[done])
    done = work(1, early[:1])
    first = from_chips(early, factor, [done])
    late = sum_blocks(to_depth(late), True, after=[first])
    return [first, from_chips(late, factor, last)]


def to_depth(blocks):
    return blocks[:1] + [exchange(block, "gz", d) for d, block in enumerate(blocks) if d]


def from_chips(blocks, factor, after=()):
    got = [exchange(block, "gy", d * CORES) for d, block in enumerate(blocks) if d]
    return sum_blocks(blocks[:1] + got, False, factor, after)[0]


def stack_kernel(n_in, *refs):
    rows = refs[0].shape[0]
    chunk = math.gcd(rows, 256)

    def body(n, carry):
        here = pl.ds(pl.multiple_of(n * chunk, chunk), chunk)
        for m in range(n_in):
            refs[-1][m, here] = refs[m][here]
        return carry

    lax.fori_loop(0, rows // chunk, body, 0)


def stack_blocks(values, after=()):
    shape = values[0].shape
    flat = [value.reshape(-1, shape[-1]) for value in values]
    out = (len(values),) + flat[0].shape
    stacked = pl.pallas_call(
        functools.partial(stack_kernel, len(values)),
        in_specs=[VMEM] * len(values) + [ANY] * len(after),
        out_specs=VMEM,
        out_shape=jax.ShapeDtypeStruct(out, values[0].dtype),
        compiler_params=pltpu.CompilerParams(vmem_limit_bytes=VMEM_LIMIT),
        cost_estimate=cost(math.prod(out), 4 * math.prod(out)),
        name="stack_blocks",
    )(*flat, *after)
    return stacked.reshape((len(values),) + shape)


def spread_chips(lay, mine):
    return stack_blocks([mine] + [exchange(mine, "gy", d * CORES) for d in range(1, lay.chips)])


def spread_depth(lay, column, after=()):
    pieces = [column] + [exchange(column, "gz", d) for d in range(1, lay.n_gz)]
    return stack_blocks(pieces, after)


def by_mode(lay, modes):
    count = modes.shape[0]
    split = modes.reshape(
        count, lay.kz // lay.step, lay.ky, lay.step, 2, lay.pack, lay.mx
    )
    return jnp.transpose(split, (1, 3, 2, 4, 6, 0, 5)).reshape(
        lay.kz, lay.ky, 2 * lay.mx, count * lay.pack
    )


def by_group(lay, modes):
    split = modes.reshape(
        lay.kz // lay.step, lay.step, lay.ky, lay.mx, 2, lay.groups, lay.pack
    )
    return jnp.transpose(split, (5, 0, 2, 1, 4, 6, 3)).reshape(
        lay.groups, lay.own, 2 * LANES
    )


def mix_kernel(modes_ref, weight_ref, *refs):
    out_ref = refs[-1]
    pair, count, channels, wide = weight_ref.shape[1:]
    per = wide // channels
    spread = []
    for a in range(pair):
        modes = jnp.concatenate([modes_ref[0, a]] * per, axis=1)
        row = lax.broadcasted_iota(jnp.int32, modes.shape, 0) % count
        owner = lax.broadcasted_iota(jnp.int32, modes.shape, 1) // channels
        zero = jnp.zeros_like(modes)
        parts = [jnp.where(row == owner + n * per, modes, zero) for n in range(count // per)]
        spread.append(jnp.concatenate(parts, axis=1))
    weights = [weight_ref[0, a].reshape(count * channels, wide) for a in range(pair)]
    mixed = dot(jnp.concatenate(spread, axis=0), jnp.concatenate(weights, axis=1))
    for a in range(pair):
        own = mixed[2 * count * a : 2 * count * (a + 1), wide * a : wide * (a + 1)]
        real, imag = own[:count], own[count:]
        turned = jnp.concatenate([-imag[:, channels:], imag[:, :channels]], axis=1)
        out_ref[0, a] = (real + turned).astype(BF16)


def mode_spec(lay, shape):
    per = lay.ky // 2
    return pl.BlockSpec((1, 2) + shape, lambda i: (i // per, i % per) + (0,) * len(shape))


def mix_modes(lay, modes_in, spectral_weight, after=()):
    shape = (lay.mx, 2 * lay.channels)
    return pl.pallas_call(
        mix_kernel,
        grid=(lay.own // 2,),
        in_specs=[mode_spec(lay, modes_in.shape[2:]), mode_spec(lay, spectral_weight.shape[2:])]
        + [ANY] * len(after),
        out_specs=mode_spec(lay, shape),
        out_shape=jax.ShapeDtypeStruct((lay.kz, lay.ky) + shape, BF16),
        compiler_params=params(),
        cost_estimate=cost(spectral_weight.size * 8, spectral_weight.size * 2),
        name="mix_modes",
    )(modes_in, spectral_weight, *after)


def pointwise_kernel(tile, field_ref, weight_ref, bias_ref, *refs):
    out_ref, blocks_ref, shift_ref = refs[-3:]
    channels, rows, depth, width = field_ref.shape

    @pl.when(pl.program_id(0) == 0)
    def _():
        shape = (tile * channels, channels)
        split = lax.broadcasted_iota(jnp.int32, shape, 0) // tile
        split = split == lax.broadcasted_iota(jnp.int32, shape, 1)
        shift = jnp.sum(jnp.where(split, bias_ref[...], 0.0), axis=1, keepdims=True)
        shift_ref[...] = jnp.broadcast_to(shift, shift_ref.shape)
        split = split.astype(BF16)
        wide = dot(split, weight_ref[...]).astype(BF16)
        wide = lax.dot_general(
            wide, split, (((1,), (1,)), ((), ())), preferred_element_type=F32
        )
        row = lax.broadcasted_iota(jnp.int32, wide.shape, 0) % tile
        column = lax.broadcasted_iota(jnp.int32, wide.shape, 1) % tile
        blocks_ref[...] = jnp.where(row == column, wide, 0.0).astype(BF16)

    for y in range(rows):
        for z in range(0, depth, tile):
            cells = field_ref[:, y, z : z + tile, :].reshape(channels * tile, width)
            mixed = (dot(blocks_ref[...], cells) + shift_ref[...]).astype(BF16)
            out_ref[:, y, z : z + tile, :] = mixed.reshape(channels, tile, width)


def pointwise(lay, field_in, weight, bias, first, count, done=None, after=()):
    span = 2
    size = lay.channels * lay.tile
    given = [] if done is None else [done]
    block = pl.BlockSpec(
        (lay.channels, span, lay.depth, lay.width), lambda i: (0, first // span + i, 0, 0)
    )
    return pl.pallas_call(
        functools.partial(pointwise_kernel, lay.tile),
        grid=(count // span,),
        in_specs=[block, whole(weight.shape), whole(bias.shape)]
        + [ANY] * (len(given) + len(after)),
        out_specs=block,
        out_shape=jax.ShapeDtypeStruct(field_in.shape, BF16),
        scratch_shapes=[pltpu.VMEM((size, size), BF16), pltpu.VMEM((size, lay.width), F32)],
        input_output_aliases={3: 0} if given else {},
        compiler_params=params(),
        cost_estimate=cost(
            2 * size * lay.channels * count * lay.depth * lay.width,
            4 * lay.channels * count * lay.depth * lay.width,
        ),
        name="pointwise",
    )(field_in, weight, bias, *given, *after)


def gelu_and_slope(v):
    bell = jnp.exp2(v * v * (-0.5 * math.log2(math.e)))
    base = 1.0 + jnp.abs(v) * (0.3275911 / math.sqrt(2.0))
    t = pl.reciprocal(base, approx=True)
    poly = 0.5 * 1.061405429
    for coefficient in (-1.453152027, 1.421413741, -0.284496736, 0.254829592):
        poly = poly * t + 0.5 * coefficient
    tail = poly * t * bell
    cdf = jnp.where(v >= 0.0, 1.0 - tail, tail)
    return v * cdf, cdf + v * (bell * (1.0 / math.sqrt(2.0 * math.pi)))


def dense_kernel(
    first, own_ref, other_ref, y_ref, z_ref, x_ref, point_ref, weight_ref, b_in_ref, *refs
):
    hidden_ref, slope_ref, b_ref, part_ref, even_ref, odd_ref = refs[-6:]
    pack, rows, depth, width = point_ref.shape
    blocks, _, steps, size, _ = part_ref.shape
    band = rows // blocks
    step = pl.program_id(0)

    @pl.when(step == 0)
    def _():
        b_ref[...] = b_in_ref[...]

    depths, chips = own_ref.shape[:2]
    per = steps // depths
    rows_here = own_ref.shape[3] // per
    for q in range(steps):
        here = pl.ds(q % per * rows_here, rows_here)
        chunks = [
            piece[q // per, :, 0, here].reshape(chips * rows_here, 2 * LANES)
            for piece in (own_ref, other_ref)
        ]
        modes = jnp.concatenate(chunks, axis=0)
        back = dot(y_ref[...], jnp.concatenate([modes, turn(modes, -1)], axis=0)).astype(BF16)
        part_ref[:, 0, q] = back.reshape(blocks, size, 2 * LANES)
        part_ref[:, 1, q] = turn(back, -1).reshape(blocks, size, 2 * LANES)
    channel = (first + step) * pack

    per = even_ref.shape[0] // (band * depth)
    span = per * band
    count = rows // span

    def spectral(out_ref, n):
        cells = [
            dot(z_ref[...], part_ref[n * per + m].reshape(2 * steps * size, 2 * LANES))
            for m in range(per)
        ]
        out_ref[...] = dot(jnp.concatenate(cells, axis=0).astype(BF16), x_ref[...])

    def activate(spectral_ref, n):
        for m in range(span):
            y = n * span + m
            parts = [b_ref[b, y] for b in range(3)]
            for c in range(pack):
                value = spectral_ref[m * depth : (m + 1) * depth, c * width : (c + 1) * width]
                value = value + point_ref[c, y].astype(F32)
                hidden, slope = gelu_and_slope(value)
                hidden = hidden.astype(BF16)
                hidden_ref[c, y] = hidden
                slope_ref[c, y] = slope.astype(BF16)
                hidden = hidden.astype(F32)
                parts = [parts[b] + hidden * weight_ref[channel + c, b] for b in range(3)]
            for b in range(3):
                b_ref[b, y] = parts[b]

    spectral(even_ref, 0)
    if count == 1:
        activate(even_ref, 0)
        return

    def body(m, carry):
        spectral(odd_ref, 2 * m + 1)
        activate(even_ref, 2 * m)
        spectral(even_ref, jnp.minimum(2 * m + 2, count - 1))
        activate(odd_ref, 2 * m + 1)
        return carry

    lax.fori_loop(0, count // 2, body, 0)


def dense(lay, own, other, tables, x_table, point, weights, b_in, first, count, kept=()):
    size = (lay.n_gz, lay.chips, 1, lay.own, 2 * LANES)
    modes = pl.BlockSpec(size, lambda i: (0, 0, i, 0, 0))
    block = (lay.pack, lay.rows, lay.depth, lay.width)
    part = pl.BlockSpec(block, lambda i: (first + i, 0, 0, 0))
    out = jax.ShapeDtypeStruct(point.shape, BF16)
    volume = lay.pack * lay.cells * lay.width
    steps = lay.mz // lay.step
    return pl.pallas_call(
        functools.partial(dense_kernel, first),
        grid=(count,),
        in_specs=[
            modes,
            modes,
            whole(tables[2].shape),
            whole(tables[3].shape),
            whole(x_table.shape),
            part,
            pl.BlockSpec(memory_space=pltpu.SMEM),
            whole(b_in.shape),
        ]
        + [ANY] * len(kept),
        out_specs=[part, part, whole(b_in.shape)],
        out_shape=[out, out, jax.ShapeDtypeStruct(b_in.shape, F32)],
        input_output_aliases={8 + n: n for n in range(len(kept))},
        scratch_shapes=[
            pltpu.VMEM((lay.blocks, 2, steps, lay.step * lay.band, 2 * LANES), BF16),
            pltpu.VMEM((CHUNK, lay.pack * lay.width), F32),
            pltpu.VMEM((CHUNK, lay.pack * lay.width), F32),
        ],
        compiler_params=params(),
        cost_estimate=cost(count * volume * 2 * 6 * LANES, count * volume * 24),
        name="dense",
    )(own, other, tables[2], tables[3], x_table, point, weights, b_in, *kept)


def stencil_kernel(total_y, total_z, origin_ref, field_ref, *refs):
    halos, (grad_ref, sums_ref, b_ref, gy_ref, rest_ref) = refs[:4], refs[4:]
    _, rows_wide, depth_wide, width = b_ref.shape
    rows, depth = grad_ref.shape[1:3]
    low_y, high_y = pl.ds(0, 2), pl.ds(rows + 2, 2)
    low_z, high_z = pl.ds(0, 2), pl.ds(depth + 2, 2)
    mid_y, mid_z = pl.ds(2, rows), pl.ds(2, depth)
    b_ref[:, :, depth + 4 :] = jnp.zeros_like(b_ref[:, :, depth + 4 :])
    b_ref[:, mid_y, mid_z] = field_ref[...]
    all_y = pl.ds(0, rows_wide)
    places = [(low_y, mid_z), (high_y, mid_z), (all_y, low_z), (all_y, high_z)]
    for ref, (y, z) in zip(halos, places):
        b_ref[:, y, z] = ref[...]
    shape = (depth_wide, width)
    lane = lax.broadcasted_iota(jnp.int32, shape, 1)
    z_cell = origin_ref[1] + lax.broadcasted_iota(jnp.int32, shape, 0) - 2
    z_inside = (z_cell >= 0) & (z_cell < total_z)
    z_own = lax.broadcasted_iota(jnp.int32, shape, 0)
    z_own = (z_own >= 2) & (z_own < depth + 2)
    scale = 1.0 / (total_y * total_z * width)

    def next_x(v):
        return jnp.where(lane == width - 1, 0.0, pltpu.roll(v, width - 1, 1))

    def last_x(v):
        return jnp.where(lane == 0, 0.0, pltpu.roll(v, 1, 1))

    def next_z(v):
        return pltpu.roll(v, depth_wide - 1, 0)

    def last_z(v):
        return pltpu.roll(v, 1, 0)

    def terms(n, loss):
        b = [b_ref[a, n + 1] for a in range(3)]
        dx = [(next_x(v) - last_x(v)) * 0.5 for v in b]
        dy = [(b_ref[a, n + 2] - b_ref[a, n]) * 0.5 for a in range(3)]
        dz = [(next_z(v) - last_z(v)) * 0.5 for v in b]
        jx = dy[2] - dz[1]
        jy = dz[0] - dx[2]
        jz = dx[1] - dy[0]
        fx = jy * b[2] - jz * b[1]
        fy = jz * b[0] - jx * b[2]
        fz = jx * b[1] - jy * b[0]
        q = dx[0] + dy[1] + dz[2]
        strength = b[0] * b[0] + b[1] * b[1] + b[2] * b[2] + 1.0
        inverse = 1.0 / strength
        ratio = (fx * fx + fy * fy + fz * fz) * inverse
        y_cell = origin_ref[0] + n - 1
        y_inside = (y_cell >= 0) & (y_cell < total_y)
        own = z_own & (n >= 1) & (n <= rows)
        loss = loss + jnp.where(own, ratio + q * q, 0.0)
        weight = jnp.where(z_inside & y_inside, 2.0 * scale, 0.0)
        inverse = inverse * weight
        pull = ratio * inverse
        fx, fy, fz = fx * inverse, fy * inverse, fz * inverse
        q = q * weight
        cx = b[1] * fz - b[2] * fy
        cy = b[2] * fx - b[0] * fz
        cz = b[0] * fy - b[1] * fx
        db = [
            fy * jz - fz * jy - pull * b[0],
            fz * jx - fx * jz - pull * b[1],
            fx * jy - fy * jx - pull * b[2],
        ]
        gx = [q, cz, -cy]
        gy = [-cz, q, cx]
        gz = [cy, -cx, q]
        for a in range(3):
            gy_ref[a, n] = gy[a]
            back = last_x(gx[a]) - next_x(gx[a]) + last_z(gz[a]) - next_z(gz[a])
            rest_ref[a, n] = db[a] + back * 0.5
        return loss

    loss = lax.fori_loop(0, rows + 2, terms, jnp.zeros(shape, F32))

    def combine(n, sums):
        done = []
        for a in range(3):
            grad = rest_ref[a, n + 1] + (gy_ref[a, n] - gy_ref[a, n + 2]) * 0.5
            grad = grad[2 : depth + 2]
            grad_ref[a, n] = grad
            done.append(sums[a] + grad)
        return tuple(done)

    sums = lax.fori_loop(0, rows, combine, (jnp.zeros((depth, width), F32),) * 3)
    sums_ref[...] = jnp.zeros_like(sums_ref)
    for a in range(3):
        sums_ref[a : a + 1, :] = jnp.sum(sums[a], axis=0, keepdims=True)
    sums_ref[3:4, :] = jnp.sum(loss, axis=0, keepdims=True)


def stencil(lay, b_field):
    halos = halo(b_field)
    origin = jnp.stack([lay.y0, lay.z0]).astype(jnp.int32)
    wide = (3, lay.rows + 2, lay.depth + 8, lay.width)
    return pl.pallas_call(
        functools.partial(stencil_kernel, lay.ny, lay.nz),
        in_specs=[
            pl.BlockSpec(memory_space=pltpu.SMEM),
        ]
        + [VMEM] * 5,
        out_specs=[pl.BlockSpec(memory_space=pltpu.VMEM)] * 2,
        out_shape=[
            jax.ShapeDtypeStruct(b_field.shape, F32),
            jax.ShapeDtypeStruct((8, lay.width), F32),
        ],
        scratch_shapes=[
            pltpu.VMEM((3, lay.rows + 4) + wide[2:], F32),
            pltpu.VMEM(wide, F32),
            pltpu.VMEM(wide, F32),
        ],
        compiler_params=pltpu.CompilerParams(vmem_limit_bytes=VMEM_LIMIT),
        name="stencil",
    )(origin, b_field, *halos)


def grad_kernel(first, n_after, weight_ref, hidden_ref, slope_ref, grad_ref, x_ref, z_ref, y_ref,
                *refs):
    pre_ref, own_ref, send_ref, sums_ref, part_ref = refs[n_after:]
    pack, rows, depth, width = hidden_ref.shape
    blocks = part_ref.shape[2]
    band = rows // blocks
    channel = (first + pl.program_id(0)) * pack

    def fold(v):
        return jnp.sum(v.reshape(-1, 8, width), axis=0)

    per = max(CHUNK // (band * depth), 1)
    span = per * band
    count = rows // span

    def slopes(n):
        sums = [0.0] * (3 * pack)
        for y in range(n * span, (n + 1) * span):
            grads = [grad_ref[b, y] for b in range(3)]
            for c in range(pack):
                w = [weight_ref[channel + c, b] for b in range(3)]
                mixed = grads[0] * w[0] + grads[1] * w[1] + grads[2] * w[2]
                pre_ref[c, y] = (mixed * slope_ref[c, y].astype(F32)).astype(BF16)
                hidden = hidden_ref[c, y].astype(F32)
                for b in range(3):
                    sums[3 * c + b] = sums[3 * c + b] + fold(hidden * grads[b])
        return sums

    def transform(n):
        total = x_transform(pre_ref.at[:, n * span : (n + 1) * span], x_ref)
        for m in range(per):
            here = total[m * band * depth : (m + 1) * band * depth]
            z_transform(here, z_ref, part_ref, n * per + m)
        return fold(total)

    parts = [slopes(0)]
    totals = []
    for n in range(1, count):
        parts.append(slopes(n))
        totals.append(transform(n - 1))
    totals.append(transform(count - 1))
    sums = [sum(column[1:], column[0]) for column in zip(*parts)]
    sums.append(sum(totals[1:], totals[0]))
    sums_ref[...] = jnp.zeros_like(sums_ref)
    for n, part in enumerate(sums):
        sums_ref[0, n : n + 1, :] = jnp.sum(part, axis=0, keepdims=True)
    y_transform(y_ref, part_ref, own_ref, send_ref)


def grad_modes(lay, hidden, slope, grad_b, x_table, tables, weights, first, count, after=()):
    out, spec = mode_blocks(lay, count)
    block = (lay.pack, lay.rows, lay.depth, lay.width)
    part = pl.BlockSpec(block, lambda i: (i, 0, 0, 0))
    given = pl.BlockSpec(block, lambda i: (first + i, 0, 0, 0))
    volume = lay.pack * lay.cells * lay.width
    lines = -(-(3 * lay.pack + 1) // 8) * 8
    return pl.pallas_call(
        functools.partial(grad_kernel, first, len(after)),
        grid=(count,),
        in_specs=[
            pl.BlockSpec(memory_space=pltpu.SMEM),
            given,
            given,
            whole(grad_b.shape),
            whole(x_table.shape),
            whole(tables[0].shape),
            whole(tables[1].shape),
        ]
        + [ANY] * len(after),
        out_specs=[
            part,
            spec,
            spec,
            pl.BlockSpec((1, lines, lay.width), lambda i: (i, 0, 0)),
        ],
        out_shape=[
            jax.ShapeDtypeStruct((count * lay.pack,) + block[1:], BF16),
            out,
            out,
            jax.ShapeDtypeStruct((count, lines, lay.width), F32),
        ],
        scratch_shapes=[part_scratch(lay)],
        compiler_params=params(),
        cost_estimate=cost(count * volume * 2 * 2 * LANES, count * volume * 10),
        name="grad_modes",
    )(weights, hidden, slope, grad_b, x_table, tables[0], tables[1], *after)


def point_kernel(tile, n_after, field_ref, grad_ref, *refs):
    out_ref, acc_ref = refs[n_after:]
    channels, rows, depth, width = field_ref.shape
    count = grad_ref.shape[0]
    step = pl.program_id(0)

    @pl.when(step == 0)
    def _():
        acc_ref[...] = jnp.zeros_like(acc_ref)

    left, right = [], []
    for y in range(rows):
        for z in range(0, depth, tile):
            left.append(field_ref[:, y, z : z + tile, :].reshape(channels * tile, width))
            right.append(grad_ref[:, y, z : z + tile, :].reshape(count * tile, width))
    acc_ref[...] += lax.dot_general(
        jnp.concatenate(left, axis=1),
        jnp.concatenate(right, axis=1),
        (((1,), (1,)), ((), ())),
        preferred_element_type=F32,
    )

    @pl.when(step == pl.num_programs(0) - 1)
    def _():
        def pick(n):
            owner = lax.broadcasted_iota(jnp.int32, (n, n * tile), 1) // tile
            return (owner == lax.broadcasted_iota(jnp.int32, (n, n * tile), 0)).astype(F32)

        row = lax.broadcasted_iota(jnp.int32, acc_ref.shape, 0)
        column = lax.broadcasted_iota(jnp.int32, acc_ref.shape, 1)
        kept = jnp.where(row % tile == column % tile, acc_ref[...], 0.0)
        half = jnp.dot(
            pick(channels), kept, precision=lax.Precision.HIGHEST, preferred_element_type=F32
        )
        out_ref[...] = lax.dot_general(
            half,
            pick(count),
            (((1,), (1,)), ((), ())),
            precision=lax.Precision.HIGHEST,
            preferred_element_type=F32,
        )


def point_grad(lay, field_in, grad_pre, first, rows, after=()):
    span = math.gcd(4, rows)

    def block(count):
        size = (count, span, lay.depth, lay.width)
        return pl.BlockSpec(size, lambda i: (0, first // span + i, 0, 0))

    count = grad_pre.shape[0]
    size = lay.channels * lay.tile
    return pl.pallas_call(
        functools.partial(point_kernel, lay.tile, len(after)),
        grid=(rows // span,),
        in_specs=[block(lay.channels), block(count)] + [ANY] * len(after),
        out_specs=pl.BlockSpec((lay.channels, count), lambda i: (0, 0)),
        out_shape=jax.ShapeDtypeStruct((lay.channels, count), F32),
        scratch_shapes=[pltpu.VMEM((size, count * lay.tile), F32)],
        compiler_params=params(),
        cost_estimate=cost(2 * size * count * lay.cells * lay.width, 3 * field_in.size),
        name="point_grad",
    )(field_in, grad_pre, *after)


def outer_kernel(modes_ref, grads_ref, *refs):
    out_ref = refs[-1]
    pair, count, channels, wide = out_ref.shape[1:]
    columns = jnp.concatenate([modes_ref[0, a] for a in range(pair)], axis=1)
    rows = []
    for a in range(pair):
        right = grads_ref[0, a]
        turned = jnp.concatenate([right[:, channels:], -right[:, :channels]], axis=1)
        right = jnp.concatenate([right, turned], axis=0)
        zero = jnp.zeros_like(right)
        rows.append(jnp.concatenate([right if n == a else zero for n in range(pair)], axis=1))
    rows = jnp.concatenate(rows, axis=0)
    owner = lax.broadcasted_iota(jnp.int32, columns.shape, 1) % count
    zero = jnp.zeros_like(columns)
    some = 8
    for k in range(0, count, some):
        left = [jnp.where(owner == k + n, columns, zero) for n in range(some)]
        out = dot(jnp.concatenate(left, axis=0), rows)
        for a in range(pair):
            here = out[:, wide * a : wide * (a + 1)]
            out_ref[0, a, k : k + some] = here.reshape(some, channels, wide)


def weight_grad(lay, columns, rows, half, done=(), after=()):
    tile = (lay.mx, lay.channels, 2 * lay.channels)
    shape = (lay.kz, lay.ky) + tile
    per = lay.ky // 2
    first = half * lay.kz // 2

    def spec(block):
        return pl.BlockSpec(
            (1, 2) + block, lambda i: (first + i // per, i % per) + (0,) * len(block)
        )

    return pl.pallas_call(
        outer_kernel,
        grid=(lay.own // 4,),
        in_specs=[spec(columns.shape[2:]), spec(rows.shape[2:])]
        + [ANY] * (len(done) + len(after)),
        out_specs=spec(tile),
        out_shape=jax.ShapeDtypeStruct(shape, F32),
        input_output_aliases={2: 0} if done else {},
        compiler_params=params(),
        cost_estimate=cost(math.prod(shape) * 2, math.prod(shape) * 2),
        name="weight_grad",
    )(columns, rows, *done, *after)


def pack_kernel(n_parts, *refs):
    small_ref, out_ref = refs[n_parts], refs[-1]
    count = refs[0].shape[0]
    total = refs[0][...]
    for ref in refs[1:n_parts]:
        total = total + ref[...]
    out_ref[...] = jnp.zeros_like(out_ref)
    out_ref[:count, :count] = total
    out_ref[count:] = small_ref[...]


def pack_sums(lay, parts, small, after):
    return pl.pallas_call(
        functools.partial(pack_kernel, len(parts)),
        in_specs=[VMEM] * (len(parts) + 1) + [ANY] * len(after),
        out_specs=VMEM,
        out_shape=jax.ShapeDtypeStruct((lay.channels + small.shape[0], LANES), F32),
        name="pack_sums",
    )(*parts, small, *after)


def unpack_kernel(cells, left_ref, right_ref, *refs):
    loss_ref, point_ref, outs_ref, bias_ref, ends_ref = refs[-5:]
    count = point_ref.shape[0]
    total = left_ref[...] + right_ref[...]
    point_ref[...] = total[:count, :count]
    outs_ref[...] = total[count : count + 3, :count]
    bias_ref[...] = total[count + 3 : count + 4, :count]
    ends_ref[...] = total[count + 4 : count + 5, :3]
    loss_ref[...] = total[count + 4 : count + 5, 3:4] / cells


def unpack_sums(lay, left, right, after):
    count = lay.channels
    shapes = [(1, 1), (count, count), (3, count), (1, count), (1, 3)]
    return pl.pallas_call(
        functools.partial(unpack_kernel, lay.width * lay.ny * lay.nz),
        in_specs=[VMEM] * 2 + [ANY] * len(after),
        out_specs=[VMEM] * len(shapes),
        out_shape=[jax.ShapeDtypeStruct(shape, F32) for shape in shapes],
        name="unpack_sums",
    )(left, right, *after)


def on_device(field_in, spectral_weight, point_weight, point_bias, out_weight, out_bias):
    lay = Layout(field_in, spectral_weight)
    tables = lay.grid_tables()
    x_table, x_back = lay.x_tables()
    weights = out_weight.astype(F32)
    scale = math.sqrt(lay.mx * lay.my * lay.mz / (lay.width * lay.ny * lay.nz))
    cuts = [0, lay.rows * 3 // 4, lay.rows]

    def point(n, done, after):
        bias = point_bias.reshape(1, lay.channels)
        first, count = cuts[n], cuts[n + 1] - cuts[n]
        return pointwise(lay, field_in, point_weight.T, bias, first, count, done, after)

    own, send = forward_modes(lay, field_in, x_table, tables, 0, lay.groups)
    points = [None]

    def point_part(n, after):
        points.append(point(n, points[-1], after))
        return points[-1]

    b_field = jnp.broadcast_to(
        out_bias[:, None, None, None], (3, lay.rows, lay.depth, lay.width)
    ).astype(F32)
    last = [x_back, tables[2], tables[3], b_field]
    modes = sum_all(lay, own, send, scale, point_part, last)
    done = points[-1]
    modes_in = by_mode(lay, jnp.concatenate(modes))
    mixed = mix_modes(lay, modes_in, spectral_weight, after=[done])
    mine = by_group(lay, mixed.reshape(lay.kz, lay.ky, lay.mx, 2, lay.groups, lay.pack))

    first = max(lay.groups * 5 // 16, 1)
    columns = [spread_chips(lay, mine[:first]), spread_chips(lay, mine[first:])]
    own = spread_depth(lay, columns[0], columns[1:])
    *kept, b_field = dense(
        lay, own, exchange(own, "gy", 1), tables, x_back, done, weights, b_field, 0, first
    )
    own = spread_depth(lay, columns[1], [b_field])
    hidden, slope, b_field = dense(
        lay, own, exchange(own, "gy", 1), tables, x_back, done, weights, b_field,
        first, lay.groups - first, kept,
    )

    grad_b, edge = stencil(lay, b_field)

    pre, own, send, sums = grad_modes(
        lay, hidden, slope, grad_b, x_table, tables, weights, 0, lay.groups
    )
    point_parts = []

    def grad_part(n, after):
        count = cuts[n + 1] - cuts[n]
        point_parts.append(point_grad(lay, field_in, pre, cuts[n], count, after))
        return point_parts[-1]

    grads = sum_all(lay, own, send, 1.0, grad_part)
    outs = jnp.sum(sums[:, : 3 * lay.pack], axis=-1).reshape(lay.channels, 3).T
    bias = sums[:, 3 * lay.pack, :LANES].reshape(lay.groups, lay.pack, lay.mx)[..., 0]
    ends = jnp.pad(jnp.sum(edge[:4], axis=-1), (0, lay.channels - 4))
    small = [outs, bias.reshape(1, lay.channels), ends.reshape(1, lay.channels)]
    small = jnp.pad(jnp.concatenate(small), ((0, 3), (0, LANES - lay.channels)))
    flat = pack_sums(lay, point_parts, small, grads[-1:])
    rows = by_mode(lay, jnp.concatenate(grads))
    rows = jnp.concatenate([rows[:, :, : lay.mx], rows[:, :, lay.mx :]], axis=-1)
    columns = jnp.transpose(modes_in, (0, 1, 3, 2))

    def gathered(axis, steps):
        return [flat] + [exchange(flat, axis, d) for d in steps]

    flat = sum_blocks(gathered("gz", range(1, lay.n_gz)), False, 1.0, [rows])[0]
    grad_spectral = weight_grad(lay, columns, rows, 0, after=[flat])
    flat = sum_blocks(gathered("gy", range(CORES, lay.n_gy, CORES)), False, 1.0, [grad_spectral])
    flat = flat[0]
    grad_spectral = weight_grad(lay, columns, rows, 1, [grad_spectral], [flat])
    loss, grad_point, outs, bias, ends = unpack_sums(lay, *gathered("gy", [1]), [grad_spectral])
    return (
        loss.reshape(()),
        grad_spectral,
        grad_point,
        bias.reshape(lay.channels),
        outs.T,
        ends.reshape(3),
    )


def solution(mesh):
    return jax.shard_map(
        on_device,
        mesh=mesh,
        in_specs=(P(None, "gy", "gz", None), P("gz", "gy", None, None, None), P(), P(), P(), P()),
        out_specs=(P(), P("gz", "gy", None, None, None), P(), P(), P(), P()),
        check_vma=False,
    )
```

```python
import functools
import math

import jax
import jax.numpy as jnp
from jax import lax
from jax.experimental import pallas as pl
from jax.experimental.pallas import tpu as pltpu
from jax.sharding import PartitionSpec as P

F32 = jnp.float32
BF16 = jnp.bfloat16
CORES = 2
LANES = 128
VMEM_LIMIT = 56 * 1024 * 1024
CHUNK = 256


def params():
    return pltpu.CompilerParams(
        vmem_limit_bytes=VMEM_LIMIT, dimension_semantics=("arbitrary",)
    )


def whole(shape):
    return pl.BlockSpec(shape, lambda i: (0,) * len(shape), pipeline_mode=pl.Buffered(1))


ANY = pl.BlockSpec(memory_space=pl.ANY)


def cost(flops, moved):
    return pl.CostEstimate(flops=flops, bytes_accessed=moved, transcendentals=0)


def dot(a, b):
    return jnp.dot(a, b, preferred_element_type=F32)


def frequencies(mode_index, mode_total):
    return jnp.where(mode_index < mode_total // 2, mode_index, mode_index - mode_total)


def twiddle(product, length):
    phases = (product % length).astype(F32) * (2.0 * math.pi / length)
    return jnp.cos(phases).astype(BF16).astype(F32), jnp.sin(phases).astype(BF16).astype(F32)


def halo(block):
    def moved(value, axis, step):
        count = lax.axis_size(axis)
        pairs = [(n, n + step) for n in range(count) if 0 <= n + step < count]
        return lax.ppermute(value, axis, pairs)

    low = moved(block[:, -2:], "gy", 1)
    high = moved(block[:, :2], "gy", -1)
    ends = [
        jnp.concatenate([part[:, :, cut] for part in (low, block, high)], axis=1)
        for cut in (slice(-2, None), slice(0, 2))
    ]
    return [low, high, moved(ends[0], "gz", 1), moved(ends[1], "gz", -1)]


class Layout:
    def __init__(self, field_in, spectral_weight):
        self.channels, self.rows, self.depth, self.width = field_in.shape
        self.kz, self.ky, self.mx = spectral_weight.shape[:3]
        self.n_gy, self.n_gz = lax.axis_size("gy"), lax.axis_size("gz")
        self.chips = self.n_gy // CORES
        self.ny, self.nz = self.rows * self.n_gy, self.depth * self.n_gz
        self.my, self.mz = self.ky * self.n_gy, self.kz * self.n_gz
        self.cells = self.rows * self.depth
        self.modes = self.my * self.mz
        self.pack = LANES // self.mx
        self.groups = self.channels // self.pack
        self.own = self.ky * self.kz
        self.band = min(LANES // self.depth, self.rows)
        self.blocks = self.rows // self.band
        self.step = min(LANES // self.rows, self.kz)
        self.tile = 8
        self.gy, self.gz = lax.axis_index("gy"), lax.axis_index("gz")
        self.y0 = self.gy * self.rows
        self.z0 = self.gz * self.depth

    def grid_table(self, mode, cell, first, length, same):
        real, imag = twiddle(mode * (first + cell[0]), length)
        return jnp.where(same, jnp.where(cell[1] == 0, real, imag), 0.0).astype(BF16)

    def grid_tables(self):
        core, chip = self.gy % CORES, self.gy // CORES

        def iotas(rows, columns):
            shape = (rows, columns)
            row = lax.broadcasted_iota(jnp.int32, shape, 0)
            return row, lax.broadcasted_iota(jnp.int32, shape, 1)

        def kz(n):
            return frequencies(((n // self.kz) ^ self.gz) * self.kz + n % self.kz, self.mz)

        def ky(n):
            h, f = n // (self.chips * self.ky), n // self.ky % self.chips
            return frequencies(((f ^ chip) * CORES + (h ^ core)) * self.ky + n % self.ky, self.my)

        band, step, depth = self.band, self.step, self.depth
        z_modes, y_modes = self.mz * band, self.my * step
        z_cells, y_cells = band * depth, self.blocks * step * band
        m, c = iotas(z_modes, 2 * z_cells)
        z_forward = self.grid_table(
            kz(m // band), (c % depth, c // z_cells), self.z0, self.nz,
            m % band == c // depth % band,
        )
        c, m = iotas(z_cells, 2 * z_modes)
        z_back = self.grid_table(
            kz(m % z_modes // band), (c % depth, m // z_modes), self.z0, self.nz,
            m % band == c // depth,
        )

        def row_of(c):
            return c // (step * band) % self.blocks * band + c % band

        m, c = iotas(y_modes, 2 * y_cells)
        y_forward = self.grid_table(
            ky(m // step), (row_of(c), c // y_cells), self.y0, self.ny,
            m % step == c // band % step,
        )
        c, m = iotas(y_cells, 2 * y_modes)
        y_back = self.grid_table(
            ky(m % y_modes // step), (row_of(c), m // y_modes), self.y0, self.ny,
            m % step == c // band % step,
        )
        return z_forward, y_forward, y_back, z_back

    def x_tables(self):
        shape = (self.width, 2 * LANES)
        x = lax.broadcasted_iota(jnp.int32, shape, 0)
        lane = lax.broadcasted_iota(jnp.int32, shape, 1)
        cos, sin = twiddle(x * frequencies(lane % self.mx, self.mx), self.width)
        table = jnp.where(lane < LANES, cos, -sin).astype(BF16)
        owner = lane % LANES // self.mx
        forward = [jnp.where(owner == c, table, 0) for c in range(self.pack)]
        lane, x = (lax.broadcasted_iota(jnp.int32, shape[::-1], d) for d in range(2))
        cos, sin = twiddle(x * frequencies(lane % self.mx, self.mx), self.width)
        table = jnp.where(lane < LANES, cos, -sin).astype(BF16)
        owner = lane % LANES // self.mx
        inverse = [jnp.where(owner == c, table, 0) for c in range(self.pack)]
        return jnp.concatenate(forward, axis=0), jnp.concatenate(inverse, axis=1)


def turn(values, sign):
    real, imag = values[:, :LANES], values[:, LANES:]
    return jnp.concatenate([imag, -real] if sign > 0 else [-imag, real], axis=1)


def z_transform(x_modes, table_ref, part_ref, n):
    x_modes = x_modes.astype(BF16)
    rhs = jnp.concatenate([x_modes, turn(x_modes, 1)], axis=0)
    modes = dot(table_ref[...], rhs).astype(BF16)
    steps, _, _, size, _ = part_ref.shape
    part_ref[:, 0, n] = modes.reshape(steps, size, 2 * LANES)
    part_ref[:, 1, n] = turn(modes, 1).reshape(steps, size, 2 * LANES)


def y_transform(table_ref, part_ref, own_ref, send_ref):
    half = table_ref.shape[0] // 2
    steps, _, blocks, size, _ = part_ref.shape
    chips = own_ref.shape[1]
    rows = half // chips
    per = steps // own_ref.shape[0]
    for q in range(steps):
        modes = dot(table_ref[...], part_ref[q].reshape(2 * blocks * size, 2 * LANES))
        modes = modes.astype(BF16)
        here = pl.ds(q % per * rows, rows)
        own_ref[q // per, :, 0, here] = modes[:half].reshape(chips, rows, 2 * LANES)
        send_ref[q // per, :, 0, here] = modes[half:].reshape(chips, rows, 2 * LANES)


def x_transform(source_ref, x_ref):
    pack, rows, depth, width = source_ref.shape
    cells = [source_ref[c].reshape(rows * depth, width) for c in range(pack)]
    return dot(jnp.concatenate(cells, axis=1), x_ref[...])


def modes_kernel(n_after, field_ref, x_ref, z_ref, y_ref, *refs):
    own_ref, send_ref, part_ref = refs[n_after:]
    total = x_transform(field_ref, x_ref)
    blocks = part_ref.shape[2]
    size = total.shape[0] // blocks
    for n in range(blocks):
        z_transform(total[n * size : (n + 1) * size], z_ref, part_ref, n)
    y_transform(y_ref, part_ref, own_ref, send_ref)


def mode_blocks(lay, count):
    shape = (lay.n_gz, lay.chips, count, lay.own, 2 * LANES)
    spec = pl.BlockSpec((lay.n_gz, lay.chips, 1, lay.own, 2 * LANES), lambda i: (0, 0, i, 0, 0))
    return jax.ShapeDtypeStruct(shape, BF16), spec


def part_scratch(lay):
    size = lay.step * lay.band
    return pltpu.VMEM((lay.mz // lay.step, 2, lay.blocks, size, 2 * LANES), BF16)


def forward_modes(lay, field_in, x_table, tables, first, count, after=()):
    out, spec = mode_blocks(lay, count)
    block = (lay.pack, lay.rows, lay.depth, lay.width)
    volume = lay.pack * lay.cells * lay.width
    return pl.pallas_call(
        functools.partial(modes_kernel, len(after)),
        grid=(count,),
        in_specs=[
            pl.BlockSpec(block, lambda i: (first + i, 0, 0, 0)),
            whole(x_table.shape),
            whole(tables[0].shape),
            whole(tables[1].shape),
        ]
        + [ANY] * len(after),
        out_specs=[spec, spec],
        out_shape=[out, out],
        scratch_shapes=[part_scratch(lay)],
        compiler_params=params(),
        cost_estimate=cost(count * volume * 2 * 2 * LANES, count * volume * 3),
        name="forward_modes",
    )(field_in, x_table, tables[0], tables[1], *after)


def exchange(value, axis, distance):
    count = lax.axis_size(axis)
    return lax.ppermute(value, axis, [(i, i ^ distance) for i in range(count)])


def sum_kernel(n_in, n_out, factor, *refs):
    rows = refs[0].shape[1]
    chunk = math.gcd(rows, 256)

    def body(n, carry):
        here = pl.ds(pl.multiple_of(n * chunk, chunk), chunk)
        for m, out_ref in enumerate(refs[-n_out:]):
            total = refs[0][m, here].astype(F32)
            for ref in refs[1:n_in]:
                total = total + ref[m, here].astype(F32)
            out_ref[here] = (total * factor).astype(out_ref.dtype)
        return carry

    lax.fori_loop(0, rows // chunk, body, 0)


VMEM = pl.BlockSpec(memory_space=pltpu.VMEM)


def sum_blocks(values, split, factor=1.0, after=(), weight=2):
    shape = values[0].shape
    n_out = shape[0] if split else 1
    rows = math.prod(shape[:-1]) // n_out
    values = [value.reshape(n_out, rows, shape[-1]) for value in values]
    outs = pl.pallas_call(
        functools.partial(sum_kernel, len(values), n_out, factor),
        in_specs=[VMEM] * len(values) + [ANY] * len(after),
        out_specs=[VMEM] * n_out,
        out_shape=[jax.ShapeDtypeStruct((rows, shape[-1]), values[0].dtype)] * n_out,
        compiler_params=pltpu.CompilerParams(vmem_limit_bytes=VMEM_LIMIT),
        cost_estimate=cost(math.prod(shape) * len(values), math.prod(shape) * weight * len(values)),
        name="sum_blocks",
    )(*values, *after)
    return [out.reshape(shape[1:] if split else shape) for out in outs]


def core_kernel(own_ref, other_ref, *refs):
    count = own_ref.shape[0]
    cut = refs[0].shape[1]
    for n in range(count):
        total = (own_ref[n, 0].astype(F32) + other_ref[n, 0].astype(F32)).astype(BF16)
        refs[n][0] = total[:cut]
        refs[count + n][0] = total[cut:]


def from_cores(lay, own, other):
    tail = (lay.own, 2 * LANES)
    cut = max(lay.groups * 5 // 8, 1)
    given = pl.BlockSpec((lay.n_gz, 1, lay.groups) + tail, lambda i: (0, i, 0, 0, 0))
    sizes = [cut] * lay.n_gz + [lay.groups - cut] * lay.n_gz
    outs = pl.pallas_call(
        core_kernel,
        grid=(lay.chips,),
        in_specs=[given, given],
        out_specs=[pl.BlockSpec((1, size) + tail, lambda i: (i, 0, 0, 0)) for size in sizes],
        out_shape=[jax.ShapeDtypeStruct((lay.chips, size) + tail, BF16) for size in sizes],
        compiler_params=params(),
        cost_estimate=cost(own.size, own.size * 6),
        name="core_sums",
    )(own, other)
    return list(outs[: lay.n_gz]), list(outs[lay.n_gz :])


def sum_all(lay, own, send, factor, work, last=()):
    early, late = from_cores(lay, own, exchange(send, "gy", 1))
    done = work(0, early[:1])
    early = sum_blocks(to_depth(early), True, after=[done])
    done = work(1, early[:1])
    first = from_chips(early, factor, [done])
    late = sum_blocks(to_depth(late), True, after=[first])
    return [first, from_chips(late, factor, last)]


def to_depth(blocks):
    return blocks[:1] + [exchange(block, "gz", d) for d, block in enumerate(blocks) if d]


def from_chips(blocks, factor, after=()):
    got = [exchange(block, "gy", d * CORES) for d, block in enumerate(blocks) if d]
    return sum_blocks(blocks[:1] + got, False, factor, after)[0]


def stack_kernel(n_in, *refs):
    rows = refs[0].shape[0]
    chunk = math.gcd(rows, 256)

    def body(n, carry):
        here = pl.ds(pl.multiple_of(n * chunk, chunk), chunk)
        for m in range(n_in):
            refs[-1][m, here] = refs[m][here]
        return carry

    lax.fori_loop(0, rows // chunk, body, 0)


def stack_blocks(values, after=()):
    shape = values[0].shape
    flat = [value.reshape(-1, shape[-1]) for value in values]
    out = (len(values),) + flat[0].shape
    stacked = pl.pallas_call(
        functools.partial(stack_kernel, len(values)),
        in_specs=[VMEM] * len(values) + [ANY] * len(after),
        out_specs=VMEM,
        out_shape=jax.ShapeDtypeStruct(out, values[0].dtype),
        compiler_params=pltpu.CompilerParams(vmem_limit_bytes=VMEM_LIMIT),
        cost_estimate=cost(math.prod(out), 4 * math.prod(out)),
        name="stack_blocks",
    )(*flat, *after)
    return stacked.reshape((len(values),) + shape)


def spread_chips(lay, mine):
    return stack_blocks([mine] + [exchange(mine, "gy", d * CORES) for d in range(1, lay.chips)])


def spread_depth(lay, column, after=()):
    pieces = [column] + [exchange(column, "gz", d) for d in range(1, lay.n_gz)]
    return stack_blocks(pieces, after)


def by_mode(lay, modes):
    count = modes.shape[0]
    split = modes.reshape(
        count, lay.kz // lay.step, lay.ky, lay.step, 2, lay.pack, lay.mx
    )
    return jnp.transpose(split, (1, 3, 2, 4, 6, 0, 5)).reshape(
        lay.kz, lay.ky, 2 * lay.mx, count * lay.pack
    )


def by_group(lay, modes):
    split = modes.reshape(
        lay.kz // lay.step, lay.step, lay.ky, lay.mx, 2, lay.groups, lay.pack
    )
    return jnp.transpose(split, (5, 0, 2, 1, 4, 6, 3)).reshape(
        lay.groups, lay.own, 2 * LANES
    )


def mix_kernel(modes_ref, weight_ref, *refs):
    out_ref = refs[-1]
    pair, count, channels, wide = weight_ref.shape[1:]
    per = wide // channels
    spread = []
    for a in range(pair):
        modes = jnp.concatenate([modes_ref[0, a]] * per, axis=1)
        row = lax.broadcasted_iota(jnp.int32, modes.shape, 0) % count
        owner = lax.broadcasted_iota(jnp.int32, modes.shape, 1) // channels
        zero = jnp.zeros_like(modes)
        parts = [jnp.where(row == owner + n * per, modes, zero) for n in range(count // per)]
        spread.append(jnp.concatenate(parts, axis=1))
    weights = [weight_ref[0, a].reshape(count * channels, wide) for a in range(pair)]
    mixed = dot(jnp.concatenate(spread, axis=0), jnp.concatenate(weights, axis=1))
    for a in range(pair):
        own = mixed[2 * count * a : 2 * count * (a + 1), wide * a : wide * (a + 1)]
        real, imag = own[:count], own[count:]
        turned = jnp.concatenate([-imag[:, channels:], imag[:, :channels]], axis=1)
        out_ref[0, a] = (real + turned).astype(BF16)


def mode_spec(lay, shape):
    per = lay.ky // 2
    return pl.BlockSpec((1, 2) + shape, lambda i: (i // per, i % per) + (0,) * len(shape))


def mix_modes(lay, modes_in, spectral_weight, after=()):
    shape = (lay.mx, 2 * lay.channels)
    return pl.pallas_call(
        mix_kernel,
        grid=(lay.own // 2,),
        in_specs=[mode_spec(lay, modes_in.shape[2:]), mode_spec(lay, spectral_weight.shape[2:])]
        + [ANY] * len(after),
        out_specs=mode_spec(lay, shape),
        out_shape=jax.ShapeDtypeStruct((lay.kz, lay.ky) + shape, BF16),
        compiler_params=params(),
        cost_estimate=cost(spectral_weight.size * 8, spectral_weight.size * 2),
        name="mix_modes",
    )(modes_in, spectral_weight, *after)


def pointwise_kernel(tile, field_ref, weight_ref, bias_ref, *refs):
    out_ref, blocks_ref, shift_ref = refs[-3:]
    channels, rows, depth, width = field_ref.shape

    @pl.when(pl.program_id(0) == 0)
    def _():
        shape = (tile * channels, channels)
        split = lax.broadcasted_iota(jnp.int32, shape, 0) // tile
        split = split == lax.broadcasted_iota(jnp.int32, shape, 1)
        shift = jnp.sum(jnp.where(split, bias_ref[...], 0.0), axis=1, keepdims=True)
        shift_ref[...] = jnp.broadcast_to(shift, shift_ref.shape)
        split = split.astype(BF16)
        wide = dot(split, weight_ref[...]).astype(BF16)
        wide = lax.dot_general(
            wide, split, (((1,), (1,)), ((), ())), preferred_element_type=F32
        )
        row = lax.broadcasted_iota(jnp.int32, wide.shape, 0) % tile
        column = lax.broadcasted_iota(jnp.int32, wide.shape, 1) % tile
        blocks_ref[...] = jnp.where(row == column, wide, 0.0).astype(BF16)

    for y in range(rows):
        for z in range(0, depth, tile):
            cells = field_ref[:, y, z : z + tile, :].reshape(channels * tile, width)
            mixed = (dot(blocks_ref[...], cells) + shift_ref[...]).astype(BF16)
            out_ref[:, y, z : z + tile, :] = mixed.reshape(channels, tile, width)


def pointwise(lay, field_in, weight, bias, first, count, done=None, after=()):
    span = 2
    size = lay.channels * lay.tile
    given = [] if done is None else [done]
    block = pl.BlockSpec(
        (lay.channels, span, lay.depth, lay.width), lambda i: (0, first // span + i, 0, 0)
    )
    return pl.pallas_call(
        functools.partial(pointwise_kernel, lay.tile),
        grid=(count // span,),
        in_specs=[block, whole(weight.shape), whole(bias.shape)]
        + [ANY] * (len(given) + len(after)),
        out_specs=block,
        out_shape=jax.ShapeDtypeStruct(field_in.shape, BF16),
        scratch_shapes=[pltpu.VMEM((size, size), BF16), pltpu.VMEM((size, lay.width), F32)],
        input_output_aliases={3: 0} if given else {},
        compiler_params=params(),
        cost_estimate=cost(
            2 * size * lay.channels * count * lay.depth * lay.width,
            4 * lay.channels * count * lay.depth * lay.width,
        ),
        name="pointwise",
    )(field_in, weight, bias, *given, *after)


def gelu_and_slope(v):
    bell = jnp.exp2(v * v * (-0.5 * math.log2(math.e)))
    base = 1.0 + jnp.abs(v) * (0.3275911 / math.sqrt(2.0))
    t = pl.reciprocal(base, approx=True)
    poly = 0.5 * 1.061405429
    for coefficient in (-1.453152027, 1.421413741, -0.284496736, 0.254829592):
        poly = poly * t + 0.5 * coefficient
    tail = poly * t * bell
    cdf = jnp.where(v >= 0.0, 1.0 - tail, tail)
    return v * cdf, cdf + v * (bell * (1.0 / math.sqrt(2.0 * math.pi)))


def dense_kernel(
    first, own_ref, other_ref, y_ref, z_ref, x_ref, point_ref, weight_ref, b_in_ref, *refs
):
    hidden_ref, slope_ref, b_ref, part_ref, even_ref, odd_ref = refs[-6:]
    pack, rows, depth, width = point_ref.shape
    blocks, _, steps, size, _ = part_ref.shape
    band = rows // blocks
    step = pl.program_id(0)

    @pl.when(step == 0)
    def _():
        b_ref[...] = b_in_ref[...]

    depths, chips = own_ref.shape[:2]
    per = steps // depths
    rows_here = own_ref.shape[3] // per
    for q in range(steps):
        here = pl.ds(q % per * rows_here, rows_here)
        chunks = [
            piece[q // per, :, 0, here].reshape(chips * rows_here, 2 * LANES)
            for piece in (own_ref, other_ref)
        ]
        modes = jnp.concatenate(chunks, axis=0)
        back = dot(y_ref[...], jnp.concatenate([modes, turn(modes, -1)], axis=0)).astype(BF16)
        part_ref[:, 0, q] = back.reshape(blocks, size, 2 * LANES)
        part_ref[:, 1, q] = turn(back, -1).reshape(blocks, size, 2 * LANES)
    channel = (first + step) * pack

    per = even_ref.shape[0] // (band * depth)
    span = per * band
    count = rows // span

    def spectral(out_ref, n):
        cells = [
            dot(z_ref[...], part_ref[n * per + m].reshape(2 * steps * size, 2 * LANES))
            for m in range(per)
        ]
        out_ref[...] = dot(jnp.concatenate(cells, axis=0).astype(BF16), x_ref[...])

    def activate(spectral_ref, n):
        for m in range(span):
            y = n * span + m
            parts = [b_ref[b, y] for b in range(3)]
            for c in range(pack):
                value = spectral_ref[m * depth : (m + 1) * depth, c * width : (c + 1) * width]
                value = value + point_ref[c, y].astype(F32)
                hidden, slope = gelu_and_slope(value)
                hidden = hidden.astype(BF16)
                hidden_ref[c, y] = hidden
                slope_ref[c, y] = slope.astype(BF16)
                hidden = hidden.astype(F32)
                parts = [parts[b] + hidden * weight_ref[channel + c, b] for b in range(3)]
            for b in range(3):
                b_ref[b, y] = parts[b]

    spectral(even_ref, 0)
    if count == 1:
        activate(even_ref, 0)
        return

    def body(m, carry):
        spectral(odd_ref, 2 * m + 1)
        activate(even_ref, 2 * m)
        spectral(even_ref, jnp.minimum(2 * m + 2, count - 1))
        activate(odd_ref, 2 * m + 1)
        return carry

    lax.fori_loop(0, count // 2, body, 0)


def dense(lay, own, other, tables, x_table, point, weights, b_in, first, count, kept=()):
    size = (lay.n_gz, lay.chips, 1, lay.own, 2 * LANES)
    modes = pl.BlockSpec(size, lambda i: (0, 0, i, 0, 0))
    block = (lay.pack, lay.rows, lay.depth, lay.width)
    part = pl.BlockSpec(block, lambda i: (first + i, 0, 0, 0))
    out = jax.ShapeDtypeStruct(point.shape, BF16)
    volume = lay.pack * lay.cells * lay.width
    steps = lay.mz // lay.step
    return pl.pallas_call(
        functools.partial(dense_kernel, first),
        grid=(count,),
        in_specs=[
            modes,
            modes,
            whole(tables[2].shape),
            whole(tables[3].shape),
            whole(x_table.shape),
            part,
            pl.BlockSpec(memory_space=pltpu.SMEM),
            whole(b_in.shape),
        ]
        + [ANY] * len(kept),
        out_specs=[part, part, whole(b_in.shape)],
        out_shape=[out, out, jax.ShapeDtypeStruct(b_in.shape, F32)],
        input_output_aliases={8 + n: n for n in range(len(kept))},
        scratch_shapes=[
            pltpu.VMEM((lay.blocks, 2, steps, lay.step * lay.band, 2 * LANES), BF16),
            pltpu.VMEM((CHUNK, lay.pack * lay.width), F32),
            pltpu.VMEM((CHUNK, lay.pack * lay.width), F32),
        ],
        compiler_params=params(),
        cost_estimate=cost(count * volume * 2 * 6 * LANES, count * volume * 24),
        name="dense",
    )(own, other, tables[2], tables[3], x_table, point, weights, b_in, *kept)


def stencil_kernel(total_y, total_z, origin_ref, field_ref, *refs):
    halos, (grad_ref, sums_ref, b_ref, gy_ref, rest_ref) = refs[:4], refs[4:]
    _, rows_wide, depth_wide, width = b_ref.shape
    rows, depth = grad_ref.shape[1:3]
    low_y, high_y = pl.ds(0, 2), pl.ds(rows + 2, 2)
    low_z, high_z = pl.ds(0, 2), pl.ds(depth + 2, 2)
    mid_y, mid_z = pl.ds(2, rows), pl.ds(2, depth)
    b_ref[:, :, depth + 4 :] = jnp.zeros_like(b_ref[:, :, depth + 4 :])
    b_ref[:, mid_y, mid_z] = field_ref[...]
    all_y = pl.ds(0, rows_wide)
    places = [(low_y, mid_z), (high_y, mid_z), (all_y, low_z), (all_y, high_z)]
    for ref, (y, z) in zip(halos, places):
        b_ref[:, y, z] = ref[...]
    shape = (depth_wide, width)
    lane = lax.broadcasted_iota(jnp.int32, shape, 1)
    z_cell = origin_ref[1] + lax.broadcasted_iota(jnp.int32, shape, 0) - 2
    z_inside = (z_cell >= 0) & (z_cell < total_z)
    z_own = lax.broadcasted_iota(jnp.int32, shape, 0)
    z_own = (z_own >= 2) & (z_own < depth + 2)
    scale = 1.0 / (total_y * total_z * width)

    def next_x(v):
        return jnp.where(lane == width - 1, 0.0, pltpu.roll(v, width - 1, 1))

    def last_x(v):
        return jnp.where(lane == 0, 0.0, pltpu.roll(v, 1, 1))

    def next_z(v):
        return pltpu.roll(v, depth_wide - 1, 0)

    def last_z(v):
        return pltpu.roll(v, 1, 0)

    def terms(n, loss):
        b = [b_ref[a, n + 1] for a in range(3)]
        dx = [(next_x(v) - last_x(v)) * 0.5 for v in b]
        dy = [(b_ref[a, n + 2] - b_ref[a, n]) * 0.5 for a in range(3)]
        dz = [(next_z(v) - last_z(v)) * 0.5 for v in b]
        jx = dy[2] - dz[1]
        jy = dz[0] - dx[2]
        jz = dx[1] - dy[0]
        fx = jy * b[2] - jz * b[1]
        fy = jz * b[0] - jx * b[2]
        fz = jx * b[1] - jy * b[0]
        q = dx[0] + dy[1] + dz[2]
        strength = b[0] * b[0] + b[1] * b[1] + b[2] * b[2] + 1.0
        inverse = 1.0 / strength
        ratio = (fx * fx + fy * fy + fz * fz) * inverse
        y_cell = origin_ref[0] + n - 1
        y_inside = (y_cell >= 0) & (y_cell < total_y)
        own = z_own & (n >= 1) & (n <= rows)
        loss = loss + jnp.where(own, ratio + q * q, 0.0)
        weight = jnp.where(z_inside & y_inside, 2.0 * scale, 0.0)
        inverse = inverse * weight
        pull = ratio * inverse
        fx, fy, fz = fx * inverse, fy * inverse, fz * inverse
        q = q * weight
        cx = b[1] * fz - b[2] * fy
        cy = b[2] * fx - b[0] * fz
        cz = b[0] * fy - b[1] * fx
        db = [
            fy * jz - fz * jy - pull * b[0],
            fz * jx - fx * jz - pull * b[1],
            fx * jy - fy * jx - pull * b[2],
        ]
        gx = [q, cz, -cy]
        gy = [-cz, q, cx]
        gz = [cy, -cx, q]
        for a in range(3):
            gy_ref[a, n] = gy[a]
            back = last_x(gx[a]) - next_x(gx[a]) + last_z(gz[a]) - next_z(gz[a])
            rest_ref[a, n] = db[a] + back * 0.5
        return loss

    loss = lax.fori_loop(0, rows + 2, terms, jnp.zeros(shape, F32))

    def combine(n, sums):
        done = []
        for a in range(3):
            grad = rest_ref[a, n + 1] + (gy_ref[a, n] - gy_ref[a, n + 2]) * 0.5
            grad = grad[2 : depth + 2]
            grad_ref[a, n] = grad
            done.append(sums[a] + grad)
        return tuple(done)

    sums = lax.fori_loop(0, rows, combine, (jnp.zeros((depth, width), F32),) * 3)
    sums_ref[...] = jnp.zeros_like(sums_ref)
    for a in range(3):
        sums_ref[a : a + 1, :] = jnp.sum(sums[a], axis=0, keepdims=True)
    sums_ref[3:4, :] = jnp.sum(loss, axis=0, keepdims=True)


def stencil(lay, b_field):
    halos = halo(b_field)
    origin = jnp.stack([lay.y0, lay.z0]).astype(jnp.int32)
    wide = (3, lay.rows + 2, lay.depth + 8, lay.width)
    return pl.pallas_call(
        functools.partial(stencil_kernel, lay.ny, lay.nz),
        in_specs=[
            pl.BlockSpec(memory_space=pltpu.SMEM),
        ]
        + [VMEM] * 5,
        out_specs=[pl.BlockSpec(memory_space=pltpu.VMEM)] * 2,
        out_shape=[
            jax.ShapeDtypeStruct(b_field.shape, F32),
            jax.ShapeDtypeStruct((8, lay.width), F32),
        ],
        scratch_shapes=[
            pltpu.VMEM((3, lay.rows + 4) + wide[2:], F32),
            pltpu.VMEM(wide, F32),
            pltpu.VMEM(wide, F32),
        ],
        compiler_params=pltpu.CompilerParams(vmem_limit_bytes=VMEM_LIMIT),
        name="stencil",
    )(origin, b_field, *halos)


def grad_kernel(first, n_after, weight_ref, hidden_ref, slope_ref, grad_ref, x_ref, z_ref, y_ref,
                *refs):
    pre_ref, own_ref, send_ref, sums_ref, part_ref = refs[n_after:]
    pack, rows, depth, width = hidden_ref.shape
    blocks = part_ref.shape[2]
    band = rows // blocks
    channel = (first + pl.program_id(0)) * pack

    def fold(v):
        return jnp.sum(v.reshape(-1, 8, width), axis=0)

    per = max(CHUNK // (band * depth), 1)
    span = per * band
    count = rows // span

    def slopes(n):
        sums = [0.0] * (3 * pack)
        for y in range(n * span, (n + 1) * span):
            grads = [grad_ref[b, y] for b in range(3)]
            for c in range(pack):
                w = [weight_ref[channel + c, b] for b in range(3)]
                mixed = grads[0] * w[0] + grads[1] * w[1] + grads[2] * w[2]
                pre_ref[c, y] = (mixed * slope_ref[c, y].astype(F32)).astype(BF16)
                hidden = hidden_ref[c, y].astype(F32)
                for b in range(3):
                    sums[3 * c + b] = sums[3 * c + b] + fold(hidden * grads[b])
        return sums

    def transform(n):
        total = x_transform(pre_ref.at[:, n * span : (n + 1) * span], x_ref)
        for m in range(per):
            here = total[m * band * depth : (m + 1) * band * depth]
            z_transform(here, z_ref, part_ref, n * per + m)
        return fold(total)

    parts = [slopes(0)]
    totals = []
    for n in range(1, count):
        parts.append(slopes(n))
        totals.append(transform(n - 1))
    totals.append(transform(count - 1))
    sums = [sum(column[1:], column[0]) for column in zip(*parts)]
    sums.append(sum(totals[1:], totals[0]))
    sums_ref[...] = jnp.zeros_like(sums_ref)
    for n, part in enumerate(sums):
        sums_ref[0, n : n + 1, :] = jnp.sum(part, axis=0, keepdims=True)
    y_transform(y_ref, part_ref, own_ref, send_ref)


def grad_modes(lay, hidden, slope, grad_b, x_table, tables, weights, first, count, after=()):
    out, spec = mode_blocks(lay, count)
    block = (lay.pack, lay.rows, lay.depth, lay.width)
    part = pl.BlockSpec(block, lambda i: (i, 0, 0, 0))
    given = pl.BlockSpec(block, lambda i: (first + i, 0, 0, 0))
    volume = lay.pack * lay.cells * lay.width
    lines = -(-(3 * lay.pack + 1) // 8) * 8
    return pl.pallas_call(
        functools.partial(grad_kernel, first, len(after)),
        grid=(count,),
        in_specs=[
            pl.BlockSpec(memory_space=pltpu.SMEM),
            given,
            given,
            whole(grad_b.shape),
            whole(x_table.shape),
            whole(tables[0].shape),
            whole(tables[1].shape),
        ]
        + [ANY] * len(after),
        out_specs=[
            part,
            spec,
            spec,
            pl.BlockSpec((1, lines, lay.width), lambda i: (i, 0, 0)),
        ],
        out_shape=[
            jax.ShapeDtypeStruct((count * lay.pack,) + block[1:], BF16),
            out,
            out,
            jax.ShapeDtypeStruct((count, lines, lay.width), F32),
        ],
        scratch_shapes=[part_scratch(lay)],
        compiler_params=params(),
        cost_estimate=cost(count * volume * 2 * 2 * LANES, count * volume * 10),
        name="grad_modes",
    )(weights, hidden, slope, grad_b, x_table, tables[0], tables[1], *after)


def point_kernel(tile, n_after, field_ref, grad_ref, *refs):
    out_ref, acc_ref = refs[n_after:]
    channels, rows, depth, width = field_ref.shape
    count = grad_ref.shape[0]
    step = pl.program_id(0)

    @pl.when(step == 0)
    def _():
        acc_ref[...] = jnp.zeros_like(acc_ref)

    left, right = [], []
    for y in range(rows):
        for z in range(0, depth, tile):
            left.append(field_ref[:, y, z : z + tile, :].reshape(channels * tile, width))
            right.append(grad_ref[:, y, z : z + tile, :].reshape(count * tile, width))
    acc_ref[...] += lax.dot_general(
        jnp.concatenate(left, axis=1),
        jnp.concatenate(right, axis=1),
        (((1,), (1,)), ((), ())),
        preferred_element_type=F32,
    )

    @pl.when(step == pl.num_programs(0) - 1)
    def _():
        def pick(n):
            owner = lax.broadcasted_iota(jnp.int32, (n, n * tile), 1) // tile
            return (owner == lax.broadcasted_iota(jnp.int32, (n, n * tile), 0)).astype(F32)

        row = lax.broadcasted_iota(jnp.int32, acc_ref.shape, 0)
        column = lax.broadcasted_iota(jnp.int32, acc_ref.shape, 1)
        kept = jnp.where(row % tile == column % tile, acc_ref[...], 0.0)
        half = jnp.dot(
            pick(channels), kept, precision=lax.Precision.HIGHEST, preferred_element_type=F32
        )
        out_ref[...] = lax.dot_general(
            half,
            pick(count),
            (((1,), (1,)), ((), ())),
            precision=lax.Precision.HIGHEST,
            preferred_element_type=F32,
        )


def point_grad(lay, field_in, grad_pre, first, rows, after=()):
    span = math.gcd(4, rows)

    def block(count):
        size = (count, span, lay.depth, lay.width)
        return pl.BlockSpec(size, lambda i: (0, first // span + i, 0, 0))

    count = grad_pre.shape[0]
    size = lay.channels * lay.tile
    return pl.pallas_call(
        functools.partial(point_kernel, lay.tile, len(after)),
        grid=(rows // span,),
        in_specs=[block(lay.channels), block(count)] + [ANY] * len(after),
        out_specs=pl.BlockSpec((lay.channels, count), lambda i: (0, 0)),
        out_shape=jax.ShapeDtypeStruct((lay.channels, count), F32),
        scratch_shapes=[pltpu.VMEM((size, count * lay.tile), F32)],
        compiler_params=params(),
        cost_estimate=cost(2 * size * count * lay.cells * lay.width, 3 * field_in.size),
        name="point_grad",
    )(field_in, grad_pre, *after)


def outer_kernel(modes_ref, grads_ref, *refs):
    out_ref = refs[-1]
    pair, count, channels, wide = out_ref.shape[1:]
    columns = jnp.concatenate([modes_ref[0, a] for a in range(pair)], axis=1)
    rows = []
    for a in range(pair):
        right = grads_ref[0, a]
        turned = jnp.concatenate([right[:, channels:], -right[:, :channels]], axis=1)
        right = jnp.concatenate([right, turned], axis=0)
        zero = jnp.zeros_like(right)
        rows.append(jnp.concatenate([right if n == a else zero for n in range(pair)], axis=1))
    rows = jnp.concatenate(rows, axis=0)
    owner = lax.broadcasted_iota(jnp.int32, columns.shape, 1) % count
    zero = jnp.zeros_like(columns)
    some = 8
    for k in range(0, count, some):
        left = [jnp.where(owner == k + n, columns, zero) for n in range(some)]
        out = dot(jnp.concatenate(left, axis=0), rows)
        for a in range(pair):
            here = out[:, wide * a : wide * (a + 1)]
            out_ref[0, a, k : k + some] = here.reshape(some, channels, wide)


def weight_grad(lay, columns, rows, half, done=(), after=()):
    tile = (lay.mx, lay.channels, 2 * lay.channels)
    shape = (lay.kz, lay.ky) + tile
    per = lay.ky // 2
    first = half * lay.kz // 2

    def spec(block):
        return pl.BlockSpec(
            (1, 2) + block, lambda i: (first + i // per, i % per) + (0,) * len(block)
        )

    return pl.pallas_call(
        outer_kernel,
        grid=(lay.own // 4,),
        in_specs=[spec(columns.shape[2:]), spec(rows.shape[2:])]
        + [ANY] * (len(done) + len(after)),
        out_specs=spec(tile),
        out_shape=jax.ShapeDtypeStruct(shape, F32),
        input_output_aliases={2: 0} if done else {},
        compiler_params=params(),
        cost_estimate=cost(math.prod(shape) * 2, math.prod(shape) * 2),
        name="weight_grad",
    )(columns, rows, *done, *after)


def pack_kernel(n_parts, *refs):
    small_ref, out_ref = refs[n_parts], refs[-1]
    count = refs[0].shape[0]
    total = refs[0][...]
    for ref in refs[1:n_parts]:
        total = total + ref[...]
    out_ref[...] = jnp.zeros_like(out_ref)
    out_ref[:count, :count] = total
    out_ref[count:] = small_ref[...]


def pack_sums(lay, parts, small, after):
    return pl.pallas_call(
        functools.partial(pack_kernel, len(parts)),
        in_specs=[VMEM] * (len(parts) + 1) + [ANY] * len(after),
        out_specs=VMEM,
        out_shape=jax.ShapeDtypeStruct((lay.channels + small.shape[0], LANES), F32),
        name="pack_sums",
    )(*parts, small, *after)


def unpack_kernel(cells, left_ref, right_ref, *refs):
    loss_ref, point_ref, outs_ref, bias_ref, ends_ref = refs[-5:]
    count = point_ref.shape[0]
    total = left_ref[...] + right_ref[...]
    point_ref[...] = total[:count, :count]
    outs_ref[...] = total[count : count + 3, :count]
    bias_ref[...] = total[count + 3 : count + 4, :count]
    ends_ref[...] = total[count + 4 : count + 5, :3]
    loss_ref[...] = total[count + 4 : count + 5, 3:4] / cells


def unpack_sums(lay, left, right, after):
    count = lay.channels
    shapes = [(1, 1), (count, count), (3, count), (1, count), (1, 3)]
    return pl.pallas_call(
        functools.partial(unpack_kernel, lay.width * lay.ny * lay.nz),
        in_specs=[VMEM] * 2 + [ANY] * len(after),
        out_specs=[VMEM] * len(shapes),
        out_shape=[jax.ShapeDtypeStruct(shape, F32) for shape in shapes],
        name="unpack_sums",
    )(left, right, *after)


def on_device(field_in, spectral_weight, point_weight, point_bias, out_weight, out_bias):
    lay = Layout(field_in, spectral_weight)
    tables = lay.grid_tables()
    x_table, x_back = lay.x_tables()
    weights = out_weight.astype(F32)
    scale = math.sqrt(lay.mx * lay.my * lay.mz / (lay.width * lay.ny * lay.nz))
    cuts = [0, lay.rows * 3 // 4, lay.rows]

    def point(n, done, after):
        bias = point_bias.reshape(1, lay.channels)
        first, count = cuts[n], cuts[n + 1] - cuts[n]
        return pointwise(lay, field_in, point_weight.T, bias, first, count, done, after)

    own, send = forward_modes(lay, field_in, x_table, tables, 0, lay.groups)
    points = [None]

    def point_part(n, after):
        points.append(point(n, points[-1], after))
        return points[-1]

    b_field = jnp.broadcast_to(
        out_bias[:, None, None, None], (3, lay.rows, lay.depth, lay.width)
    ).astype(F32)
    last = [x_back, tables[2], tables[3], b_field]
    modes = sum_all(lay, own, send, scale, point_part, last)
    done = points[-1]
    modes_in = by_mode(lay, jnp.concatenate(modes))
    mixed = mix_modes(lay, modes_in, spectral_weight, after=[done])
    mine = by_group(lay, mixed.reshape(lay.kz, lay.ky, lay.mx, 2, lay.groups, lay.pack))

    first = max(lay.groups // 4, 1)
    columns = [spread_chips(lay, mine[:first]), spread_chips(lay, mine[first:])]
    own = spread_depth(lay, columns[0], columns[1:])
    *kept, b_field = dense(
        lay, own, exchange(own, "gy", 1), tables, x_back, done, weights, b_field, 0, first
    )
    own = spread_depth(lay, columns[1], [b_field])
    hidden, slope, b_field = dense(
        lay, own, exchange(own, "gy", 1), tables, x_back, done, weights, b_field,
        first, lay.groups - first, kept,
    )

    grad_b, edge = stencil(lay, b_field)

    pre, own, send, sums = grad_modes(
        lay, hidden, slope, grad_b, x_table, tables, weights, 0, lay.groups
    )
    point_parts = []

    def grad_part(n, after):
        count = cuts[n + 1] - cuts[n]
        point_parts.append(point_grad(lay, field_in, pre, cuts[n], count, after))
        return point_parts[-1]

    grads = sum_all(lay, own, send, 1.0, grad_part)
    outs = jnp.sum(sums[:, : 3 * lay.pack], axis=-1).reshape(lay.channels, 3).T
    bias = sums[:, 3 * lay.pack, :LANES].reshape(lay.groups, lay.pack, lay.mx)[..., 0]
    ends = jnp.pad(jnp.sum(edge[:4], axis=-1), (0, lay.channels - 4))
    small = [outs, bias.reshape(1, lay.channels), ends.reshape(1, lay.channels)]
    small = jnp.pad(jnp.concatenate(small), ((0, 3), (0, LANES - lay.channels)))
    flat = pack_sums(lay, point_parts, small, grads[-1:])
    rows = by_mode(lay, jnp.concatenate(grads))
    rows = jnp.concatenate([rows[:, :, : lay.mx], rows[:, :, lay.mx :]], axis=-1)
    columns = jnp.transpose(modes_in, (0, 1, 3, 2))

    def gathered(axis, steps):
        return [flat] + [exchange(flat, axis, d) for d in steps]

    flat = sum_blocks(gathered("gz", range(1, lay.n_gz)), False, 1.0, [rows])[0]
    grad_spectral = weight_grad(lay, columns, rows, 0, after=[flat])
    flat = sum_blocks(gathered("gy", range(CORES, lay.n_gy, CORES)), False, 1.0, [grad_spectral])
    flat = flat[0]
    grad_spectral = weight_grad(lay, columns, rows, 1, [grad_spectral], [flat])
    loss, grad_point, outs, bias, ends = unpack_sums(lay, *gathered("gy", [1]), [grad_spectral])
    return (
        loss.reshape(()),
        grad_spectral,
        grad_point,
        bias.reshape(lay.channels),
        outs.T,
        ends.reshape(3),
    )


def solution(mesh):
    return jax.shard_map(
        on_device,
        mesh=mesh,
        in_specs=(P(None, "gy", "gz", None), P("gz", "gy", None, None, None), P(), P(), P(), P()),
        out_specs=(P(), P("gz", "gy", None, None, None), P(), P(), P(), P()),
        check_vma=False,
    )
```
